256 devices in a mesh: gx: 8 (over x, core), gy: 32 (over y, z).
Axes of the slice: x: 4, y: 4, z: 8, core: 2. Of those that a mesh axis runs over, the one named last changes fastest.
Arguments:
- rhs: float32 [64, 64, 128, 128], P(None, 'gx', 'gy'), may hold values from -1.5 to 1.5
- coef_x: float32 [3, 64, 128, 128], P(None, 'gx', 'gy'), may hold values from 0 to 10, as said below
- coef_y: float32 [3, 64, 128, 128], P(None, 'gx', 'gy'), may hold values from 0 to 10, as said below
- out_coupling_x: float32 [64, 64], replicated, may hold values from -2 to 2
- in_coupling_x: float32 [64, 64], replicated, may hold values from -2 to 2
- inverse_x: float32 [64, 64], replicated, may hold values from -2 to 2
- boundary_inverse: float32 [3, 64, 64], replicated, may hold values from -2 to 2
- out_coupling_y: float32 [64, 64], replicated, may hold values from -2 to 2
- in_coupling_y: float32 [64, 64], replicated, may hold values from -2 to 2
- inverse_y: float32 [64, 64], replicated, may hold values from -2 to 2
- bc_flags: int32 [128, 128], P('gy'), may hold values from 0 to 2
- line_order: int32 [64, 128], P('gx'), may hold values from 0 to 1
Outputs:
- adjoint: float32 [64, 64, 128, 128], P(None, 'gx', 'gy')
The draws below stay inside these ranges and needn't reach their ends.
Inputs may be any that keep to these rules, and one draw needn't show every extreme that they name: `coef_x`: components 0 and 1 lie strictly between 0 and 1, component 2 between 2 and 10. `coef_y`: components 0 and 1 lie strictly between 0 and 1, component 2 between 2 and 10.
All inputs are finite; a program needn't handle non-finite values.
Results may differ from the reference program's by a relative error of at most 0.0002.
Values sent between devices are 32-bit elements; how exact they have to be, the bound alone decides.
No kernel may reach another device: no remote copies, remote signals or barrier semaphores. Data moves between devices by JAX's collectives and lax.ppermute only.
A program may use at most 128 MiB of HBM per device.

```python
import jax
import jax.numpy as jnp
from jax import lax

NP = 64
NZE = 128
NXE = 64
NYE = 128


def rate_field(key, line_shape, complete_shape, level_low, level_high):
    noise_level_key, perturbation_key, spike_noise_key, layer_depth_key = jax.random.split(key, 4)
    noise_level = jax.random.uniform(noise_level_key, line_shape, jnp.float32, level_low, level_high)
    small_perturbation = jax.random.uniform(perturbation_key, complete_shape, jnp.float32, 0.996, 1.0)
    spike_noise = jax.random.bernoulli(spike_noise_key, 1.0 / 64.0, complete_shape)
    layer_depth = jax.random.uniform(layer_depth_key, complete_shape, jnp.float32, 0.5, 0.8)
    return noise_level * small_perturbation * jnp.where(spike_noise, layer_depth, 1.0)


def mass_field(key, complete_shape):
    return jnp.exp(jax.random.uniform(key, complete_shape, jnp.float32, jnp.log(2.0), jnp.log(10.0)))


def coefficient_stack(key, line_shape):
    complete_shape = (NXE, NYE, NZE)
    inflow_key, outflow_key, mass_key = jax.random.split(key, 3)
    level_low = 0.98
    inflow = rate_field(inflow_key, line_shape, complete_shape, level_low, 0.9995)
    outflow = rate_field(outflow_key, line_shape, complete_shape, level_low, 0.9995)
    return jnp.stack([inflow, outflow, mass_field(mass_key, complete_shape)])


def coupling_matrix(key):
    diag_key, skew_key = jax.random.split(key)
    diagonal = jax.random.uniform(diag_key, (NP,), jnp.float32, 0.965, 0.975)
    skew_scale = 0.2 / (2.0 * (2.0 * NP) ** 0.5)
    noise_part = jnp.clip(jax.random.normal(skew_key, (NP, NP), jnp.float32), -4.0, 4.0) * skew_scale
    return jnp.diag(diagonal) + noise_part - noise_part.T


def inverse_matrix(key, low_diag, high_diag):
    diag_key, off_key = jax.random.split(key)
    diagonal = jax.random.uniform(diag_key, (NP,), jnp.float32, low_diag, high_diag)
    off_part = jnp.clip(jax.random.normal(off_key, (NP, NP), jnp.float32), -4.0, 4.0) * (0.25 / NP ** 0.5)
    return jnp.diag(diagonal) + off_part


def draw_coef_x(key, part):
    return coefficient_stack(jax.random.fold_in(key, 101), (1, NYE, NZE))


def draw_coef_y(key, part):
    return coefficient_stack(jax.random.fold_in(key, 102), (NXE, 1, NZE))


def draw_out_coupling_x(key, part):
    return coupling_matrix(jax.random.fold_in(key, 103))


def draw_in_coupling_x(key, part):
    return coupling_matrix(jax.random.fold_in(key, 104))


def draw_inverse_x(key, part):
    return inverse_matrix(jax.random.fold_in(key, 105), 0.8, 1.2)


def draw_boundary_inverse(key, part):
    base_key = jax.random.fold_in(key, 106)
    return jnp.stack([inverse_matrix(jax.random.fold_in(base_key, flag_kind), 0.4, 1.6) for flag_kind in range(3)])


def draw_out_coupling_y(key, part):
    return coupling_matrix(jax.random.fold_in(key, 107))


def draw_in_coupling_y(key, part):
    return coupling_matrix(jax.random.fold_in(key, 108))


def draw_inverse_y(key, part):
    return inverse_matrix(jax.random.fold_in(key, 109), 0.8, 1.2)


def set_ends(drawn, own_key, smallest, largest):
    dims = drawn.shape
    index_at = [jax.random.randint(jax.random.fold_in(own_key, axis), (), 0, dims[axis]) for axis in range(len(dims))]
    drawn = drawn.at[tuple(index_at)].set(smallest)
    longest = dims.index(max(dims))
    index_at[longest] = (index_at[longest] + 1) % dims[longest]
    return drawn.at[tuple(index_at)].set(largest)


def level_of(rng, dims, pieces, smallest, largest):
    def one(dim, blocks):
        draws = jax.random.uniform(jax.random.fold_in(jax.random.fold_in(rng, 6), dim), (blocks,), jnp.float32, smallest / len(pieces), largest / len(pieces))
        return jnp.repeat(jnp.exp(draws), dims[dim] // blocks).reshape((-1,) + (1,) * (len(dims) - dim - 1))

    loudness = one(*pieces[0])
    for cut in pieces[1:]:
        loudness = loudness * one(*cut)
    return loudness


def scatter_about(stream_key, dims, spread, reach, cuts=(), held_as=jnp.bfloat16):
    factor_of = level_of(stream_key, dims, cuts, -0.22, 0.18) if cuts else 1.0
    entries = jax.random.normal(stream_key, dims, jnp.float32) * spread * factor_of
    return jnp.minimum(jnp.maximum(entries, -reach), reach).astype(held_as)


def setup_inputs(seed: int = 0) -> dict:
    splits = jax.random.split(jax.random.key(seed), 13)
    return {
        "rhs": scatter_about(splits[0], (NP, NXE, NYE, NZE), 0.1, 1.5, ((1, 8), (2, 32)), jnp.float32),
        "coef_x": draw_coef_x(jax.random.fold_in(splits[12], 71), 0),
        "coef_y": draw_coef_y(jax.random.fold_in(splits[12], 71), 0),
        "out_coupling_x": draw_out_coupling_x(jax.random.fold_in(splits[12], 71), 0),
        "in_coupling_x": draw_in_coupling_x(jax.random.fold_in(splits[12], 71), 0),
        "inverse_x": draw_inverse_x(jax.random.fold_in(splits[12], 71), 0),
        "boundary_inverse": draw_boundary_inverse(jax.random.fold_in(splits[12], 71), 0),
        "out_coupling_y": draw_out_coupling_y(jax.random.fold_in(splits[12], 71), 0),
        "in_coupling_y": draw_in_coupling_y(jax.random.fold_in(splits[12], 71), 0),
        "inverse_y": draw_inverse_y(jax.random.fold_in(splits[12], 71), 0),
        "bc_flags": set_ends(jax.random.randint(splits[10], (NYE, NZE), 0, 3), jax.random.fold_in(splits[10], 1), 0, 2).astype(jnp.int32),
        "line_order": set_ends(jax.random.randint(splits[11], (NXE, NZE), 0, 2), jax.random.fold_in(splits[11], 1), 0, 1).astype(jnp.int32),
    }


PRECISE = lax.Precision.HIGHEST


def line_sweep(values, rates, matrix, reverse):
    seq_values = jnp.moveaxis(values, 1, 0)

    def advance(carried, item):
        source, rate_here = item
        current = source + carried
        passed = rate_here[None] * jnp.tensordot(matrix, current, axes=[[0], [0]], precision=PRECISE)
        return passed, current

    start_carry = jnp.zeros(seq_values.shape[1:], jnp.float32)
    _, outputs = lax.scan(advance, start_carry, (seq_values, rates), reverse=reverse)
    return jnp.moveaxis(outputs, 0, 1)


def reference(rhs, coef_x, coef_y, out_coupling_x, in_coupling_x, inverse_x, boundary_inverse, out_coupling_y, in_coupling_y, inverse_y, bc_flags, line_order):
    outflow_x = line_sweep(rhs, coef_x[1], out_coupling_x, False)
    scaled_x = jnp.tensordot(inverse_x, outflow_x, axes=[[0], [0]], precision=PRECISE) / coef_x[2][None]

    def boundary_plane(position):
        plane_cut = outflow_x[:, position]
        combined = jnp.zeros_like(plane_cut)
        for flag_kind in range(3):
            product = jnp.tensordot(boundary_inverse[flag_kind], plane_cut, axes=[[0], [0]], precision=PRECISE)
            combined = combined + jnp.where((bc_flags == flag_kind)[None], product, 0.0)
        return combined / coef_x[2][position][None]

    scaled_x = scaled_x.at[:, 0].set(boundary_plane(0)).at[:, NXE - 1].set(boundary_plane(NXE - 1))
    adjoint_x = line_sweep(scaled_x, coef_x[0], in_coupling_x, True)
    flipped = (line_order > 0)[None, :, None, :]
    oriented = jnp.where(flipped, jnp.flip(adjoint_x, 2), adjoint_x)
    coef_oriented = jnp.where(flipped, jnp.flip(coef_y, 2), coef_y)
    along_y = jnp.transpose(oriented, (0, 2, 1, 3))
    rates_y = jnp.transpose(coef_oriented, (0, 2, 1, 3))
    outflow_y = line_sweep(along_y, rates_y[1], out_coupling_y, False)
    scaled_y = jnp.tensordot(inverse_y, outflow_y, axes=[[0], [0]], precision=PRECISE) / rates_y[2][None]
    solved_y = line_sweep(scaled_y, rates_y[0], in_coupling_y, True)
    solved = jnp.transpose(solved_y, (0, 2, 1, 3))
    return jnp.where(flipped, jnp.flip(solved, 2), solved)
```

```python
import functools

import jax
import jax.numpy as jnp
from jax import lax
from jax.experimental import pallas as pl
from jax.experimental.pallas import tpu as pltpu
from jax.sharding import PartitionSpec as P

NP = 64
LANES = 128
CX = 8
CY = 4
SX = 8
SY = 32
F32 = jnp.float32
BF16 = jnp.bfloat16
VMEM_LIMIT = 48 * 1024 * 1024


def rounded(v):
    return v.astype(BF16).astype(F32)


def split_matrix(m):
    high = rounded(m)
    rest = m - high
    mid = rounded(rest)
    low = rest - mid
    part = lax.broadcasted_iota(jnp.int32, m.shape, 1) // NP
    return jnp.where(part == 1, mid, jnp.where(part == 3, low, high)).astype(BF16)


def split_vectors(v):
    high = v.astype(BF16)
    low = (v - high.astype(F32)).astype(BF16)
    return jnp.concatenate([high, high, low, high], axis=0)


def product(parts, vectors):
    return jnp.dot(parts, vectors, preferred_element_type=F32)


def apply(parts, v):
    return product(parts, split_vectors(v))


def lane_iota(shape):
    return lax.broadcasted_iota(jnp.int32, shape, len(shape) - 1)


def roll(v, shift):
    shift = shift % LANES
    return v if shift == 0 else pltpu.roll(v, shift, 1)


def row_of(block):
    return jnp.concatenate([block[r : r + 1] for r in range(block.shape[0])], axis=1)


def columns(v):
    return [v[:, LANES * j : LANES * (j + 1)] for j in range(v.shape[1] // LANES)]


def regroup(blocks, width):
    n = LANES // width
    rolled = [[roll(b, width * k) for k in range(n)] for b in blocks]
    group = lane_iota(blocks[0].shape) // width
    outs = []
    for a in range(n):
        acc = rolled[0][(0 - a) % n]
        for q in range(1, n):
            acc = jnp.where(group == q, rolled[q][(q - a) % n], acc)
        outs.append(acc)
    return outs


def replicate(block, width):
    return regroup([block] * (LANES // width), width)


def shifted(v, t, width, ncol, reverse):
    cols = columns(v)
    group = lane_iota(cols[0].shape) // width
    n = LANES // width
    out = []
    for j in range(ncol):
        k = j + t if reverse else j - t
        carry = abs(k // ncol)
        src = cols[k % ncol]
        if carry:
            if reverse:
                src = jnp.where(group < n - carry, roll(src, -width * carry), 0.0)
            else:
                src = jnp.where(group >= carry, roll(src, width * carry), 0.0)
        out.append(src)
    return jnp.concatenate(out, axis=1)


def scan_segments(v, rate, powers, width, ncol, reverse):
    for k in range(powers.shape[0]):
        t = 1 << k
        v = v + rate * apply(powers[k], shifted(v, t, width, ncol, reverse))
        if k + 1 < powers.shape[0]:
            rate = rate * shifted(rate, t, width, ncol, reverse)
    return v


def x_sweep(rank, load, coef_ref, flags_ref, both, down, bounds, scaled_ref, enter, leave, store):
    def rates(which, i):
        return row_of(coef_ref[which, CY * i : CY * (i + 1), :])

    flags = row_of(flags_ref[...])
    carry = enter
    for i in range(CX):
        f = load(i)
        if carry is not None:
            f = f + carry
        vectors = split_vectors(f)
        out = product(both, vectors)
        carry = rates(1, i) * out[:NP]
        scaled = out[NP:]
        if i == 0 or i == CX - 1:
            ends = product(bounds, vectors)
            chosen = jnp.where(
                flags == 0, ends[:NP], jnp.where(flags == 1, ends[NP : 2 * NP], ends[2 * NP :])
            )
            scaled = jnp.where(rank == (0 if i == 0 else SX - 1), chosen, scaled)
        scaled_ref[i] = scaled * (1.0 / rates(2, i))
    outgoing = carry
    carry = leave
    for i in reversed(range(CX)):
        g = scaled_ref[i]
        if carry is not None:
            g = g + carry
        if store is not None:
            store(i, g)
        if store is None or i > 0:
            carry = rates(0, i) * apply(down, g)
    return outgoing, carry


def x_local_kernel(rank_ref, rhs_ref, coef_ref, flags_ref, mats_ref, out_ref, scaled_ref):
    rank = rank_ref[0]
    parts = split_matrix(mats_ref[0 : 6 * NP])
    both, down, bounds = parts[: 2 * NP], parts[2 * NP : 3 * NP], parts[3 * NP :]

    def load(i):
        return jnp.concatenate(
            [rhs_ref[pl.ds(CY * i + y, NP, stride=CX * CY), :] for y in range(CY)], axis=1
        )

    f, g = x_sweep(
        rank, load, coef_ref, flags_ref, both, down, bounds, scaled_ref, None, None, None
    )
    for y, (fy, gy) in enumerate(zip(columns(f), columns(g))):
        even, odd = regroup([fy, gy], NP)
        out_ref[2 * y, 0:NP, :] = even
        out_ref[2 * y + 1, 0:NP, :] = odd
    down_rate = coef_ref[0, 0:CY, :]
    up_rate = jnp.ones_like(down_rate)
    gains = []
    for i in range(CX):
        gains.append(down_rate * up_rate / coef_ref[2, CY * i : CY * (i + 1), :])
        up_rate = up_rate * coef_ref[1, CY * i : CY * (i + 1), :]
        if i + 1 < CX:
            down_rate = down_rate * coef_ref[0, CY * (i + 1) : CY * (i + 2), :]
    last = gains.pop()
    is_last = rank == SX - 1
    flags = flags_ref[...]
    gains.append(jnp.where(is_last, 0.0, last))
    for kind in range(3):
        gains.append(jnp.where(jnp.logical_and(is_last, flags == kind), last, 0.0))
    values = [up_rate, down_rate] + gains + [jnp.zeros_like(last)] * 3
    for r in range(8):
        even, odd = regroup([values[2 * r], values[2 * r + 1]], NP)
        for y in range(CY):
            out_ref[2 * y, NP + r : NP + r + 1, :] = even[y : y + 1]
            out_ref[2 * y + 1, NP + r : NP + r + 1, :] = odd[y : y + 1]


def x_owner_kernel(in_ref, gain_ref, up_ref, down_ref, norm_ref, out_ref):
    half = SX // 2
    fs, gs, sa, sb = [], [], [], []
    for j in range(half):
        f, g = regroup([in_ref[j], in_ref[half + j]], NP)
        fs.append(f[:NP])
        gs.append(g[:NP])
        sa.append(f[NP:])
        sb.append(g[NP:])
    f = jnp.concatenate(fs, axis=1)
    g = jnp.concatenate(gs, axis=1)
    even = jnp.concatenate(sa, axis=1)
    odd = jnp.concatenate(sb, axis=1)
    scalar = [(even if k % 2 == 0 else odd)[k // 2 : k // 2 + 1] for k in range(13)]
    width, ncol = NP, half
    up_rate = scalar[0] * norm_ref[0:1, 0:1]
    down_rate = scalar[1] * norm_ref[1:2, 0:1]
    h = scan_segments(
        shifted(f, 1, width, ncol, False),
        shifted(up_rate, 1, width, ncol, False),
        up_ref,
        width,
        ncol,
        False,
    )
    vectors = split_vectors(h)
    through = product(gain_ref[0 : CX * NP], vectors)
    for i in range(CX):
        g = g + scalar[2 + i] * through[NP * i : NP * (i + 1)]
    ends = product(gain_ref[CX * NP :], vectors[:, LANES * (half - 1) :])
    extra = 0.0
    for kind in range(3):
        extra = extra + (
            scalar[10 + kind][:, LANES * (half - 1) :] * ends[NP * kind : NP * (kind + 1)]
        )
    g = jnp.concatenate([g[:, : LANES * (half - 1)], g[:, LANES * (half - 1) :] + extra], axis=1)
    e = scan_segments(
        shifted(g, 1, width, ncol, True),
        shifted(down_rate, 1, width, ncol, True),
        down_ref,
        width,
        ncol,
        True,
    )
    for j, (hj, ej) in enumerate(zip(columns(h), columns(e))):
        first, second = regroup([hj, ej], NP)
        out_ref[j] = first
        out_ref[half + j] = second


def y_rates(coef_ref, which, flip, p):
    here = coef_ref[which, pl.ds(p, CX, stride=CY), :]
    there = coef_ref[which, pl.ds(CY - 1 - p, CX, stride=CY), :]
    return jnp.where(flip, there, here)


def y_sweep(load, rates, both, down, enter, leave, scaled_ref, store):
    carry = enter
    for p in range(CY):
        f = load(p)
        if carry is not None:
            f = f + carry
        out = apply(both, f)
        carry = row_of(rates(1, p)) * out[:NP]
        scaled_ref[p] = out[NP:] * row_of(1.0 / rates(2, p))
    outgoing = carry
    carry = leave
    for p in reversed(range(CY)):
        g = scaled_ref[p]
        if carry is not None:
            g = g + carry
        if store is not None:
            store(p, g)
        if store is None or p > 0:
            carry = row_of(rates(0, p)) * apply(down, g)
    return outgoing, carry


def middle_kernel(
    rank_ref,
    rhs_ref,
    coef_ref,
    flags_ref,
    mats_ref,
    in_ref,
    coef_y_ref,
    order_ref,
    adj_ref,
    out_ref,
    scaled_ref,
    scaled_y_ref,
):
    rank = rank_ref[0]
    parts = split_matrix(mats_ref[...])
    both, down, bounds = parts[: 2 * NP], parts[2 * NP : 3 * NP], parts[3 * NP : 6 * NP]

    def load(i):
        return jnp.concatenate(
            [rhs_ref[pl.ds(CY * i + y, NP, stride=CX * CY), :] for y in range(CY)], axis=1
        )

    hs, es = [], []
    for y in range(CY):
        h, e = regroup([in_ref[2 * y], in_ref[2 * y + 1]], NP)
        hs.append(h)
        es.append(e)

    def store(i, g):
        for y in range(CY):
            adj_ref[y, :, LANES * i : LANES * (i + 1)] = g[:, LANES * y : LANES * (y + 1)]

    x_sweep(
        rank,
        load,
        coef_ref,
        flags_ref,
        both,
        down,
        bounds,
        scaled_ref,
        jnp.concatenate(hs, axis=1),
        jnp.concatenate(es, axis=1),
        store,
    )
    both_y, down_y = parts[6 * NP : 8 * NP], parts[8 * NP :]
    flip = order_ref[...] > 0
    flip_row = row_of(order_ref[...]) > 0

    def load_y(p):
        return jnp.where(flip_row, adj_ref[CY - 1 - p], adj_ref[p])

    rates = functools.partial(y_rates, coef_y_ref)

    def oriented(which, p):
        return rates(which, flip, p)

    f, g = y_sweep(load_y, oriented, both_y, down_y, None, None, scaled_y_ref, None)
    for x, (fx, gx) in enumerate(zip(columns(f), columns(g))):
        chunks = regroup([fx[:32], fx[32:], gx[:32], gx[32:]], 32)
        for a in range(4):
            out_ref[4 * x + a, 0:32, :] = chunks[a]
    down_rate = oriented(0, 0)
    up_rate = jnp.ones_like(down_rate)
    gains = []
    for p in range(CY):
        gains.append(down_rate * up_rate / oriented(2, p))
        up_rate = up_rate * oriented(1, p)
        if p + 1 < CY:
            down_rate = down_rate * oriented(0, p + 1)
    values = [up_rate, down_rate] + gains + [flip.astype(F32), jnp.zeros_like(up_rate)]
    for r, value in enumerate(values):
        for a, block in enumerate(replicate(value, 32)):
            for x in range(CX):
                out_ref[4 * x + a, 32 + r : 33 + r, :] = block[x : x + 1]


def y_owner_kernel(in_ref, gain_ref, up_ref, down_ref, norm_ref, out_ref, res_ref):
    width, ncol = 32, 8
    flip = in_ref[0, 38:39, :] > 0.5

    def oriented(s):
        return jnp.where(flip, in_ref[SY - 1 - s], in_ref[s])

    fs, gs, ss = [], [], []
    for j in range(ncol):
        blocks = [oriented(ncol * a + j) for a in range(4)]
        outs = regroup([b[:32] for b in blocks], width)
        fs.append(jnp.concatenate(outs[:2], axis=0))
        gs.append(jnp.concatenate(outs[2:], axis=0))
        group = lane_iota((8, LANES)) // width
        acc = blocks[0][32:40]
        for a in range(1, 4):
            acc = jnp.where(group == a, blocks[a][32:40], acc)
        ss.append(acc)
    f = jnp.concatenate(fs, axis=1)
    g = jnp.concatenate(gs, axis=1)
    scalars = jnp.concatenate(ss, axis=1)
    up_rate = scalars[0:1] * norm_ref[0:1, 0:1]
    down_rate = scalars[1:2] * norm_ref[1:2, 0:1]
    h = scan_segments(
        shifted(f, 1, width, ncol, False),
        shifted(up_rate, 1, width, ncol, False),
        up_ref,
        width,
        ncol,
        False,
    )
    through = apply(gain_ref[...], h)
    for p in range(CY):
        g = g + scalars[2 + p : 3 + p] * through[NP * p : NP * (p + 1)]
    e = scan_segments(
        shifted(g, 1, width, ncol, True),
        shifted(down_rate, 1, width, ncol, True),
        down_ref,
        width,
        ncol,
        True,
    )
    for j, (hj, ej) in enumerate(zip(columns(h), columns(e))):
        outs = regroup([hj[:32], hj[32:], ej[:32], ej[32:]], width)
        for a in range(4):
            res_ref[ncol * a + j] = outs[a]
    for s in range(SY):
        out_ref[s] = jnp.where(flip, res_ref[SY - 1 - s], res_ref[s])


def y_final_kernel(adj_ref, coef_y_ref, order_ref, mats_ref, in_ref, out_ref, scaled_ref, solved_ref):
    parts = split_matrix(mats_ref[6 * NP :])
    both, down = parts[: 2 * NP], parts[2 * NP :]
    flip = order_ref[...] > 0
    flip_row = row_of(order_ref[...]) > 0
    hs, es = [], []
    for x in range(CX):
        outs = regroup([in_ref[4 * x + a] for a in range(4)], 32)
        hs.append(jnp.concatenate(outs[:2], axis=0))
        es.append(jnp.concatenate(outs[2:], axis=0))

    def load(p):
        return jnp.where(flip_row, adj_ref[CY - 1 - p], adj_ref[p])

    def store(p, g):
        solved_ref[p] = g

    y_sweep(
        load,
        lambda which, p: y_rates(coef_y_ref, which, flip, p),
        both,
        down,
        jnp.concatenate(hs, axis=1),
        jnp.concatenate(es, axis=1),
        scaled_ref,
        store,
    )
    for y in range(CY):
        plane = jnp.where(flip_row, solved_ref[CY - 1 - y], solved_ref[y])
        for x, block in enumerate(columns(plane)):
            out_ref[pl.ds(CY * x + y, NP, stride=CX * CY), :] = block


def precise(a, b):
    return jnp.dot(a[:, :NP], b, precision=lax.Precision.HIGHEST, preferred_element_type=F32)


def prepare(cells, doublings, up, down, scale, bounds, gain_ref, up_ref, down_ref, norm_ref):
    halves = cells.bit_length() - 1
    ups, downs = [up], [down]
    for _ in range(halves):
        ups.append(precise(ups[-1], ups[-1]))
        downs.append(precise(downs[-1], downs[-1]))
    scaled = scale
    stack = down
    for k in range(halves):
        scaled = jnp.concatenate([scaled, precise(scaled, ups[k])], axis=0)
        stack = jnp.concatenate([stack, precise(stack, downs[k])], axis=0)
    for j in range(cells):
        rows = slice(NP * j, NP * (j + 1))
        gain_ref[rows, :] = split_matrix(precise(stack[rows], scaled[rows]))
    if bounds is not None:
        for k in range(halves):
            bounds = precise(bounds, ups[k])
        for kind in range(3):
            rows = slice(NP * (cells + kind), NP * (cells + kind + 1))
            ends = bounds[NP * kind : NP * (kind + 1)]
            gain_ref[rows, :] = split_matrix(precise(downs[halves], ends))
    norm_ref[...] = jnp.zeros(norm_ref.shape, F32)
    for row, (power, ref) in enumerate(((ups[halves], up_ref), (downs[halves], down_ref))):
        norm = jnp.max(jnp.sum(jnp.abs(power[:, :NP]), axis=1, keepdims=True), axis=0, keepdims=True)
        norm = jnp.maximum(norm, 1e-30)
        norm_ref[row : row + 1, :] = jnp.broadcast_to(norm, (1, LANES))
        power = power / norm
        for k in range(doublings):
            ref[k] = split_matrix(power)
            if k + 1 < doublings:
                power = precise(power, power)


def prepare_x_kernel(mats_ref, gain_ref, up_ref, down_ref, norm_ref):
    prepare(
        CX,
        3,
        mats_ref[0:NP],
        mats_ref[2 * NP : 3 * NP],
        mats_ref[NP : 2 * NP],
        mats_ref[3 * NP : 6 * NP],
        gain_ref,
        up_ref,
        down_ref,
        norm_ref,
    )


def prepare_y_kernel(mats_ref, gain_ref, up_ref, down_ref, norm_ref):
    prepare(
        CY,
        5,
        mats_ref[6 * NP : 7 * NP],
        mats_ref[8 * NP : 9 * NP],
        mats_ref[7 * NP : 8 * NP],
        None,
        gain_ref,
        up_ref,
        down_ref,
        norm_ref,
    )


def shape(*dims, dtype=F32):
    return jax.ShapeDtypeStruct(dims, dtype)


def call(kernel, out_shape, n_in, scratch=(), scalars=0):
    whole = pl.BlockSpec(memory_space=pltpu.VMEM)
    specs = [pl.BlockSpec(memory_space=pltpu.SMEM)] * scalars + [whole] * n_in
    outs = jax.tree.map(lambda _: whole, out_shape)
    return pl.pallas_call(
        kernel,
        out_shape=out_shape,
        in_specs=specs,
        out_specs=outs,
        scratch_shapes=list(scratch),
        compiler_params=pltpu.CompilerParams(vmem_limit_bytes=VMEM_LIMIT),
    )


def prepared(kernel, gains, doublings, mats):
    outs = (
        shape(gains * NP, 4 * NP, dtype=BF16),
        shape(doublings, NP, 4 * NP, dtype=BF16),
        shape(doublings, NP, 4 * NP, dtype=BF16),
        shape(8, LANES),
    )
    return call(kernel, outs, 1)(mats)


def per_device(
    rhs,
    coef_x,
    coef_y,
    out_coupling_x,
    in_coupling_x,
    inverse_x,
    boundary_inverse,
    out_coupling_y,
    in_coupling_y,
    inverse_y,
    bc_flags,
    line_order,
):
    rank = lax.axis_index("gx").astype(jnp.int32).reshape(1)
    mats = jnp.concatenate(
        [
            jnp.stack([out_coupling_x, inverse_x, in_coupling_x]),
            boundary_inverse,
            jnp.stack([out_coupling_y, inverse_y, in_coupling_y]),
        ],
        0,
    )
    mats = jnp.swapaxes(mats, 1, 2).reshape(9 * NP, NP)
    mats = jnp.concatenate([mats] * 4, axis=1)
    rhs = rhs.reshape(NP * CX * CY, LANES)
    coef_x = coef_x.reshape(3, CX * CY, LANES)
    coef_y = coef_y.reshape(3, CX * CY, LANES)

    sent = call(
        x_local_kernel,
        shape(SX, NP + 8, LANES),
        4,
        [pltpu.VMEM((CX, NP, CY * LANES), F32)],
        1,
    )(rank, rhs, coef_x, bc_flags, mats)
    got = lax.all_to_all(sent, "gx", 0, 0, tiled=True)
    prep_x = prepared(prepare_x_kernel, CX + 3, 3, mats)
    back = call(x_owner_kernel, shape(SX, NP, LANES), 5)(got, *prep_x)
    terms = lax.all_to_all(back, "gx", 0, 0, tiled=True)
    prep_y = prepared(prepare_y_kernel, CY, 5, mats)
    adj, sent = call(
        middle_kernel,
        (shape(CY, NP, CX * LANES), shape(SY, 40, LANES)),
        7,
        [
            pltpu.VMEM((CX, NP, CY * LANES), F32),
            pltpu.VMEM((CY, NP, CX * LANES), F32),
        ],
        1,
    )(rank, rhs, coef_x, bc_flags, mats, terms, coef_y, line_order)
    got = lax.all_to_all(sent, "gy", 0, 0, tiled=True)
    back = call(
        y_owner_kernel, shape(SY, 32, LANES), 5, [pltpu.VMEM((SY, 32, LANES), F32)]
    )(got, *prep_y)
    terms = lax.all_to_all(back, "gy", 0, 0, tiled=True)
    out = call(
        y_final_kernel,
        shape(NP * CX * CY, LANES),
        5,
        [
            pltpu.VMEM((CY, NP, CX * LANES), F32),
            pltpu.VMEM((CY, NP, CX * LANES), F32),
        ],
    )(adj, coef_y, line_order, mats, terms)
    return out.reshape(NP, CX, CY, LANES)


def solution(mesh):
    grid = P(None, "gx", "gy", None)
    in_specs = (grid, grid, grid) + (P(),) * 7 + (P("gy", None), P("gx", None))
    return jax.shard_map(
        per_device, mesh=mesh, in_specs=in_specs, out_specs=grid, check_vma=False
    )
```

```python
import jax
import jax.numpy as jnp
from jax import lax
from jax.experimental import pallas as pl
from jax.experimental.pallas import tpu as pltpu
from jax.sharding import PartitionSpec as P

NP = 64
LANES = 128
CX = 8
PIECES = 4
CY = 4
SX = 8
SY = 32
ROWS = 34
F32 = jnp.float32
BF16 = jnp.bfloat16
VMEM_LIMIT = 48 * 1024 * 1024


def rounded(v):
    return v.astype(BF16).astype(F32)


def split_matrix(m):
    high = rounded(m)
    rest = m - high
    mid = rounded(rest)
    low = rest - mid
    part = lax.broadcasted_iota(jnp.int32, m.shape, 1) // NP
    return jnp.where(part == 1, mid, jnp.where(part == 3, low, high)).astype(BF16)


def split_vectors(v):
    high = v.astype(BF16)
    low = (v - high.astype(F32)).astype(BF16)
    return jnp.concatenate([high, high, low, high], axis=0)


def product(parts, vectors):
    return jnp.dot(parts, vectors, preferred_element_type=F32)


def apply(parts, v):
    return product(parts, split_vectors(v))


def lane_iota(shape):
    return lax.broadcasted_iota(jnp.int32, shape, len(shape) - 1)


def roll(v, shift):
    shift = shift % LANES
    return v if shift == 0 else pltpu.roll(v, shift, 1)


def row_of(block):
    return jnp.concatenate([block[r : r + 1] for r in range(block.shape[0])], axis=1)


def columns(v):
    return [v[:, LANES * j : LANES * (j + 1)] for j in range(v.shape[1] // LANES)]


def regroup(blocks, width):
    n = LANES // width
    rolled = [[roll(b, width * k) for k in range(n)] for b in blocks]
    group = lane_iota(blocks[0].shape) // width
    outs = []
    for a in range(n):
        acc = rolled[0][(0 - a) % n]
        for q in range(1, n):
            acc = jnp.where(group == q, rolled[q][(q - a) % n], acc)
        outs.append(acc)
    return outs


def replicate(block, width):
    return regroup([block] * (LANES // width), width)


def shifted(v, t, width, ncol, reverse):
    cols = columns(v)
    group = lane_iota(cols[0].shape) // width
    n = LANES // width
    out = []
    for j in range(ncol):
        k = j + t if reverse else j - t
        carry = abs(k // ncol)
        src = cols[k % ncol]
        if carry:
            if reverse:
                src = jnp.where(group < n - carry, roll(src, -width * carry), 0.0)
            else:
                src = jnp.where(group >= carry, roll(src, width * carry), 0.0)
        out.append(src)
    return jnp.concatenate(out, axis=1)


def scan_segments(v, rate, powers, width, ncol, reverse):
    for k in range(powers.shape[0]):
        t = 1 << k
        v = v + rate * apply(powers[k], shifted(v, t, width, ncol, reverse))
        if k + 1 < powers.shape[0]:
            rate = rate * shifted(rate, t, width, ncol, reverse)
    return v


def tiled(m):
    pair = jnp.concatenate([m, m], axis=0).T
    return jnp.concatenate([pair, pair], axis=1)


def multiply(a, b):
    parts = split_matrix(a)
    high = b.astype(BF16)
    rest = b - high.astype(F32)
    mid = rest.astype(BF16)
    low = (rest - mid.astype(F32)).astype(BF16)
    none = jnp.zeros_like(low)
    return product(parts, jnp.concatenate([high, high, mid, high], axis=0)) + product(
        parts, jnp.concatenate([low, mid, none, none], axis=0)
    )


def prepare(cells, doublings, up, down, scale, bounds, gain_ref, from_ref, up_ref, down_ref, norm_ref):
    halves = cells.bit_length() - 1
    ups, downs = [up], [down]
    for _ in range(halves):
        ups.append(multiply(ups[-1], ups[-1]))
        downs.append(multiply(downs[-1], downs[-1]))
    scaled = scale
    stack = down
    for k in range(halves):
        scaled = jnp.concatenate([scaled, multiply(scaled, ups[k])], axis=0)
        stack = jnp.concatenate([stack, multiply(stack, downs[k])], axis=0)
    from_ref[0 : cells * NP, :] = split_matrix(scaled)
    for j in range(cells):
        rows = slice(NP * j, NP * (j + 1))
        gain_ref[rows, :] = split_matrix(multiply(stack[rows], scaled[rows]))
    if bounds is not None:
        for k in range(halves):
            bounds = multiply(bounds, ups[k])
        from_ref[cells * NP :, :] = split_matrix(bounds)
        for kind in range(3):
            rows = slice(NP * (cells + kind), NP * (cells + kind + 1))
            ends = bounds[NP * kind : NP * (kind + 1)]
            gain_ref[rows, :] = split_matrix(multiply(downs[halves], ends))
    norm_ref[...] = jnp.zeros(norm_ref.shape, F32)
    for row, (power, ref) in enumerate(((ups[halves], up_ref), (downs[halves], down_ref))):
        norm = jnp.max(jnp.sum(jnp.abs(power[:, :NP]), axis=1, keepdims=True), axis=0, keepdims=True)
        norm = jnp.maximum(norm, 1e-30)
        norm_ref[row : row + 1, :] = jnp.broadcast_to(norm, (1, LANES))
        power = power / norm
        for k in range(doublings):
            ref[k] = split_matrix(power)
            if k + 1 < doublings:
                power = multiply(power, power)


def prepare_kernel(mats_ref, raw_ref, parts_ref, *outs):
    ux, wx, b0, b1, b2, dx = [mats_ref[NP * k : NP * (k + 1), :] for k in range(6)]
    uy, wy, dy = [tiled(raw_ref[k]) for k in range(3)]
    for k, m in enumerate((dx, uy, wy, dy)):
        parts_ref[NP * k : NP * (k + 1), :] = split_matrix(m)
    prepare(CX, 3, ux, dx, wx, jnp.concatenate([b0, b1, b2], axis=0), *outs[:5])
    prepare(CY, 5, uy, dy, wy, None, *outs[5:])


def x_rates(coef_ref, which, i):
    return coef_ref[which, CY * i : CY * (i + 1), :]


def x_local_kernel(
    rank_ref,
    rhs_hbm,
    coef_hbm,
    flags_hbm,
    ux,
    wx,
    dx,
    b,
    uy,
    wy,
    dy,
    coef_y_hbm,
    order_hbm,
    out_ref,
    scaled_ref,
    mats_ref,
    raw_y_ref,
    coef_ref,
    flags_ref,
    coef_y_ref,
    order_ref,
    rhs_ref,
    raw_ref,
    bounds_ref,
    sems,
):
    rank = rank_ref[0]
    sources = [ux, wx, b, dx, coef_hbm, flags_hbm]
    targets = [raw_ref.at[0], raw_ref.at[1], bounds_ref, raw_ref.at[2], coef_ref, flags_ref]
    for k in range(PIECES):
        sources.append(rhs_hbm.at[:, 8 * k : 8 * (k + 1), :])
        targets.append(rhs_ref.at[k])
    sources += [uy, wy, dy, coef_y_hbm, order_hbm]
    targets += [raw_y_ref.at[0], raw_y_ref.at[1], raw_y_ref.at[2], coef_y_ref, order_ref]
    copies = []
    for k, (source, target) in enumerate(zip(sources, targets)):
        copies.append(pltpu.make_async_copy(source, target, sems.at[k]))
        copies[-1].start()
    for copy in copies[:6]:
        copy.wait()

    def place(row, m):
        value = tiled(m)
        mats_ref[NP * row : NP * (row + 1), :] = value
        return split_matrix(value)

    every = jnp.concatenate(
        [place(0, raw_ref[0]), place(1, raw_ref[1])] + [place(2 + k, bounds_ref[k]) for k in range(3)],
        axis=0,
    )
    both = every[: 2 * NP]
    down = place(5, raw_ref[2])
    planes = rhs_ref.reshape(PIECES * NP * 8, LANES)

    flags = row_of(flags_ref[...])
    carry = 0.0
    for i in range(CX):
        k = CY * i // 8
        if CY * i % 8 == 0:
            copies[6 + k].wait()
        start = k * NP * 8 + CY * i % 8
        f = carry + jnp.concatenate(
            [planes[pl.ds(start + y, NP, stride=8), :] for y in range(CY)], axis=1
        )
        if i == 0 or i == CX - 1:
            out = apply(every, f)
            ends = out[2 * NP :]
            chosen = jnp.where(
                flags == 0, ends[:NP], jnp.where(flags == 1, ends[NP : 2 * NP], ends[2 * NP :])
            )
            scaled = jnp.where(rank == (0 if i == 0 else SX - 1), chosen, out[NP : 2 * NP])
        else:
            out = apply(both, f)
            scaled = out[NP:]
        carry = row_of(x_rates(coef_ref, 1, i)) * out[:NP]
        scaled_ref[i] = scaled * row_of(1.0 / x_rates(coef_ref, 2, i))
    f = carry
    carry = 0.0
    for i in reversed(range(CX)):
        carry = row_of(x_rates(coef_ref, 0, i)) * apply(down, scaled_ref[i] + carry)
    g = carry
    for copy in copies[6 + PIECES :]:
        copy.wait()
    for y, (fy, gy) in enumerate(zip(columns(f), columns(g))):
        even, odd = regroup([fy, gy], NP)
        out_ref[2 * y, 0:NP, :] = even
        out_ref[2 * y + 1, 0:NP, :] = odd
    down_rate = x_rates(coef_ref, 0, 0)
    up_rate = jnp.ones_like(down_rate)
    gains = []
    for i in range(CX):
        gains.append(down_rate * up_rate / x_rates(coef_ref, 2, i))
        up_rate = up_rate * x_rates(coef_ref, 1, i)
        if i + 1 < CX:
            down_rate = down_rate * x_rates(coef_ref, 0, i + 1)
    last = gains.pop()
    is_last = rank == SX - 1
    flags = flags_ref[...]
    gains.append(jnp.where(is_last, 0.0, last))
    for kind in range(3):
        gains.append(jnp.where(jnp.logical_and(is_last, flags == kind), last, 0.0))
    values = [up_rate, down_rate] + gains + [jnp.zeros_like(last)] * 3
    for r in range(8):
        even, odd = regroup([values[2 * r], values[2 * r + 1]], NP)
        for y in range(CY):
            out_ref[2 * y, NP + r : NP + r + 1, :] = even[y : y + 1]
            out_ref[2 * y + 1, NP + r : NP + r + 1, :] = odd[y : y + 1]


def x_owner_kernel(in_ref, gain_ref, up_ref, down_ref, norm_ref, out_ref):
    half = SX // 2
    fs, gs, sa, sb = [], [], [], []
    for j in range(half):
        f, g = regroup([in_ref[j], in_ref[half + j]], NP)
        fs.append(f[:NP])
        gs.append(g[:NP])
        sa.append(f[NP:])
        sb.append(g[NP:])
    f = jnp.concatenate(fs, axis=1)
    g = jnp.concatenate(gs, axis=1)
    even = jnp.concatenate(sa, axis=1)
    odd = jnp.concatenate(sb, axis=1)
    scalar = [(even if k % 2 == 0 else odd)[k // 2 : k // 2 + 1] for k in range(13)]
    width, ncol = NP, half
    up_rate = scalar[0] * norm_ref[0:1, 0:1]
    down_rate = scalar[1] * norm_ref[1:2, 0:1]
    h = scan_segments(
        shifted(f, 1, width, ncol, False),
        shifted(up_rate, 1, width, ncol, False),
        up_ref,
        width,
        ncol,
        False,
    )
    vectors = split_vectors(h)
    through = product(gain_ref[0 : CX * NP], vectors)
    for i in range(CX):
        g = g + scalar[2 + i] * through[NP * i : NP * (i + 1)]
    ends = product(gain_ref[CX * NP :], vectors[:, LANES * (half - 1) :])
    extra = 0.0
    for kind in range(3):
        extra = extra + (
            scalar[10 + kind][:, LANES * (half - 1) :] * ends[NP * kind : NP * (kind + 1)]
        )
    g = jnp.concatenate([g[:, : LANES * (half - 1)], g[:, LANES * (half - 1) :] + extra], axis=1)
    e = scan_segments(
        shifted(g, 1, width, ncol, True),
        shifted(down_rate, 1, width, ncol, True),
        down_ref,
        width,
        ncol,
        True,
    )
    for j, (hj, ej) in enumerate(zip(columns(h), columns(e))):
        first, second = regroup([hj, ej], NP)
        out_ref[j] = first
        out_ref[half + j] = second


def y_rates(coef_ref, which, flip, p):
    here = coef_ref[which, pl.ds(p, CX, stride=CY), :]
    there = coef_ref[which, pl.ds(CY - 1 - p, CX, stride=CY), :]
    return jnp.where(flip, there, here)


def middle_kernel(
    rank_ref,
    local_ref,
    coef_ref,
    flags_ref,
    parts_ref,
    from_ref,
    in_ref,
    coef_y_ref,
    order_ref,
    scaled_ref,
    out_ref,
    adj_ref,
):
    rank = rank_ref[0]
    parts = parts_ref[...]
    down, both_y, down_y = parts[:NP], parts[NP : 3 * NP], parts[3 * NP :]
    hs, es = [], []
    for y in range(CY):
        h, e = regroup([in_ref[2 * y], in_ref[2 * y + 1]], NP)
        hs.append(h)
        es.append(e)
    through = apply(from_ref[...], jnp.concatenate(hs, axis=1))
    flags = row_of(flags_ref[...])
    up_rates = [jnp.ones((CY, LANES), F32)]
    for i in range(CX - 1):
        up_rates.append(up_rates[-1] * x_rates(coef_ref, 1, i))
    carry = jnp.concatenate(es, axis=1)
    for i in reversed(range(CX)):
        term = through[NP * i : NP * (i + 1)]
        if i == CX - 1:
            ends = through[NP * CX :]
            chosen = jnp.where(
                flags == 0, ends[:NP], jnp.where(flags == 1, ends[NP : 2 * NP], ends[2 * NP :])
            )
            term = jnp.where(rank == SX - 1, chosen, term)
        g = local_ref[i] + row_of(up_rates[i] / x_rates(coef_ref, 2, i)) * term + carry
        for y in range(CY):
            adj_ref[y, :, LANES * i : LANES * (i + 1)] = g[:, LANES * y : LANES * (y + 1)]
        if i > 0:
            carry = row_of(x_rates(coef_ref, 0, i)) * apply(down, g)

    flip = order_ref[...] > 0
    flip_row = row_of(order_ref[...]) > 0

    def oriented(which, p):
        return y_rates(coef_y_ref, which, flip, p)

    carry = 0.0
    for p in range(CY):
        out = apply(both_y, jnp.where(flip_row, adj_ref[CY - 1 - p], adj_ref[p]) + carry)
        carry = row_of(oriented(1, p)) * out[:NP]
        scaled_ref[p] = out[NP:] * row_of(1.0 / oriented(2, p))
    f = carry
    carry = 0.0
    for p in reversed(range(CY)):
        carry = row_of(oriented(0, p)) * apply(down_y, scaled_ref[p] + carry)
    g = carry

    down_rate = oriented(0, 0)
    up_rate = jnp.ones_like(down_rate)
    gains = []
    for p in range(CY):
        gains.append(down_rate * up_rate / oriented(2, p))
        up_rate = up_rate * oriented(1, p)
        if p + 1 < CY:
            down_rate = down_rate * oriented(0, p + 1)
    first = regroup([up_rate, down_rate, gains[0], gains[1]], 32)
    second = regroup([gains[2], gains[3], flip.astype(F32), jnp.zeros_like(up_rate)], 32)
    for x, (fx, gx) in enumerate(zip(columns(f), columns(g))):
        chunks = regroup([fx[:32], fx[32:], gx[:32], gx[32:]], 32)
        for a in range(4):
            row = ROWS * (4 * x + a)
            out_ref[row : row + 32, :] = chunks[a]
            out_ref[row + 32 : row + 33, :] = first[a][x : x + 1]
            out_ref[row + 33 : row + 34, :] = second[a][x : x + 1]


def y_owner_kernel(in_ref, gain_ref, up_ref, down_ref, norm_ref, out_ref, res_ref):
    width, ncol = 32, 8
    flip = replicate(in_ref[33:34, :], width)[2] > 0.5

    def oriented(s):
        t = SY - 1 - s
        return jnp.where(flip, in_ref[ROWS * t : ROWS * (t + 1), :], in_ref[ROWS * s : ROWS * (s + 1), :])

    fs, gs, ss = [], [], []
    for j in range(ncol):
        outs = regroup([oriented(ncol * a + j) for a in range(4)], width)
        fs.append(jnp.concatenate([outs[0][:32], outs[1][:32]], axis=0))
        gs.append(jnp.concatenate([outs[2][:32], outs[3][:32]], axis=0))
        ss.append([o[32:33] for o in outs] + [o[33:34] for o in outs[:2]])
    f = jnp.concatenate(fs, axis=1)
    g = jnp.concatenate(gs, axis=1)
    scalars = [jnp.concatenate([s[k] for s in ss], axis=1) for k in range(6)]
    up_rate = scalars[0] * norm_ref[0:1, 0:1]
    down_rate = scalars[1] * norm_ref[1:2, 0:1]
    h = scan_segments(
        shifted(f, 1, width, ncol, False),
        shifted(up_rate, 1, width, ncol, False),
        up_ref,
        width,
        ncol,
        False,
    )
    through = apply(gain_ref[...], h)
    for p in range(CY):
        g = g + scalars[2 + p] * through[NP * p : NP * (p + 1)]
    e = scan_segments(
        shifted(g, 1, width, ncol, True),
        shifted(down_rate, 1, width, ncol, True),
        down_ref,
        width,
        ncol,
        True,
    )
    for j, (hj, ej) in enumerate(zip(columns(h), columns(e))):
        outs = regroup([hj[:32], hj[32:], ej[:32], ej[32:]], width)
        for a in range(4):
            res_ref[ncol * a + j] = outs[a]
    for s in range(SY):
        out_ref[s] = jnp.where(flip, res_ref[SY - 1 - s], res_ref[s])


def y_final_kernel(local_ref, coef_y_ref, order_ref, parts_ref, from_ref, in_ref, out_ref, solved_ref):
    down = parts_ref[3 * NP :, :]
    flip = order_ref[...] > 0
    flip_row = row_of(order_ref[...]) > 0

    def oriented(which, p):
        return y_rates(coef_y_ref, which, flip, p)

    hs, es = [], []
    for x in range(CX):
        outs = regroup([in_ref[4 * x + a] for a in range(4)], 32)
        hs.append(jnp.concatenate(outs[:2], axis=0))
        es.append(jnp.concatenate(outs[2:], axis=0))
    through = apply(from_ref[...], jnp.concatenate(hs, axis=1))
    up_rates = [jnp.ones((CX, LANES), F32)]
    for p in range(CY - 1):
        up_rates.append(up_rates[-1] * oriented(1, p))
    carry = jnp.concatenate(es, axis=1)
    for p in reversed(range(CY)):
        term = row_of(up_rates[p] / oriented(2, p)) * through[NP * p : NP * (p + 1)]
        g = local_ref[p] + term + carry
        solved_ref[p] = g
        if p > 0:
            carry = row_of(oriented(0, p)) * apply(down, g)
    for y in range(CY):
        plane = jnp.where(flip_row, solved_ref[CY - 1 - y], solved_ref[y])
        for x, block in enumerate(columns(plane)):
            out_ref[pl.ds(CY * x + y, NP, stride=CX * CY), :] = block


def in_hbm(a):
    return pltpu.with_memory_space_constraint(a, pltpu.HBM)


def shape(*dims, dtype=F32):
    return jax.ShapeDtypeStruct(dims, dtype)


def call(kernel, out_shape, n_in, scratch=(), scalars=0, space=pltpu.VMEM):
    whole = pl.BlockSpec(memory_space=pltpu.VMEM)
    specs = [pl.BlockSpec(memory_space=pltpu.SMEM)] * scalars
    specs += [pl.BlockSpec(memory_space=space)] * n_in
    outs = jax.tree.map(lambda _: whole, out_shape)
    return pl.pallas_call(
        kernel,
        out_shape=out_shape,
        in_specs=specs,
        out_specs=outs,
        scratch_shapes=list(scratch),
        compiler_params=pltpu.CompilerParams(vmem_limit_bytes=VMEM_LIMIT),
    )


def prepared_shapes(cells, extra, doublings):
    return (
        shape((cells + extra) * NP, 4 * NP, dtype=BF16),
        shape((cells + extra) * NP, 4 * NP, dtype=BF16),
        shape(doublings, NP, 4 * NP, dtype=BF16),
        shape(doublings, NP, 4 * NP, dtype=BF16),
        shape(8, LANES),
    )


def per_device(
    rhs,
    coef_x,
    coef_y,
    out_coupling_x,
    in_coupling_x,
    inverse_x,
    boundary_inverse,
    out_coupling_y,
    in_coupling_y,
    inverse_y,
    bc_flags,
    line_order,
):
    rank = lax.axis_index("gx").astype(jnp.int32).reshape(1)
    mats = (
        out_coupling_x,
        inverse_x,
        in_coupling_x,
        boundary_inverse,
        out_coupling_y,
        inverse_y,
        in_coupling_y,
    )
    rhs = rhs.reshape(NP, CX * CY, LANES)
    coef_x = coef_x.reshape(3, CX * CY, LANES)
    coef_y = coef_y.reshape(3, CX * CY, LANES)

    sent, local, tiles, raw_y, coef_x, flags, coef_y, order = call(
        x_local_kernel,
        (
            shape(SX, NP + 8, LANES),
            shape(CX, NP, CY * LANES),
            shape(6 * NP, 4 * NP),
            shape(3, NP, NP),
            shape(3, CX * CY, LANES),
            shape(CY, LANES, dtype=jnp.int32),
            shape(3, CX * CY, LANES),
            shape(CX, LANES, dtype=jnp.int32),
        ),
        12,
        [
            pltpu.VMEM((PIECES, NP, 8, LANES), F32),
            pltpu.VMEM((3, NP, NP), F32),
            pltpu.VMEM((3, NP, NP), F32),
            pltpu.SemaphoreType.DMA((11 + PIECES,)),
        ],
        1,
        pltpu.HBM,
    )(rank, *[in_hbm(a) for a in (rhs, coef_x, bc_flags) + mats + (coef_y, line_order)])
    got = lax.all_to_all(sent, "gx", 0, 0, tiled=True)
    prep_shapes = (shape(4 * NP, 4 * NP, dtype=BF16),)
    prep_shapes += prepared_shapes(CX, 3, 3) + prepared_shapes(CY, 0, 5)
    prep = call(prepare_kernel, prep_shapes, 2)(tiles, raw_y)
    parts, gain_x, from_x, up_x, down_x, norm_x, gain_y, from_y, up_y, down_y, norm_y = prep
    back = call(x_owner_kernel, shape(SX, NP, LANES), 5)(got, gain_x, up_x, down_x, norm_x)
    terms = lax.all_to_all(back, "gx", 0, 0, tiled=True)
    local, sent = call(
        middle_kernel,
        (shape(CY, NP, CX * LANES), shape(SY * ROWS, LANES)),
        8,
        [pltpu.VMEM((CY, NP, CX * LANES), F32)],
        1,
    )(rank, local, coef_x, flags, parts, from_x, terms, coef_y, order)
    got = lax.all_to_all(sent.reshape(SY, ROWS // 2, 2, LANES), "gy", 0, 0, tiled=True)
    back = call(
        y_owner_kernel, shape(SY, 32, LANES), 5, [pltpu.VMEM((SY, 32, LANES), F32)]
    )(got.reshape(SY * ROWS, LANES), gain_y, up_y, down_y, norm_y)
    terms = lax.all_to_all(back, "gy", 0, 0, tiled=True)
    out = call(
        y_final_kernel,
        shape(NP * CX * CY, LANES),
        6,
        [pltpu.VMEM((CY, NP, CX * LANES), F32)],
    )(local, coef_y, order, parts, from_y, terms)
    return out.reshape(NP, CX, CY, LANES)


def solution(mesh):
    grid = P(None, "gx", "gy", None)
    in_specs = (grid, grid, grid) + (P(),) * 7 + (P("gy", None), P("gx", None))
    return jax.shard_map(
        per_device, mesh=mesh, in_specs=in_specs, out_specs=grid, check_vma=False
    )
```

```python
import jax
import jax.numpy as jnp
from jax import lax
from jax.experimental import pallas as pl
from jax.experimental.pallas import tpu as pltpu
from jax.sharding import PartitionSpec as P

NP = 64
LANES = 128
CX = 8
PIECES = 4
CY = 4
SX = 8
SY = 32
ROWS = 34
F32 = jnp.float32
BF16 = jnp.bfloat16
VMEM_LIMIT = 48 * 1024 * 1024


def rounded(v):
    return v.astype(BF16).astype(F32)


def split_matrix(m):
    high = rounded(m)
    rest = m - high
    mid = rounded(rest)
    low = rest - mid
    part = lax.broadcasted_iota(jnp.int32, m.shape, 1) // NP
    return jnp.where(part == 1, mid, jnp.where(part == 3, low, high)).astype(BF16)


def split_vectors(v):
    high = v.astype(BF16)
    low = (v - high.astype(F32)).astype(BF16)
    return jnp.concatenate([high, high, low, high], axis=0)


def product(parts, vectors):
    return jnp.dot(parts, vectors, preferred_element_type=F32)


def apply(parts, v):
    return product(parts, split_vectors(v))


def lane_iota(shape):
    return lax.broadcasted_iota(jnp.int32, shape, len(shape) - 1)


def roll(v, shift):
    shift = shift % LANES
    return v if shift == 0 else pltpu.roll(v, shift, 1)


def row_of(block):
    return jnp.concatenate([block[r : r + 1] for r in range(block.shape[0])], axis=1)


def columns(v):
    return [v[:, LANES * j : LANES * (j + 1)] for j in range(v.shape[1] // LANES)]


def regroup(blocks, width):
    n = LANES // width
    rolled = [[roll(b, width * k) for k in range(n)] for b in blocks]
    group = lane_iota(blocks[0].shape) // width
    outs = []
    for a in range(n):
        acc = rolled[0][(0 - a) % n]
        for q in range(1, n):
            acc = jnp.where(group == q, rolled[q][(q - a) % n], acc)
        outs.append(acc)
    return outs


def replicate(block, width):
    return regroup([block] * (LANES // width), width)


def shifted(v, t, width, ncol, reverse):
    cols = columns(v)
    group = lane_iota(cols[0].shape) // width
    n = LANES // width
    out = []
    for j in range(ncol):
        k = j + t if reverse else j - t
        carry = abs(k // ncol)
        src = cols[k % ncol]
        if carry:
            if reverse:
                src = jnp.where(group < n - carry, roll(src, -width * carry), 0.0)
            else:
                src = jnp.where(group >= carry, roll(src, width * carry), 0.0)
        out.append(src)
    return jnp.concatenate(out, axis=1)


def block(stack, k):
    return stack[NP * k : NP * (k + 1)]


def scan_segments(v, rate, powers, counts, width, ncol, reverse):
    stride, row = 1, 0
    for count in counts:
        out = apply(powers[NP * row : NP * (row + count), :], v)
        weight = rate
        for t in range(1, count + 1):
            v = v + weight * shifted(block(out, t - 1), stride * t, width, ncol, reverse)
            weight = rate * shifted(weight, stride, width, ncol, reverse)
        rate = weight
        row += count
        stride *= count + 1
    return v


def tiled(m):
    pair = jnp.concatenate([m, m], axis=0).T
    return jnp.concatenate([pair, pair], axis=1)


def multiply(a, b):
    parts = split_matrix(a)
    high = b.astype(BF16)
    rest = b - high.astype(F32)
    mid = rest.astype(BF16)
    low = (rest - mid.astype(F32)).astype(BF16)
    none = jnp.zeros_like(low)
    return product(parts, jnp.concatenate([high, high, mid, high], axis=0)) + product(
        parts, jnp.concatenate([low, mid, none, none], axis=0)
    )


def powers_of(m, count):
    stack = m
    while stack.shape[0] < count * NP:
        done = stack.shape[0] // NP
        more = min(done, count - done)
        stack = jnp.concatenate([stack, multiply(stack[: NP * more], block(stack, done - 1))], axis=0)
    return stack


def prepare(cells, far, up, down, scale, bounds, gain_ref, from_ref, up_ref, down_ref, norm_ref):
    halves = cells.bit_length() - 1
    ups, downs = [up], [down]
    for _ in range(halves):
        ups.append(multiply(ups[-1], ups[-1]))
        downs.append(multiply(downs[-1], downs[-1]))
    scaled = scale
    stack = down
    for k in range(halves):
        scaled = jnp.concatenate([scaled, multiply(scaled, ups[k])], axis=0)
        stack = jnp.concatenate([stack, multiply(stack, downs[k])], axis=0)
    from_ref[0 : cells * NP, :] = split_matrix(scaled)
    for j in range(cells):
        rows = slice(NP * j, NP * (j + 1))
        gain_ref[rows, :] = split_matrix(multiply(stack[rows], scaled[rows]))
    if bounds is not None:
        for k in range(halves):
            bounds = multiply(bounds, ups[k])
        from_ref[cells * NP :, :] = split_matrix(bounds)
        for kind in range(3):
            rows = slice(NP * (cells + kind), NP * (cells + kind + 1))
            ends = bounds[NP * kind : NP * (kind + 1)]
            gain_ref[rows, :] = split_matrix(multiply(downs[halves], ends))
    norm_ref[...] = jnp.zeros(norm_ref.shape, F32)
    for row, (power, ref) in enumerate(((ups[halves], up_ref), (downs[halves], down_ref))):
        norm = jnp.max(jnp.sum(jnp.abs(power[:, :NP]), axis=1, keepdims=True), axis=0, keepdims=True)
        norm = jnp.maximum(norm, 1e-30)
        norm_ref[row : row + 1, :] = jnp.broadcast_to(norm, (1, LANES))
        power = power / norm
        near = powers_of(power, 7)
        ref[0 : 7 * NP, :] = split_matrix(near)
        if far:
            power8 = multiply(block(near, 3), block(near, 3))
            power16 = multiply(power8, power8)
            power24 = multiply(power16, power8)
            ref[7 * NP :, :] = split_matrix(jnp.concatenate([power8, power16, power24], axis=0))


def prepare_x_kernel(mats_ref, parts_ref, *outs):
    ux, wx, b0, b1, b2, dx = [mats_ref[NP * k : NP * (k + 1), :] for k in range(6)]
    parts_ref[...] = split_matrix(powers_of(dx, 6))
    prepare(CX, False, ux, dx, wx, jnp.concatenate([b0, b1, b2], axis=0), *outs)


def prepare_y_kernel(raw_ref, parts_ref, *outs):
    uy, wy, dy = [tiled(raw_ref[k]) for k in range(3)]
    uy2 = multiply(uy, uy)
    wuy = multiply(jnp.concatenate([wy, uy2], axis=0), uy)
    wuy2 = multiply(wy, uy2)
    stacks = [uy, wy, block(wuy, 0), wuy2, block(wuy, 1), powers_of(dy, 4)]
    parts_ref[...] = split_matrix(jnp.concatenate(stacks, axis=0))
    prepare(CY, True, uy, dy, wy, None, *outs)


def x_rates(coef_ref, which, i):
    return coef_ref[which, CY * i : CY * (i + 1), :]


def x_local_kernel(
    rank_ref,
    rhs_hbm,
    coef_hbm,
    flags_hbm,
    ux,
    wx,
    dx,
    b,
    uy,
    wy,
    dy,
    coef_y_hbm,
    order_hbm,
    out_ref,
    scaled_ref,
    mats_ref,
    raw_y_ref,
    flags_ref,
    coef_y_ref,
    order_ref,
    rhs_ref,
    coef_ref,
    raw_ref,
    bounds_ref,
    sems,
):
    rank = rank_ref[0]
    sources = [ux, wx, b, dx, coef_hbm, flags_hbm]
    targets = [raw_ref.at[0], raw_ref.at[1], bounds_ref, raw_ref.at[2], coef_ref, flags_ref]
    for k in range(PIECES):
        sources.append(rhs_hbm.at[:, 8 * k : 8 * (k + 1), :])
        targets.append(rhs_ref.at[k])
    sources += [uy, wy, dy, coef_y_hbm, order_hbm]
    targets += [raw_y_ref.at[0], raw_y_ref.at[1], raw_y_ref.at[2], coef_y_ref, order_ref]
    copies = []
    for k, (source, target) in enumerate(zip(sources, targets)):
        copies.append(pltpu.make_async_copy(source, target, sems.at[k]))
        copies[-1].start()
    for copy in copies[:6]:
        copy.wait()

    def place(row, m):
        value = tiled(m)
        mats_ref[NP * row : NP * (row + 1), :] = value
        return split_matrix(value)

    up, scale = place(0, raw_ref[0]), place(1, raw_ref[1])
    bounds = [place(2 + k, bounds_ref[k]) for k in range(3)]
    down = place(5, raw_ref[2])
    up_scale = jnp.concatenate([up, scale], axis=0)
    end_stack = jnp.concatenate([up, scale] + bounds, axis=0)
    u, w = mats_ref[0:NP, :], mats_ref[NP : 2 * NP, :]
    d = mats_ref[5 * NP :, :]
    u2 = multiply(u, u)
    wu = split_matrix(multiply(w, u))
    u4 = split_matrix(multiply(u2, u2))
    u2 = split_matrix(u2)
    d2 = multiply(d, d)
    down24 = split_matrix(jnp.concatenate([d2, multiply(d2, d2)], axis=0))
    planes = rhs_ref.reshape(PIECES * NP * 8, LANES)

    ups = [x_rates(coef_ref, 1, i) for i in range(CX)]
    downs = [x_rates(coef_ref, 0, i) for i in range(CX)]
    flags = row_of(flags_ref[...])

    def given(i):
        start = (CY * i // 8) * NP * 8 + CY * i % 8
        return jnp.concatenate(
            [planes[pl.ds(start + y, NP, stride=8), :] for y in range(CY)], axis=1
        )

    def at_end(i, out):
        chosen = jnp.where(
            flags == 0, block(out, 2), jnp.where(flags == 1, block(out, 3), block(out, 4))
        )
        return jnp.where(rank == (0 if i == 0 else SX - 1), chosen, block(out, 1))

    def scaled(i, value):
        value = value * row_of(1.0 / x_rates(coef_ref, 2, i))
        scaled_ref[i] = value
        return value

    s, v, part = [None] * CX, [], []
    for k in range(PIECES):
        copies[6 + k].wait()
        out = apply(end_stack if k == 0 else up_scale, given(2 * k))
        v.append(given(2 * k + 1) + row_of(ups[2 * k]) * block(out, 0))
        part.append(at_end(0, out) if k == 0 else block(out, 1))
    two = [None] + [ups[2 * k] * ups[2 * k - 1] for k in range(1, 4)]
    s[0] = scaled(0, part[0])
    out = apply(jnp.concatenate([scale, wu, u2], axis=0), v[0])
    s[1] = scaled(1, block(out, 0))
    s[2] = scaled(2, part[1] + row_of(ups[1]) * block(out, 1))
    f3 = v[1] + row_of(two[1]) * block(out, 2)
    f7 = v[3] + row_of(two[3]) * apply(u2, v[2])
    out = apply(jnp.concatenate([scale, wu, u2, u4], axis=0), f3)
    s[3] = scaled(3, block(out, 0))
    s[4] = scaled(4, part[2] + row_of(ups[3]) * block(out, 1))
    f5 = v[2] + row_of(two[2]) * block(out, 2)
    f7 = f7 + row_of(two[3] * two[2]) * block(out, 3)
    out = apply(jnp.concatenate([scale, wu], axis=0), f5)
    s[5] = scaled(5, block(out, 0))
    s[6] = scaled(6, part[3] + row_of(ups[5]) * block(out, 1))
    out = apply(end_stack, f7)
    f = row_of(ups[7]) * block(out, 0)
    s[7] = scaled(7, at_end(7, out))
    pair = [s[2 * k] + row_of(downs[2 * k + 1]) * apply(down, s[2 * k + 1]) for k in range(4)]
    two = [downs[2 * k + 1] * downs[2 * k + 2] for k in range(3)]
    first = pair[0] + row_of(two[0]) * apply(down24[:NP], pair[1])
    second = pair[2] + row_of(two[2]) * apply(down24[:NP], pair[3])
    g = first + row_of(two[0] * two[1]) * apply(down24[NP:], second)
    g = row_of(downs[0]) * apply(down, g)
    for copy in copies[6 + PIECES :]:
        copy.wait()
    for y, (fy, gy) in enumerate(zip(columns(f), columns(g))):
        even, odd = regroup([fy, gy], NP)
        out_ref[2 * y, 0:NP, :] = even
        out_ref[2 * y + 1, 0:NP, :] = odd
    down_rate = x_rates(coef_ref, 0, 0)
    up_rate = jnp.ones_like(down_rate)
    gains = []
    for i in range(CX):
        gains.append(down_rate * up_rate / x_rates(coef_ref, 2, i))
        up_rate = up_rate * x_rates(coef_ref, 1, i)
        if i + 1 < CX:
            down_rate = down_rate * x_rates(coef_ref, 0, i + 1)
    last = gains.pop()
    is_last = rank == SX - 1
    flags = flags_ref[...]
    gains.append(jnp.where(is_last, 0.0, last))
    for kind in range(3):
        gains.append(jnp.where(jnp.logical_and(is_last, flags == kind), last, 0.0))
    values = [up_rate, down_rate] + gains + [jnp.zeros_like(last)] * 3
    for r in range(8):
        even, odd = regroup([values[2 * r], values[2 * r + 1]], NP)
        for y in range(CY):
            out_ref[2 * y, NP + r : NP + r + 1, :] = even[y : y + 1]
            out_ref[2 * y + 1, NP + r : NP + r + 1, :] = odd[y : y + 1]


def x_owner_kernel(in_ref, gain_ref, up_ref, down_ref, norm_ref, out_ref):
    half = SX // 2
    fs, gs, sa, sb = [], [], [], []
    for j in range(half):
        f, g = regroup([in_ref[j], in_ref[half + j]], NP)
        fs.append(f[:NP])
        gs.append(g[:NP])
        sa.append(f[NP:])
        sb.append(g[NP:])
    f = jnp.concatenate(fs, axis=1)
    g = jnp.concatenate(gs, axis=1)
    even = jnp.concatenate(sa, axis=1)
    odd = jnp.concatenate(sb, axis=1)
    scalar = [(even if k % 2 == 0 else odd)[k // 2 : k // 2 + 1] for k in range(13)]
    width, ncol = NP, half
    up_rate = scalar[0] * norm_ref[0:1, 0:1]
    down_rate = scalar[1] * norm_ref[1:2, 0:1]
    h = scan_segments(
        shifted(f, 1, width, ncol, False),
        shifted(up_rate, 1, width, ncol, False),
        up_ref,
        (7,),
        width,
        ncol,
        False,
    )
    vectors = split_vectors(h)
    through = product(gain_ref[0 : CX * NP], vectors)
    for i in range(CX):
        g = g + scalar[2 + i] * through[NP * i : NP * (i + 1)]
    ends = product(gain_ref[CX * NP :], vectors[:, LANES * (half - 1) :])
    extra = 0.0
    for kind in range(3):
        extra = extra + (
            scalar[10 + kind][:, LANES * (half - 1) :] * ends[NP * kind : NP * (kind + 1)]
        )
    g = jnp.concatenate([g[:, : LANES * (half - 1)], g[:, LANES * (half - 1) :] + extra], axis=1)
    e = scan_segments(
        shifted(g, 1, width, ncol, True),
        shifted(down_rate, 1, width, ncol, True),
        down_ref,
        (7,),
        width,
        ncol,
        True,
    )
    for j, (hj, ej) in enumerate(zip(columns(h), columns(e))):
        first, second = regroup([hj, ej], NP)
        out_ref[j] = first
        out_ref[half + j] = second


def y_rates(coef_ref, which, flip, p):
    here = coef_ref[which, pl.ds(p, CX, stride=CY), :]
    there = coef_ref[which, pl.ds(CY - 1 - p, CX, stride=CY), :]
    return jnp.where(flip, there, here)


def middle_kernel(
    rank_ref,
    local_ref,
    coef_ref,
    flags_ref,
    parts_ref,
    parts_y_ref,
    from_ref,
    in_ref,
    coef_y_ref,
    order_ref,
    scaled_ref,
    out_ref,
    adj_ref,
):
    rank = rank_ref[0]
    parts = parts_ref[...]
    parts_y = parts_y_ref[...]
    down = parts
    u_y, w_y, wu_y, wu2_y, u3_y = [block(parts_y, k) for k in range(5)]
    up_scale_y = parts_y[: 2 * NP]
    down_y = parts_y[5 * NP :]
    hs, es = [], []
    for y in range(CY):
        h, e = regroup([in_ref[2 * y], in_ref[2 * y + 1]], NP)
        hs.append(h)
        es.append(e)
    through = apply(from_ref[...], jnp.concatenate(hs, axis=1))
    flags = row_of(flags_ref[...])
    up_rates = [jnp.ones((CY, LANES), F32)]
    for i in range(CX - 1):
        up_rates.append(up_rates[-1] * x_rates(coef_ref, 1, i))
    downs = [x_rates(coef_ref, 0, i) for i in range(CX)]

    def scaled(i):
        term = through[NP * i : NP * (i + 1)]
        if i == CX - 1:
            ends = through[NP * CX :]
            chosen = jnp.where(
                flags == 0, ends[:NP], jnp.where(flags == 1, ends[NP : 2 * NP], ends[2 * NP :])
            )
            term = jnp.where(rank == SX - 1, chosen, term)
        return local_ref[i] + row_of(up_rates[i] / x_rates(coef_ref, 2, i)) * term

    def keep(i, g):
        for y in range(CY):
            adj_ref[y, :, LANES * i : LANES * (i + 1)] = g[:, LANES * y : LANES * (y + 1)]

    s = [scaled(i) for i in range(CX)]
    s[7] = s[7] + jnp.concatenate(es, axis=1)
    keep(7, s[7])
    pair = [s[2 * k] + row_of(downs[2 * k + 1]) * apply(block(down, 0), s[2 * k + 1]) for k in range(4)]
    two = [downs[2 * k + 1] * downs[2 * k + 2] for k in range(3)]
    g = [pair[0], s[1], pair[1], s[3], pair[2], s[5]]
    for k in (3, 2, 1):
        out = apply(down[: 2 * k * NP], pair[k])
        weight = None
        for j in reversed(range(k)):
            odd = downs[2 * j + 2] if weight is None else weight * downs[2 * j + 2]
            weight = two[j] if weight is None else weight * two[j]
            power = 2 * (k - j)
            g[2 * j + 1] = g[2 * j + 1] + row_of(odd) * block(out, power - 2)
            g[2 * j] = g[2 * j] + row_of(weight) * block(out, power - 1)
    for i in range(6):
        keep(i, g[i])
    keep(6, pair[3])

    flip = order_ref[...] > 0
    flip_row = row_of(order_ref[...]) > 0

    def oriented(which, p):
        return y_rates(coef_y_ref, which, flip, p)

    a = [jnp.where(flip_row, adj_ref[CY - 1 - p], adj_ref[p]) for p in range(CY)]
    ups = [oriented(1, p) for p in range(CY)]
    downs = [oriented(0, p) for p in range(CY)]
    inverse = [row_of(1.0 / oriented(2, p)) for p in range(CY)]
    out = apply(up_scale_y, a[0])
    f1 = a[1] + row_of(ups[0]) * block(out, 0)
    s = [block(out, 1)]
    out2 = apply(up_scale_y, a[2])
    v3 = a[3] + row_of(ups[2]) * block(out2, 0)
    out1 = apply(jnp.concatenate([w_y, wu_y, wu2_y, u3_y], axis=0), f1)
    out3 = apply(up_scale_y, v3)
    two = ups[1] * ups[2]
    s.append(block(out1, 0))
    s.append(block(out2, 1) + row_of(ups[1]) * block(out1, 1))
    s.append(block(out3, 1) + row_of(two) * block(out1, 2))
    f = row_of(ups[3]) * block(out3, 0) + row_of(ups[3] * two) * block(out1, 3)
    g, weight = 0.0, downs[0]
    for p in range(CY):
        value = s[p] * inverse[p]
        scaled_ref[p] = value
        g = g + row_of(weight) * apply(block(down_y, p), value)
        if p + 1 < CY:
            weight = weight * downs[p + 1]

    down_rate = oriented(0, 0)
    up_rate = jnp.ones_like(down_rate)
    gains = []
    for p in range(CY):
        gains.append(down_rate * up_rate / oriented(2, p))
        up_rate = up_rate * oriented(1, p)
        if p + 1 < CY:
            down_rate = down_rate * oriented(0, p + 1)
    first = regroup([up_rate, down_rate, gains[0], gains[1]], 32)
    second = regroup([gains[2], gains[3], flip.astype(F32), jnp.zeros_like(up_rate)], 32)
    for x, (fx, gx) in enumerate(zip(columns(f), columns(g))):
        chunks = regroup([fx[:32], fx[32:], gx[:32], gx[32:]], 32)
        for a in range(4):
            row = ROWS * (4 * x + a)
            out_ref[row : row + 32, :] = chunks[a]
            out_ref[row + 32 : row + 33, :] = first[a][x : x + 1]
            out_ref[row + 33 : row + 34, :] = second[a][x : x + 1]


def y_owner_kernel(in_ref, gain_ref, up_ref, down_ref, norm_ref, out_ref, res_ref):
    width, ncol = 32, 8
    flip = replicate(in_ref[33:34, :], width)[2] > 0.5

    def oriented(s):
        t = SY - 1 - s
        return jnp.where(flip, in_ref[ROWS * t : ROWS * (t + 1), :], in_ref[ROWS * s : ROWS * (s + 1), :])

    fs, gs, ss = [], [], []
    for j in range(ncol):
        outs = regroup([oriented(ncol * a + j) for a in range(4)], width)
        fs.append(jnp.concatenate([outs[0][:32], outs[1][:32]], axis=0))
        gs.append(jnp.concatenate([outs[2][:32], outs[3][:32]], axis=0))
        ss.append([o[32:33] for o in outs] + [o[33:34] for o in outs[:2]])
    f = jnp.concatenate(fs, axis=1)
    g = jnp.concatenate(gs, axis=1)
    scalars = [jnp.concatenate([s[k] for s in ss], axis=1) for k in range(6)]
    up_rate = scalars[0] * norm_ref[0:1, 0:1]
    down_rate = scalars[1] * norm_ref[1:2, 0:1]
    h = scan_segments(
        shifted(f, 1, width, ncol, False),
        shifted(up_rate, 1, width, ncol, False),
        up_ref,
        (7, 3),
        width,
        ncol,
        False,
    )
    through = apply(gain_ref[...], h)
    for p in range(CY):
        g = g + scalars[2 + p] * through[NP * p : NP * (p + 1)]
    e = scan_segments(
        shifted(g, 1, width, ncol, True),
        shifted(down_rate, 1, width, ncol, True),
        down_ref,
        (7, 3),
        width,
        ncol,
        True,
    )
    for j, (hj, ej) in enumerate(zip(columns(h), columns(e))):
        outs = regroup([hj[:32], hj[32:], ej[:32], ej[32:]], width)
        for a in range(4):
            res_ref[ncol * a + j] = outs[a]
    for s in range(SY):
        out_ref[s] = jnp.where(flip, res_ref[SY - 1 - s], res_ref[s])


def y_final_kernel(local_ref, coef_y_ref, order_ref, parts_ref, from_ref, in_ref, out_ref, solved_ref):
    down = parts_ref[5 * NP : 8 * NP, :]
    flip = order_ref[...] > 0
    flip_row = row_of(order_ref[...]) > 0

    def oriented(which, p):
        return y_rates(coef_y_ref, which, flip, p)

    hs, es = [], []
    for x in range(CX):
        outs = regroup([in_ref[4 * x + a] for a in range(4)], 32)
        hs.append(jnp.concatenate(outs[:2], axis=0))
        es.append(jnp.concatenate(outs[2:], axis=0))
    through = apply(from_ref[...], jnp.concatenate(hs, axis=1))
    up_rates = [jnp.ones((CX, LANES), F32)]
    for p in range(CY - 1):
        up_rates.append(up_rates[-1] * oriented(1, p))
    downs = [oriented(0, p) for p in range(CY)]
    s = []
    for p in range(CY):
        term = row_of(up_rates[p] / oriented(2, p)) * through[NP * p : NP * (p + 1)]
        s.append(local_ref[p] + term)
    s[3] = s[3] + jnp.concatenate(es, axis=1)
    g = list(s)
    for p in (3, 2, 1):
        out = apply(down[: NP * p], s[p])
        weight = None
        for j in reversed(range(p)):
            weight = downs[j + 1] if weight is None else weight * downs[j + 1]
            g[j] = g[j] + row_of(weight) * block(out, p - 1 - j)
    for p in range(CY):
        solved_ref[p] = g[p]
    for y in range(CY):
        plane = jnp.where(flip_row, solved_ref[CY - 1 - y], solved_ref[y])
        for x, piece in enumerate(columns(plane)):
            out_ref[pl.ds(CY * x + y, NP, stride=CX * CY), :] = piece


def in_hbm(a):
    return pltpu.with_memory_space_constraint(a, pltpu.HBM)


def shape(*dims, dtype=F32):
    return jax.ShapeDtypeStruct(dims, dtype)


def call(kernel, out_shape, n_in, scratch=(), scalars=0, space=pltpu.VMEM):
    whole = pl.BlockSpec(memory_space=pltpu.VMEM)
    specs = [pl.BlockSpec(memory_space=pltpu.SMEM)] * scalars
    specs += [pl.BlockSpec(memory_space=space)] * n_in
    outs = jax.tree.map(lambda _: whole, out_shape)
    return pl.pallas_call(
        kernel,
        out_shape=out_shape,
        in_specs=specs,
        out_specs=outs,
        scratch_shapes=list(scratch),
        compiler_params=pltpu.CompilerParams(vmem_limit_bytes=VMEM_LIMIT),
    )


def prepared_shapes(cells, extra, powers):
    return (
        shape((cells + extra) * NP, 4 * NP, dtype=BF16),
        shape((cells + extra) * NP, 4 * NP, dtype=BF16),
        shape(powers * NP, 4 * NP, dtype=BF16),
        shape(powers * NP, 4 * NP, dtype=BF16),
        shape(8, LANES),
    )


def per_device(
    rhs,
    coef_x,
    coef_y,
    out_coupling_x,
    in_coupling_x,
    inverse_x,
    boundary_inverse,
    out_coupling_y,
    in_coupling_y,
    inverse_y,
    bc_flags,
    line_order,
):
    rank = lax.axis_index("gx").astype(jnp.int32).reshape(1)
    mats = (
        out_coupling_x,
        inverse_x,
        in_coupling_x,
        boundary_inverse,
        out_coupling_y,
        inverse_y,
        in_coupling_y,
    )
    rhs = rhs.reshape(NP, CX * CY, LANES)
    coef_x = coef_x.reshape(3, CX * CY, LANES)
    coef_y = coef_y.reshape(3, CX * CY, LANES)

    sent, local, tiles, raw_y, flags, coef_y, order = call(
        x_local_kernel,
        (
            shape(SX, NP + 8, LANES),
            shape(CX, NP, CY * LANES),
            shape(6 * NP, 4 * NP),
            shape(3, NP, NP),
            shape(CY, LANES, dtype=jnp.int32),
            shape(3, CX * CY, LANES),
            shape(CX, LANES, dtype=jnp.int32),
        ),
        12,
        [
            pltpu.VMEM((PIECES, NP, 8, LANES), F32),
            pltpu.VMEM((3, CX * CY, LANES), F32),
            pltpu.VMEM((3, NP, NP), F32),
            pltpu.VMEM((3, NP, NP), F32),
            pltpu.SemaphoreType.DMA((11 + PIECES,)),
        ],
        1,
        pltpu.HBM,
    )(rank, *[in_hbm(a) for a in (rhs, coef_x, bc_flags) + mats + (coef_y, line_order)])
    got = lax.all_to_all(sent, "gx", 0, 0, tiled=True)
    parts_x, gain_x, from_x, up_x, down_x, norm_x = call(
        prepare_x_kernel,
        (shape(6 * NP, 4 * NP, dtype=BF16),) + prepared_shapes(CX, 3, 7),
        1,
    )(tiles)
    back = call(x_owner_kernel, shape(SX, NP, LANES), 5)(got, gain_x, up_x, down_x, norm_x)
    raw_y, back = lax.optimization_barrier((raw_y, back))
    terms = lax.all_to_all(back, "gx", 0, 0, tiled=True)
    parts_y, gain_y, from_y, up_y, down_y, norm_y = call(
        prepare_y_kernel,
        (shape(9 * NP, 4 * NP, dtype=BF16),) + prepared_shapes(CY, 0, 10),
        1,
    )(raw_y)
    local, sent = call(
        middle_kernel,
        (shape(CY, NP, CX * LANES), shape(SY * ROWS, LANES)),
        9,
        [pltpu.VMEM((CY, NP, CX * LANES), F32)],
        1,
    )(rank, local, coef_x, flags, parts_x, parts_y, from_x, terms, coef_y, order)
    got = lax.all_to_all(sent.reshape(SY, ROWS // 2, 2, LANES), "gy", 0, 0, tiled=True)
    back = call(
        y_owner_kernel, shape(SY, 32, LANES), 5, [pltpu.VMEM((SY, 32, LANES), F32)]
    )(got.reshape(SY * ROWS, LANES), gain_y, up_y, down_y, norm_y)
    terms = lax.all_to_all(back, "gy", 0, 0, tiled=True)
    out = call(
        y_final_kernel,
        shape(NP * CX * CY, LANES),
        6,
        [pltpu.VMEM((CY, NP, CX * LANES), F32)],
    )(local, coef_y, order, parts_y, from_y, terms)
    return out.reshape(NP, CX, CY, LANES)


def solution(mesh):
    grid = P(None, "gx", "gy", None)
    in_specs = (grid, grid, grid) + (P(),) * 7 + (P("gy", None), P("gx", None))
    return jax.shard_map(
        per_device, mesh=mesh, in_specs=in_specs, out_specs=grid, check_vma=False
    )
```

```python
import jax
import jax.numpy as jnp
from jax import lax
from jax.experimental import pallas as pl
from jax.experimental.pallas import tpu as pltpu
from jax.sharding import PartitionSpec as P

NP = 64
LANES = 128
CX = 8
PIECES = 4
HALVES = 2
CY = 4
SX = 8
SY = 32
ROWS = 34
F32 = jnp.float32
BF16 = jnp.bfloat16
VMEM_LIMIT = 48 * 1024 * 1024


def rounded(v):
    return v.astype(BF16).astype(F32)


def split_matrix(m):
    high = rounded(m)
    rest = m - high
    mid = rounded(rest)
    low = rest - mid
    part = lax.broadcasted_iota(jnp.int32, m.shape, 1) // NP
    return jnp.where(part == 1, mid, jnp.where(part == 3, low, high)).astype(BF16)


def split_vectors(v):
    high = v.astype(BF16)
    low = (v - high.astype(F32)).astype(BF16)
    return jnp.concatenate([high, high, low, high], axis=0)


def product(parts, vectors):
    return jnp.dot(parts, vectors, preferred_element_type=F32)


def apply(parts, v):
    return product(parts, split_vectors(v))


def lane_iota(shape):
    return lax.broadcasted_iota(jnp.int32, shape, len(shape) - 1)


def roll(v, shift):
    shift = shift % LANES
    return v if shift == 0 else pltpu.roll(v, shift, 1)


def row_of(block):
    return jnp.concatenate([block[r : r + 1] for r in range(block.shape[0])], axis=1)


def columns(v):
    return [v[:, LANES * j : LANES * (j + 1)] for j in range(v.shape[1] // LANES)]


def regroup(blocks, width):
    n = LANES // width
    rolled = [[roll(b, width * k) for k in range(n)] for b in blocks]
    group = lane_iota(blocks[0].shape) // width
    outs = []
    for a in range(n):
        acc = rolled[0][(0 - a) % n]
        for q in range(1, n):
            acc = jnp.where(group == q, rolled[q][(q - a) % n], acc)
        outs.append(acc)
    return outs


def replicate(block, width):
    return regroup([block] * (LANES // width), width)


def shifted(v, t, width, ncol, reverse):
    cols = columns(v)
    group = lane_iota(cols[0].shape) // width
    n = LANES // width
    out = []
    for j in range(ncol):
        k = j + t if reverse else j - t
        carry = abs(k // ncol)
        src = cols[k % ncol]
        if carry:
            if reverse:
                src = jnp.where(group < n - carry, roll(src, -width * carry), 0.0)
            else:
                src = jnp.where(group >= carry, roll(src, width * carry), 0.0)
        out.append(src)
    return jnp.concatenate(out, axis=1)


def block(stack, k):
    return stack[NP * k : NP * (k + 1)]


def scan_segments(v, rate, powers, counts, width, ncol, reverse):
    stride, row = 1, 0
    for count in counts:
        out = apply(powers[NP * row : NP * (row + count), :], v)
        weight = rate
        for t in range(1, count + 1):
            v = v + weight * shifted(block(out, t - 1), stride * t, width, ncol, reverse)
            weight = rate * shifted(weight, stride, width, ncol, reverse)
        rate = weight
        row += count
        stride *= count + 1
    return v


def tiled(m):
    pair = jnp.concatenate([m, m], axis=0).T
    return jnp.concatenate([pair, pair], axis=1)


def multiply(a, b):
    parts = split_matrix(a)
    high = b.astype(BF16)
    rest = b - high.astype(F32)
    mid = rest.astype(BF16)
    low = (rest - mid.astype(F32)).astype(BF16)
    none = jnp.zeros_like(low)
    return product(parts, jnp.concatenate([high, high, mid, high], axis=0)) + product(
        parts, jnp.concatenate([low, mid, none, none], axis=0)
    )


def powers_of(m, count):
    stack = m
    while stack.shape[0] < count * NP:
        done = stack.shape[0] // NP
        more = min(done, count - done)
        stack = jnp.concatenate([stack, multiply(stack[: NP * more], block(stack, done - 1))], axis=0)
    return stack


def prepare(cells, far, up, down, scale, bounds, gain_ref, from_ref, up_ref, down_ref, norm_ref):
    halves = cells.bit_length() - 1
    ups = [up]
    for _ in range(halves):
        ups.append(multiply(ups[-1], ups[-1]))
    scaled = scale
    for k in range(halves):
        scaled = jnp.concatenate([scaled, multiply(scaled, ups[k])], axis=0)
    downs = powers_of(down, cells)
    stack = split_matrix(downs)
    from_ref[0 : cells * NP, :] = split_matrix(scaled)
    for j in range(cells):
        gain = apply(block(stack, j), block(scaled, j))
        gain_ref[NP * j : NP * (j + 1), :] = split_matrix(gain)
    if bounds is not None:
        for k in range(halves):
            bounds = multiply(bounds, ups[k])
        from_ref[cells * NP :, :] = split_matrix(bounds)
        for kind in range(3):
            gain = apply(block(stack, cells - 1), block(bounds, kind))
            gain_ref[NP * (cells + kind) : NP * (cells + kind + 1), :] = split_matrix(gain)
    norm_ref[...] = jnp.zeros(norm_ref.shape, F32)
    tops = ((ups[halves], up_ref), (block(downs, cells - 1), down_ref))
    for row, (power, ref) in enumerate(tops):
        norm = jnp.max(jnp.sum(jnp.abs(power[:, :NP]), axis=1, keepdims=True), axis=0, keepdims=True)
        norm = jnp.maximum(norm, 1e-30)
        norm_ref[row : row + 1, :] = jnp.broadcast_to(norm, (1, LANES))
        near = powers_of(power / norm, 7)
        ref[0 : 7 * NP, :] = split_matrix(near)
        if far:
            power8 = multiply(block(near, 3), block(near, 3))
            power16 = multiply(power8, power8)
            power24 = multiply(power16, power8)
            ref[7 * NP :, :] = split_matrix(jnp.concatenate([power8, power16, power24], axis=0))
    return ups, scaled, stack


def prepare_kernel(mats_ref, raw_ref, parts_ref, parts_y_ref, *outs):
    ux, wx, b0, b1, b2, dx = [mats_ref[NP * k : NP * (k + 1), :] for k in range(6)]
    bounds = jnp.concatenate([b0, b1, b2], axis=0)
    _, _, stack = prepare(CX, False, ux, dx, wx, bounds, *outs[:5])
    parts_ref[...] = stack[: 6 * NP]
    uy, wy, dy = [tiled(raw_ref[k]) for k in range(3)]
    ups, scaled, stack = prepare(CY, True, uy, dy, wy, None, *outs[5:])
    extra = [uy, scaled[: 3 * NP], multiply(ups[1], uy)]
    parts_y_ref[0 : 5 * NP, :] = split_matrix(jnp.concatenate(extra, axis=0))
    parts_y_ref[5 * NP :, :] = stack


def x_rates(coef_ref, which, i):
    return coef_ref[which, CY * i : CY * (i + 1), :]


def x_local_kernel(
    rank_ref,
    rhs_hbm,
    coef_hbm,
    flags_hbm,
    ux,
    wx,
    dx,
    b,
    uy,
    wy,
    dy,
    coef_y_hbm,
    order_hbm,
    out_ref,
    scaled_ref,
    mats_ref,
    raw_y_ref,
    flags_ref,
    coef_y_ref,
    order_ref,
    rhs_ref,
    coef_ref,
    raw_ref,
    bounds_ref,
    sems,
):
    rank = rank_ref[0]
    sources = [ux, wx, b, dx, coef_hbm, flags_hbm]
    targets = [raw_ref.at[0], raw_ref.at[1], bounds_ref, raw_ref.at[2], coef_ref, flags_ref]
    for k in range(PIECES):
        sources.append(rhs_hbm.at[:, 8 * k : 8 * (k + 1), :])
        targets.append(rhs_ref.at[k])
    sources += [uy, wy, dy, coef_y_hbm, order_hbm]
    targets += [raw_y_ref.at[0], raw_y_ref.at[1], raw_y_ref.at[2], coef_y_ref, order_ref]
    copies = []
    for k, (source, target) in enumerate(zip(sources, targets)):
        copies.append(pltpu.make_async_copy(source, target, sems.at[k]))
        copies[-1].start()
    for copy in copies[:6]:
        copy.wait()

    def place(row, m):
        value = tiled(m)
        mats_ref[NP * row : NP * (row + 1), :] = value
        return split_matrix(value)

    up, scale = place(0, raw_ref[0]), place(1, raw_ref[1])
    bounds = [place(2 + k, bounds_ref[k]) for k in range(3)]
    down = place(5, raw_ref[2])
    up_scale = jnp.concatenate([up, scale], axis=0)
    end_stack = jnp.concatenate([up, scale] + bounds, axis=0)
    u, w = mats_ref[0:NP, :], mats_ref[NP : 2 * NP, :]
    d = mats_ref[5 * NP :, :]
    u2 = multiply(u, u)
    wu = split_matrix(multiply(w, u))
    u4 = split_matrix(multiply(u2, u2))
    u2 = split_matrix(u2)
    d2 = multiply(d, d)
    down24 = split_matrix(jnp.concatenate([d2, multiply(d2, d2)], axis=0))
    planes = rhs_ref.reshape(PIECES * NP * 8, LANES)

    ups = [x_rates(coef_ref, 1, i) for i in range(CX)]
    downs = [x_rates(coef_ref, 0, i) for i in range(CX)]
    flags = row_of(flags_ref[...])

    def given(i):
        start = (CY * i // 8) * NP * 8 + CY * i % 8
        return jnp.concatenate(
            [planes[pl.ds(start + y, NP, stride=8), :] for y in range(CY)], axis=1
        )

    def at_end(i, out):
        chosen = jnp.where(
            flags == 0, block(out, 2), jnp.where(flags == 1, block(out, 3), block(out, 4))
        )
        return jnp.where(rank == (0 if i == 0 else SX - 1), chosen, block(out, 1))

    def scaled(i, value):
        value = value * row_of(1.0 / x_rates(coef_ref, 2, i))
        scaled_ref[i] = value
        return value

    s, v, part = [None] * CX, [], []
    for k in range(PIECES):
        copies[6 + k].wait()
        out = apply(end_stack if k == 0 else up_scale, given(2 * k))
        v.append(given(2 * k + 1) + row_of(ups[2 * k]) * block(out, 0))
        part.append(at_end(0, out) if k == 0 else block(out, 1))
    two = [None] + [ups[2 * k] * ups[2 * k - 1] for k in range(1, 4)]
    s[0] = scaled(0, part[0])
    out = apply(jnp.concatenate([scale, wu, u2], axis=0), v[0])
    s[1] = scaled(1, block(out, 0))
    s[2] = scaled(2, part[1] + row_of(ups[1]) * block(out, 1))
    f3 = v[1] + row_of(two[1]) * block(out, 2)
    f7 = v[3] + row_of(two[3]) * apply(u2, v[2])
    out = apply(jnp.concatenate([scale, wu, u2, u4], axis=0), f3)
    s[3] = scaled(3, block(out, 0))
    s[4] = scaled(4, part[2] + row_of(ups[3]) * block(out, 1))
    f5 = v[2] + row_of(two[2]) * block(out, 2)
    f7 = f7 + row_of(two[3] * two[2]) * block(out, 3)
    out = apply(jnp.concatenate([scale, wu], axis=0), f5)
    s[5] = scaled(5, block(out, 0))
    s[6] = scaled(6, part[3] + row_of(ups[5]) * block(out, 1))
    out = apply(end_stack, f7)
    f = row_of(ups[7]) * block(out, 0)
    s[7] = scaled(7, at_end(7, out))
    pair = [s[2 * k] + row_of(downs[2 * k + 1]) * apply(down, s[2 * k + 1]) for k in range(4)]
    two = [downs[2 * k + 1] * downs[2 * k + 2] for k in range(3)]
    first = pair[0] + row_of(two[0]) * apply(down24[:NP], pair[1])
    second = pair[2] + row_of(two[2]) * apply(down24[:NP], pair[3])
    g = first + row_of(two[0] * two[1]) * apply(down24[NP:], second)
    g = row_of(downs[0]) * apply(down, g)
    for copy in copies[6 + PIECES :]:
        copy.wait()
    for y, (fy, gy) in enumerate(zip(columns(f), columns(g))):
        even, odd = regroup([fy, gy], NP)
        out_ref[2 * y, 0:NP, :] = even
        out_ref[2 * y + 1, 0:NP, :] = odd
    down_rate = x_rates(coef_ref, 0, 0)
    up_rate = jnp.ones_like(down_rate)
    gains = []
    for i in range(CX):
        gains.append(down_rate * up_rate / x_rates(coef_ref, 2, i))
        up_rate = up_rate * x_rates(coef_ref, 1, i)
        if i + 1 < CX:
            down_rate = down_rate * x_rates(coef_ref, 0, i + 1)
    last = gains.pop()
    is_last = rank == SX - 1
    flags = flags_ref[...]
    gains.append(jnp.where(is_last, 0.0, last))
    for kind in range(3):
        gains.append(jnp.where(jnp.logical_and(is_last, flags == kind), last, 0.0))
    values = [up_rate, down_rate] + gains + [jnp.zeros_like(last)] * 3
    for r in range(8):
        even, odd = regroup([values[2 * r], values[2 * r + 1]], NP)
        for y in range(CY):
            out_ref[2 * y, NP + r : NP + r + 1, :] = even[y : y + 1]
            out_ref[2 * y + 1, NP + r : NP + r + 1, :] = odd[y : y + 1]


def x_owner_kernel(in_ref, gain_ref, up_ref, down_ref, norm_ref, out_ref):
    half = SX // 2
    fs, gs, sa, sb = [], [], [], []
    for j in range(half):
        f, g = regroup([in_ref[j], in_ref[half + j]], NP)
        fs.append(f[:NP])
        gs.append(g[:NP])
        sa.append(f[NP:])
        sb.append(g[NP:])
    f = jnp.concatenate(fs, axis=1)
    g = jnp.concatenate(gs, axis=1)
    even = jnp.concatenate(sa, axis=1)
    odd = jnp.concatenate(sb, axis=1)
    scalar = [(even if k % 2 == 0 else odd)[k // 2 : k // 2 + 1] for k in range(13)]
    width, ncol = NP, half
    up_rate = scalar[0] * norm_ref[0:1, 0:1]
    down_rate = scalar[1] * norm_ref[1:2, 0:1]
    h = scan_segments(
        shifted(f, 1, width, ncol, False),
        shifted(up_rate, 1, width, ncol, False),
        up_ref,
        (7,),
        width,
        ncol,
        False,
    )
    vectors = split_vectors(h)
    through = product(gain_ref[0 : CX * NP], vectors)
    for i in range(CX):
        g = g + scalar[2 + i] * through[NP * i : NP * (i + 1)]
    ends = product(gain_ref[CX * NP :], vectors[:, LANES * (half - 1) :])
    extra = 0.0
    for kind in range(3):
        extra = extra + (
            scalar[10 + kind][:, LANES * (half - 1) :] * ends[NP * kind : NP * (kind + 1)]
        )
    g = jnp.concatenate([g[:, : LANES * (half - 1)], g[:, LANES * (half - 1) :] + extra], axis=1)
    e = scan_segments(
        shifted(g, 1, width, ncol, True),
        shifted(down_rate, 1, width, ncol, True),
        down_ref,
        (7,),
        width,
        ncol,
        True,
    )
    for j, (hj, ej) in enumerate(zip(columns(h), columns(e))):
        first, second = regroup([hj, ej], NP)
        out_ref[j] = first
        out_ref[half + j] = second


def y_rates(coef_ref, which, flip, p):
    here = coef_ref[which, pl.ds(p, CX, stride=CY), :]
    there = coef_ref[which, pl.ds(CY - 1 - p, CX, stride=CY), :]
    return jnp.where(flip, there, here)


def middle_kernel(
    rank_ref,
    local_ref,
    coef_ref,
    flags_ref,
    parts_ref,
    parts_y_ref,
    from_ref,
    in_ref,
    coef_y_ref,
    order_ref,
    scaled_ref,
    out_ref,
    adj_ref,
):
    rank = rank_ref[0]
    parts = parts_ref[...]
    parts_y = parts_y_ref[...]
    down = parts
    u_y, w_y, wu_y, wu2_y, u3_y = [block(parts_y, k) for k in range(5)]
    up_scale_y = parts_y[: 2 * NP]
    down_y = parts_y[5 * NP :]
    hs, es = [], []
    for y in range(CY):
        h, e = regroup([in_ref[2 * y], in_ref[2 * y + 1]], NP)
        hs.append(h)
        es.append(e)
    through = apply(from_ref[...], jnp.concatenate(hs, axis=1))
    flags = row_of(flags_ref[...])
    up_rates = [jnp.ones((CY, LANES), F32)]
    for i in range(CX - 1):
        up_rates.append(up_rates[-1] * x_rates(coef_ref, 1, i))
    downs = [x_rates(coef_ref, 0, i) for i in range(CX)]

    def scaled(i):
        term = through[NP * i : NP * (i + 1)]
        if i == CX - 1:
            ends = through[NP * CX :]
            chosen = jnp.where(
                flags == 0, ends[:NP], jnp.where(flags == 1, ends[NP : 2 * NP], ends[2 * NP :])
            )
            term = jnp.where(rank == SX - 1, chosen, term)
        return local_ref[i] + row_of(up_rates[i] / x_rates(coef_ref, 2, i)) * term

    def keep(i, g):
        for y in range(CY):
            adj_ref[y, :, LANES * i : LANES * (i + 1)] = g[:, LANES * y : LANES * (y + 1)]

    s = [scaled(i) for i in range(CX)]
    s[7] = s[7] + jnp.concatenate(es, axis=1)
    keep(7, s[7])
    pair = [s[2 * k] + row_of(downs[2 * k + 1]) * apply(block(down, 0), s[2 * k + 1]) for k in range(4)]
    two = [downs[2 * k + 1] * downs[2 * k + 2] for k in range(3)]
    g = [pair[0], s[1], pair[1], s[3], pair[2], s[5]]
    for k in (3, 2, 1):
        out = apply(down[: 2 * k * NP], pair[k])
        weight = None
        for j in reversed(range(k)):
            odd = downs[2 * j + 2] if weight is None else weight * downs[2 * j + 2]
            weight = two[j] if weight is None else weight * two[j]
            power = 2 * (k - j)
            g[2 * j + 1] = g[2 * j + 1] + row_of(odd) * block(out, power - 2)
            g[2 * j] = g[2 * j] + row_of(weight) * block(out, power - 1)
    for i in range(6):
        keep(i, g[i])
    keep(6, pair[3])

    flip = order_ref[...] > 0
    flip_row = row_of(order_ref[...]) > 0

    def oriented(which, p):
        return y_rates(coef_y_ref, which, flip, p)

    a = [jnp.where(flip_row, adj_ref[CY - 1 - p], adj_ref[p]) for p in range(CY)]
    ups = [oriented(1, p) for p in range(CY)]
    downs = [oriented(0, p) for p in range(CY)]
    inverse = [row_of(1.0 / oriented(2, p)) for p in range(CY)]
    out = apply(up_scale_y, a[0])
    f1 = a[1] + row_of(ups[0]) * block(out, 0)
    s = [block(out, 1)]
    out2 = apply(up_scale_y, a[2])
    v3 = a[3] + row_of(ups[2]) * block(out2, 0)
    out1 = apply(jnp.concatenate([w_y, wu_y, wu2_y, u3_y], axis=0), f1)
    out3 = apply(up_scale_y, v3)
    two = ups[1] * ups[2]
    s.append(block(out1, 0))
    s.append(block(out2, 1) + row_of(ups[1]) * block(out1, 1))
    s.append(block(out3, 1) + row_of(two) * block(out1, 2))
    f = row_of(ups[3]) * block(out3, 0) + row_of(ups[3] * two) * block(out1, 3)
    g, weight = 0.0, downs[0]
    for p in range(CY):
        value = s[p] * inverse[p]
        scaled_ref[p] = value
        g = g + row_of(weight) * apply(block(down_y, p), value)
        if p + 1 < CY:
            weight = weight * downs[p + 1]

    down_rate = oriented(0, 0)
    up_rate = jnp.ones_like(down_rate)
    gains = []
    for p in range(CY):
        gains.append(down_rate * up_rate / oriented(2, p))
        up_rate = up_rate * oriented(1, p)
        if p + 1 < CY:
            down_rate = down_rate * oriented(0, p + 1)
    first = regroup([up_rate, down_rate, gains[0], gains[1]], 32)
    second = regroup([gains[2], gains[3], flip.astype(F32), jnp.zeros_like(up_rate)], 32)
    for x, (fx, gx) in enumerate(zip(columns(f), columns(g))):
        chunks = regroup([fx[:32], fx[32:], gx[:32], gx[32:]], 32)
        for a in range(4):
            row = ROWS * (4 * x + a)
            out_ref[row : row + 32, :] = chunks[a]
            out_ref[row + 32 : row + 33, :] = first[a][x : x + 1]
            out_ref[row + 33 : row + 34, :] = second[a][x : x + 1]


def y_owner_kernel(in_ref, gain_ref, up_ref, down_ref, norm_ref, out_ref, res_ref):
    width, ncol = 32, 8
    flip = replicate(in_ref[33:34, :], width)[2] > 0.5

    def oriented(s):
        t = SY - 1 - s
        return jnp.where(flip, in_ref[ROWS * t : ROWS * (t + 1), :], in_ref[ROWS * s : ROWS * (s + 1), :])

    fs, gs, ss = [], [], []
    for j in range(ncol):
        outs = regroup([oriented(ncol * a + j) for a in range(4)], width)
        fs.append(jnp.concatenate([outs[0][:32], outs[1][:32]], axis=0))
        gs.append(jnp.concatenate([outs[2][:32], outs[3][:32]], axis=0))
        ss.append([o[32:33] for o in outs] + [o[33:34] for o in outs[:2]])
    f = jnp.concatenate(fs, axis=1)
    g = jnp.concatenate(gs, axis=1)
    scalars = [jnp.concatenate([s[k] for s in ss], axis=1) for k in range(6)]
    up_rate = scalars[0] * norm_ref[0:1, 0:1]
    down_rate = scalars[1] * norm_ref[1:2, 0:1]
    h = scan_segments(
        shifted(f, 1, width, ncol, False),
        shifted(up_rate, 1, width, ncol, False),
        up_ref,
        (7, 3),
        width,
        ncol,
        False,
    )
    through = apply(gain_ref[...], h)
    for p in range(CY):
        g = g + scalars[2 + p] * through[NP * p : NP * (p + 1)]
    e = scan_segments(
        shifted(g, 1, width, ncol, True),
        shifted(down_rate, 1, width, ncol, True),
        down_ref,
        (7, 3),
        width,
        ncol,
        True,
    )
    for j, (hj, ej) in enumerate(zip(columns(h), columns(e))):
        outs = regroup([hj[:32], hj[32:], ej[:32], ej[32:]], width)
        for a in range(4):
            res_ref[ncol * a + j] = outs[a]
    for s in range(SY):
        out_ref[s] = jnp.where(flip, res_ref[SY - 1 - s], res_ref[s])


def y_final_kernel(
    local_ref, coef_y_ref, order_ref, parts_ref, from_ref, in_ref, out_hbm, out_ref, sems
):
    down = parts_ref[5 * NP : 8 * NP, :]
    flip = order_ref[...] > 0

    def oriented(which, p):
        return y_rates(coef_y_ref, which, flip, p)

    up_rates = [jnp.ones((CX, LANES), F32)]
    for p in range(CY - 1):
        up_rates.append(up_rates[-1] * oriented(1, p))
    term_rates = [up_rates[p] / oriented(2, p) for p in range(CY)]
    downs = [oriented(0, p) for p in range(CY)]
    part = CX // HALVES
    copies = []
    for half in range(HALVES):
        first = part * half
        lanes = slice(LANES * first, LANES * (first + part))

        def row(rate):
            return row_of(rate[first : first + part])

        hs, es = [], []
        for x in range(first, first + part):
            outs = regroup([in_ref[4 * x + a] for a in range(4)], 32)
            hs.append(jnp.concatenate(outs[:2], axis=0))
            es.append(jnp.concatenate(outs[2:], axis=0))
        through = apply(from_ref[...], jnp.concatenate(hs, axis=1))
        s = [local_ref[p, :, lanes] + row(term_rates[p]) * block(through, p) for p in range(CY)]
        s[3] = s[3] + jnp.concatenate(es, axis=1)
        g = list(s)
        for p in (3, 2, 1):
            out = apply(down[: NP * p], s[p])
            weight = None
            for j in reversed(range(p)):
                weight = downs[j + 1] if weight is None else weight * downs[j + 1]
                g[j] = g[j] + row(weight) * block(out, p - 1 - j)
        flip_row = row_of(order_ref[first : first + part, :]) > 0
        planes = out_ref.at[half].reshape(NP * CY * part, LANES)
        for y in range(CY):
            plane = jnp.where(flip_row, g[CY - 1 - y], g[y])
            for x, piece in enumerate(columns(plane)):
                planes[pl.ds(CY * x + y, NP, stride=CY * part), :] = piece
        target = out_hbm.at[:, CY * first : CY * (first + part), :]
        copies.append(pltpu.make_async_copy(out_ref.at[half], target, sems.at[half]))
        copies[-1].start()
    for copy in copies:
        copy.wait()


def in_hbm(a):
    return pltpu.with_memory_space_constraint(a, pltpu.HBM)


def shape(*dims, dtype=F32):
    return jax.ShapeDtypeStruct(dims, dtype)


def call(kernel, out_shape, n_in, scratch=(), scalars=0, space=pltpu.VMEM, out_space=pltpu.VMEM):
    whole = pl.BlockSpec(memory_space=out_space)
    specs = [pl.BlockSpec(memory_space=pltpu.SMEM)] * scalars
    specs += [pl.BlockSpec(memory_space=space)] * n_in
    outs = jax.tree.map(lambda _: whole, out_shape)
    return pl.pallas_call(
        kernel,
        out_shape=out_shape,
        in_specs=specs,
        out_specs=outs,
        scratch_shapes=list(scratch),
        compiler_params=pltpu.CompilerParams(vmem_limit_bytes=VMEM_LIMIT),
    )


def prepared_shapes(cells, extra, powers):
    return (
        shape((cells + extra) * NP, 4 * NP, dtype=BF16),
        shape((cells + extra) * NP, 4 * NP, dtype=BF16),
        shape(powers * NP, 4 * NP, dtype=BF16),
        shape(powers * NP, 4 * NP, dtype=BF16),
        shape(8, LANES),
    )


def per_device(
    rhs,
    coef_x,
    coef_y,
    out_coupling_x,
    in_coupling_x,
    inverse_x,
    boundary_inverse,
    out_coupling_y,
    in_coupling_y,
    inverse_y,
    bc_flags,
    line_order,
):
    rank = lax.axis_index("gx").astype(jnp.int32).reshape(1)
    mats = (
        out_coupling_x,
        inverse_x,
        in_coupling_x,
        boundary_inverse,
        out_coupling_y,
        inverse_y,
        in_coupling_y,
    )
    rhs = rhs.reshape(NP, CX * CY, LANES)
    coef_x = coef_x.reshape(3, CX * CY, LANES)
    coef_y = coef_y.reshape(3, CX * CY, LANES)

    sent, local, tiles, raw_y, flags, coef_y, order = call(
        x_local_kernel,
        (
            shape(SX, NP + 8, LANES),
            shape(CX, NP, CY * LANES),
            shape(6 * NP, 4 * NP),
            shape(3, NP, NP),
            shape(CY, LANES, dtype=jnp.int32),
            shape(3, CX * CY, LANES),
            shape(CX, LANES, dtype=jnp.int32),
        ),
        12,
        [
            pltpu.VMEM((PIECES, NP, 8, LANES), F32),
            pltpu.VMEM((3, CX * CY, LANES), F32),
            pltpu.VMEM((3, NP, NP), F32),
            pltpu.VMEM((3, NP, NP), F32),
            pltpu.SemaphoreType.DMA((11 + PIECES,)),
        ],
        1,
        pltpu.HBM,
    )(rank, *[in_hbm(a) for a in (rhs, coef_x, bc_flags) + mats + (coef_y, line_order)])
    got = lax.all_to_all(sent, "gx", 0, 0, tiled=True)
    prep_shapes = (shape(6 * NP, 4 * NP, dtype=BF16), shape(9 * NP, 4 * NP, dtype=BF16))
    prep = call(
        prepare_kernel, prep_shapes + prepared_shapes(CX, 3, 7) + prepared_shapes(CY, 0, 10), 2
    )(tiles, raw_y)
    parts_x, parts_y = prep[:2]
    gain_x, from_x, up_x, down_x, norm_x = prep[2:7]
    gain_y, from_y, up_y, down_y, norm_y = prep[7:]
    back = call(x_owner_kernel, shape(SX, NP, LANES), 5)(got, gain_x, up_x, down_x, norm_x)
    terms = lax.all_to_all(back, "gx", 0, 0, tiled=True)
    local, sent = call(
        middle_kernel,
        (shape(CY, NP, CX * LANES), shape(SY * ROWS, LANES)),
        9,
        [pltpu.VMEM((CY, NP, CX * LANES), F32)],
        1,
    )(rank, local, coef_x, flags, parts_x, parts_y, from_x, terms, coef_y, order)
    got = lax.all_to_all(sent.reshape(SY, ROWS // 2, 2, LANES), "gy", 0, 0, tiled=True)
    back = call(
        y_owner_kernel, shape(SY, 32, LANES), 5, [pltpu.VMEM((SY, 32, LANES), F32)]
    )(got.reshape(SY * ROWS, LANES), gain_y, up_y, down_y, norm_y)
    terms = lax.all_to_all(back, "gy", 0, 0, tiled=True)
    out = call(
        y_final_kernel,
        shape(NP, CX * CY, LANES),
        6,
        [
            pltpu.VMEM((HALVES, NP, CX * CY // HALVES, LANES), F32),
            pltpu.SemaphoreType.DMA((HALVES,)),
        ],
        out_space=pltpu.HBM,
    )(local, coef_y, order, parts_y, from_y, terms)
    return out.reshape(NP, CX, CY, LANES)


def solution(mesh):
    grid = P(None, "gx", "gy", None)
    in_specs = (grid, grid, grid) + (P(),) * 7 + (P("gy", None), P("gx", None))
    return jax.shard_map(
        per_device, mesh=mesh, in_specs=in_specs, out_specs=grid, check_vma=False
    )
```

```python
import jax
import jax.numpy as jnp
from jax import lax
from jax.experimental import pallas as pl
from jax.experimental.pallas import tpu as pltpu
from jax.sharding import PartitionSpec as P

NP = 64
LANES = 128
CX = 8
PIECES = 4
HALVES = 2
CY = 4
SX = 8
SY = 32
ROWS = 34
F32 = jnp.float32
BF16 = jnp.bfloat16
VMEM_LIMIT = 48 * 1024 * 1024


def rounded(v):
    return v.astype(BF16).astype(F32)


def split_matrix(m):
    high = rounded(m)
    rest = m - high
    mid = rounded(rest)
    low = rest - mid
    part = lax.broadcasted_iota(jnp.int32, m.shape, 1) // NP
    return jnp.where(part == 1, mid, jnp.where(part == 3, low, high)).astype(BF16)


def split_vectors(v):
    high = v.astype(BF16)
    low = (v - high.astype(F32)).astype(BF16)
    return jnp.concatenate([high, high, low, high], axis=0)


def product(parts, vectors):
    return jnp.dot(parts, vectors, preferred_element_type=F32)


def apply(parts, v):
    return product(parts, split_vectors(v))


def lane_iota(shape):
    return lax.broadcasted_iota(jnp.int32, shape, len(shape) - 1)


def roll(v, shift):
    shift = shift % LANES
    return v if shift == 0 else pltpu.roll(v, shift, 1)


def row_of(block):
    return jnp.concatenate([block[r : r + 1] for r in range(block.shape[0])], axis=1)


def columns(v):
    return [v[:, LANES * j : LANES * (j + 1)] for j in range(v.shape[1] // LANES)]


def regroup(blocks, width):
    n = LANES // width
    rolled = [[roll(b, width * k) for k in range(n)] for b in blocks]
    group = lane_iota(blocks[0].shape) // width
    outs = []
    for a in range(n):
        acc = rolled[0][(0 - a) % n]
        for q in range(1, n):
            acc = jnp.where(group == q, rolled[q][(q - a) % n], acc)
        outs.append(acc)
    return outs


def replicate(block, width):
    return regroup([block] * (LANES // width), width)


def shifted(v, t, width, ncol, reverse):
    cols = columns(v)
    group = lane_iota(cols[0].shape) // width
    n = LANES // width
    out = []
    for j in range(ncol):
        k = j + t if reverse else j - t
        carry = abs(k // ncol)
        src = cols[k % ncol]
        if carry:
            if reverse:
                src = jnp.where(group < n - carry, roll(src, -width * carry), 0.0)
            else:
                src = jnp.where(group >= carry, roll(src, width * carry), 0.0)
        out.append(src)
    return jnp.concatenate(out, axis=1)


def block(stack, k):
    return stack[NP * k : NP * (k + 1)]


def scan_segments(v, rate, powers, counts, width, ncol, reverse):
    stride, row = 1, 0
    for count in counts:
        out = apply(powers[NP * row : NP * (row + count), :], v)
        weight = rate
        for t in range(1, count + 1):
            v = v + weight * shifted(block(out, t - 1), stride * t, width, ncol, reverse)
            weight = rate * shifted(weight, stride, width, ncol, reverse)
        rate = weight
        row += count
        stride *= count + 1
    return v


def tiled(m):
    pair = jnp.concatenate([m, m], axis=0).T
    return jnp.concatenate([pair, pair], axis=1)


def multiply(a, b):
    parts = split_matrix(a)
    high = b.astype(BF16)
    rest = b - high.astype(F32)
    mid = rest.astype(BF16)
    low = (rest - mid.astype(F32)).astype(BF16)
    none = jnp.zeros_like(low)
    return product(parts, jnp.concatenate([high, high, mid, high], axis=0)) + product(
        parts, jnp.concatenate([low, mid, none, none], axis=0)
    )


def powers_of(m, count):
    stack = m
    while stack.shape[0] < count * NP:
        done = stack.shape[0] // NP
        more = min(done, count - done)
        stack = jnp.concatenate([stack, multiply(stack[: NP * more], block(stack, done - 1))], axis=0)
    return stack


def prepare(cells, far, up, down, scale, bounds, gain_ref, from_ref, up_ref, down_ref, done):
    halves = cells.bit_length() - 1
    ups = [up]
    for _ in range(halves):
        ups.append(multiply(ups[-1], ups[-1]))
    scaled = scale
    for k in range(halves):
        scaled = jnp.concatenate([scaled, apply(split_matrix(scaled), ups[k])], axis=0)
    from_ref[0 : cells * NP, :] = split_matrix(scaled)
    if bounds is not None:
        for k in range(halves):
            bounds = apply(split_matrix(bounds), ups[k])
        from_ref[cells * NP :, :] = split_matrix(bounds)
    done(from_ref)
    downs = powers_of(down, cells)
    stack = split_matrix(downs)
    for j in range(cells):
        gain = apply(block(stack, j), block(scaled, j))
        gain_ref[NP * j : NP * (j + 1), :] = split_matrix(gain)
    if bounds is not None:
        for kind in range(3):
            gain = apply(block(stack, cells - 1), block(bounds, kind))
            gain_ref[NP * (cells + kind) : NP * (cells + kind + 1), :] = split_matrix(gain)
    done(gain_ref)
    tops = ((ups[halves], up_ref), (block(downs, cells - 1), down_ref))
    for power, ref in tops:
        norm = jnp.max(jnp.sum(jnp.abs(power[:, :NP]), axis=1, keepdims=True), axis=0, keepdims=True)
        norm = jnp.maximum(norm, 1e-30)
        count = ref.shape[0] // NP
        ref[count * NP :, :] = split_matrix(jnp.broadcast_to(norm, (16, 4 * NP)))
        near = powers_of(power / norm, 7)
        ref[0 : 7 * NP, :] = split_matrix(near)
        if far:
            power8 = multiply(block(near, 3), block(near, 3))
            power16 = multiply(power8, power8)
            power24 = multiply(power16, power8)
            ref[7 * NP : 10 * NP, :] = split_matrix(
                jnp.concatenate([power8, power16, power24], axis=0)
            )
        done(ref)
    return ups, scaled, stack


def norm_of(ref):
    parts = ref[ref.shape[0] - 16 :, :].astype(F32)[0:1]
    return parts[:, 0:1] + parts[:, NP : NP + 1] + parts[:, 3 * NP : 3 * NP + 1]


def prepare_kernel(
    mats_ref,
    raw_ref,
    gain_ref,
    up_ref,
    down_ref,
    from_hbm,
    parts_hbm,
    parts_y_hbm,
    gain_y_hbm,
    from_y_hbm,
    up_y_hbm,
    down_y_hbm,
    from_ref,
    parts_ref,
    parts_y_ref,
    gain_y_ref,
    from_y_ref,
    up_y_ref,
    down_y_ref,
    sems,
):
    targets = (
        (from_ref, from_hbm),
        (parts_ref, parts_hbm),
        (parts_y_ref, parts_y_hbm),
        (gain_y_ref, gain_y_hbm),
        (from_y_ref, from_y_hbm),
        (up_y_ref, up_y_hbm),
        (down_y_ref, down_y_hbm),
    )
    sends = []

    def done(ref):
        for k, (source, target) in enumerate(targets):
            if source is ref:
                sends.append(pltpu.make_async_copy(source, target, sems.at[k]))
                sends[-1].start()

    ux, wx, b0, b1, b2, dx = [mats_ref[NP * k : NP * (k + 1), :] for k in range(6)]
    bounds = jnp.concatenate([b0, b1, b2], axis=0)
    _, _, stack = prepare(
        CX, False, ux, dx, wx, bounds, gain_ref, from_ref, up_ref, down_ref, done
    )
    parts_ref[...] = stack[: 6 * NP]
    done(parts_ref)
    uy, wy, dy = [tiled(raw_ref[k]) for k in range(3)]
    ups, scaled, stack = prepare(
        CY, True, uy, dy, wy, None, gain_y_ref, from_y_ref, up_y_ref, down_y_ref, done
    )
    extra = [uy, scaled[: 3 * NP], multiply(ups[1], uy)]
    parts_y_ref[0 : 5 * NP, :] = split_matrix(jnp.concatenate(extra, axis=0))
    parts_y_ref[5 * NP :, :] = stack
    done(parts_y_ref)
    for copy in sends:
        copy.wait()


def x_rates(coef_ref, which, i):
    return coef_ref[which, CY * i : CY * (i + 1), :]


def x_local_kernel(
    rank_ref,
    rhs_hbm,
    coef_hbm,
    flags_hbm,
    ux,
    wx,
    dx,
    b,
    uy,
    wy,
    dy,
    order_hbm,
    out_ref,
    scaled_ref,
    mats_ref,
    raw_y_ref,
    rhs_ref,
    coef_ref,
    flags_ref,
    order_ref,
    raw_ref,
    bounds_ref,
    sems,
):
    rank = rank_ref[0]
    sources = [ux, wx, b, dx, coef_hbm, flags_hbm]
    targets = [raw_ref.at[0], raw_ref.at[1], bounds_ref, raw_ref.at[2], coef_ref, flags_ref]
    for k in range(PIECES):
        sources.append(rhs_hbm.at[:, 8 * k : 8 * (k + 1), :])
        targets.append(rhs_ref.at[k])
    sources += [uy, wy, dy, order_hbm]
    targets += [raw_y_ref.at[0], raw_y_ref.at[1], raw_y_ref.at[2], order_ref]
    copies = []
    for k, (source, target) in enumerate(zip(sources, targets)):
        copies.append(pltpu.make_async_copy(source, target, sems.at[k]))
        copies[-1].start()
    for copy in copies[:6]:
        copy.wait()

    def place(row, m):
        value = tiled(m)
        mats_ref[NP * row : NP * (row + 1), :] = value
        return split_matrix(value)

    up, scale = place(0, raw_ref[0]), place(1, raw_ref[1])
    bounds = [place(2 + k, bounds_ref[k]) for k in range(3)]
    down = place(5, raw_ref[2])
    up_scale = jnp.concatenate([up, scale], axis=0)
    end_stack = jnp.concatenate([up, scale] + bounds, axis=0)
    u, w = mats_ref[0:NP, :], mats_ref[NP : 2 * NP, :]
    d = mats_ref[5 * NP :, :]
    u2 = multiply(u, u)
    wu = split_matrix(multiply(w, u))
    u4 = split_matrix(multiply(u2, u2))
    u2 = split_matrix(u2)
    d2 = multiply(d, d)
    down24 = split_matrix(jnp.concatenate([d2, multiply(d2, d2)], axis=0))
    planes = rhs_ref.reshape(PIECES * NP * 8, LANES)

    ups = [x_rates(coef_ref, 1, i) for i in range(CX)]
    downs = [x_rates(coef_ref, 0, i) for i in range(CX)]
    flags = row_of(flags_ref[...])

    def given(i):
        start = (CY * i // 8) * NP * 8 + CY * i % 8
        return jnp.concatenate(
            [planes[pl.ds(start + y, NP, stride=8), :] for y in range(CY)], axis=1
        )

    def at_end(i, out):
        chosen = jnp.where(
            flags == 0, block(out, 2), jnp.where(flags == 1, block(out, 3), block(out, 4))
        )
        return jnp.where(rank == (0 if i == 0 else SX - 1), chosen, block(out, 1))

    def scaled(i, value):
        value = value * row_of(1.0 / x_rates(coef_ref, 2, i))
        scaled_ref[i] = value
        return value

    s, v, part = [None] * CX, [], []
    for k in range(PIECES):
        copies[6 + k].wait()
        out = apply(end_stack if k == 0 else up_scale, given(2 * k))
        v.append(given(2 * k + 1) + row_of(ups[2 * k]) * block(out, 0))
        part.append(at_end(0, out) if k == 0 else block(out, 1))
    two = [None] + [ups[2 * k] * ups[2 * k - 1] for k in range(1, 4)]
    s[0] = scaled(0, part[0])
    out = apply(jnp.concatenate([scale, wu, u2], axis=0), v[0])
    s[1] = scaled(1, block(out, 0))
    s[2] = scaled(2, part[1] + row_of(ups[1]) * block(out, 1))
    f3 = v[1] + row_of(two[1]) * block(out, 2)
    f7 = v[3] + row_of(two[3]) * apply(u2, v[2])
    out = apply(jnp.concatenate([scale, wu, u2, u4], axis=0), f3)
    s[3] = scaled(3, block(out, 0))
    s[4] = scaled(4, part[2] + row_of(ups[3]) * block(out, 1))
    f5 = v[2] + row_of(two[2]) * block(out, 2)
    f7 = f7 + row_of(two[3] * two[2]) * block(out, 3)
    out = apply(jnp.concatenate([scale, wu], axis=0), f5)
    s[5] = scaled(5, block(out, 0))
    s[6] = scaled(6, part[3] + row_of(ups[5]) * block(out, 1))
    out = apply(end_stack, f7)
    f = row_of(ups[7]) * block(out, 0)
    s[7] = scaled(7, at_end(7, out))
    pair = [s[2 * k] + row_of(downs[2 * k + 1]) * apply(down, s[2 * k + 1]) for k in range(4)]
    two = [downs[2 * k + 1] * downs[2 * k + 2] for k in range(3)]
    first = pair[0] + row_of(two[0]) * apply(down24[:NP], pair[1])
    second = pair[2] + row_of(two[2]) * apply(down24[:NP], pair[3])
    g = first + row_of(two[0] * two[1]) * apply(down24[NP:], second)
    g = row_of(downs[0]) * apply(down, g)
    for copy in copies[6 + PIECES :]:
        copy.wait()
    scaled_ref[CX, 0:CY, 0:LANES] = flags_ref[...].astype(F32)
    scaled_ref[CX, 8 : 8 + CX, 0:LANES] = order_ref[...].astype(F32)
    for y, (fy, gy) in enumerate(zip(columns(f), columns(g))):
        even, odd = regroup([fy, gy], NP)
        out_ref[2 * y, 0:NP, :] = even
        out_ref[2 * y + 1, 0:NP, :] = odd
    down_rate = x_rates(coef_ref, 0, 0)
    up_rate = jnp.ones_like(down_rate)
    gains = []
    for i in range(CX):
        gains.append(down_rate * up_rate / x_rates(coef_ref, 2, i))
        up_rate = up_rate * x_rates(coef_ref, 1, i)
        if i + 1 < CX:
            down_rate = down_rate * x_rates(coef_ref, 0, i + 1)
    last = gains.pop()
    is_last = rank == SX - 1
    flags = flags_ref[...]
    gains.append(jnp.where(is_last, 0.0, last))
    for kind in range(3):
        gains.append(jnp.where(jnp.logical_and(is_last, flags == kind), last, 0.0))
    values = [up_rate, down_rate] + gains + [jnp.zeros_like(last)] * 3
    for r in range(8):
        even, odd = regroup([values[2 * r], values[2 * r + 1]], NP)
        for y in range(CY):
            out_ref[2 * y, NP + r : NP + r + 1, :] = even[y : y + 1]
            out_ref[2 * y + 1, NP + r : NP + r + 1, :] = odd[y : y + 1]


def x_owner_kernel(in_ref, gain_ref, up_ref, down_ref, out_ref):
    half = SX // 2
    fs, gs, sa, sb = [], [], [], []
    for j in range(half):
        f, g = regroup([in_ref[j], in_ref[half + j]], NP)
        fs.append(f[:NP])
        gs.append(g[:NP])
        sa.append(f[NP:])
        sb.append(g[NP:])
    f = jnp.concatenate(fs, axis=1)
    g = jnp.concatenate(gs, axis=1)
    even = jnp.concatenate(sa, axis=1)
    odd = jnp.concatenate(sb, axis=1)
    scalar = [(even if k % 2 == 0 else odd)[k // 2 : k // 2 + 1] for k in range(13)]
    width, ncol = NP, half
    up_rate = scalar[0] * norm_of(up_ref)
    down_rate = scalar[1] * norm_of(down_ref)
    h = scan_segments(
        shifted(f, 1, width, ncol, False),
        shifted(up_rate, 1, width, ncol, False),
        up_ref,
        (7,),
        width,
        ncol,
        False,
    )
    vectors = split_vectors(h)
    through = product(gain_ref[0 : CX * NP], vectors)
    for i in range(CX):
        g = g + scalar[2 + i] * through[NP * i : NP * (i + 1)]
    ends = product(gain_ref[CX * NP :], vectors[:, LANES * (half - 1) :])
    extra = 0.0
    for kind in range(3):
        extra = extra + (
            scalar[10 + kind][:, LANES * (half - 1) :] * ends[NP * kind : NP * (kind + 1)]
        )
    g = jnp.concatenate([g[:, : LANES * (half - 1)], g[:, LANES * (half - 1) :] + extra], axis=1)
    e = scan_segments(
        shifted(g, 1, width, ncol, True),
        shifted(down_rate, 1, width, ncol, True),
        down_ref,
        (7,),
        width,
        ncol,
        True,
    )
    for j, (hj, ej) in enumerate(zip(columns(h), columns(e))):
        first, second = regroup([hj, ej], NP)
        out_ref[j] = first
        out_ref[half + j] = second


def y_rates(coef_ref, which, flip, p):
    here = coef_ref[which, pl.ds(p, CX, stride=CY), :]
    there = coef_ref[which, pl.ds(CY - 1 - p, CX, stride=CY), :]
    return jnp.where(flip, there, here)


def middle_kernel(
    rank_ref,
    local_ref,
    coef_ref,
    parts_ref,
    parts_y_ref,
    from_ref,
    in_ref,
    coef_y_ref,
    scaled_ref,
    out_ref,
    adj_ref,
):
    rank = rank_ref[0]
    parts = parts_ref[...]
    parts_y = parts_y_ref[...]
    down = parts
    u_y, w_y, wu_y, wu2_y, u3_y = [block(parts_y, k) for k in range(5)]
    up_scale_y = parts_y[: 2 * NP]
    down_y = parts_y[5 * NP :]
    hs, es = [], []
    for y in range(CY):
        h, e = regroup([in_ref[2 * y], in_ref[2 * y + 1]], NP)
        hs.append(h)
        es.append(e)
    through = apply(from_ref[...], jnp.concatenate(hs, axis=1))
    up_rates = [jnp.ones((CY, LANES), F32)]
    for i in range(CX - 1):
        up_rates.append(up_rates[-1] * x_rates(coef_ref, 1, i))
    downs = [x_rates(coef_ref, 0, i) for i in range(CX)]

    def scaled(i):
        term = through[NP * i : NP * (i + 1)]
        if i == CX - 1:
            ends = through[NP * CX :]
            chosen = jnp.where(
                flags == 0, ends[:NP], jnp.where(flags == 1, ends[NP : 2 * NP], ends[2 * NP :])
            )
            term = jnp.where(rank == SX - 1, chosen, term)
        return local_ref[i] + row_of(up_rates[i] / x_rates(coef_ref, 2, i)) * term

    def keep(i, g):
        for y in range(CY):
            adj_ref[y, :, LANES * i : LANES * (i + 1)] = g[:, LANES * y : LANES * (y + 1)]

    s = [scaled(i) for i in range(CX - 1)]
    pair = [
        s[2 * k] + row_of(downs[2 * k + 1]) * apply(block(down, 0), s[2 * k + 1]) for k in range(3)
    ]
    flags = row_of(local_ref[CX, 0:CY, 0:LANES])
    s.append(scaled(CX - 1) + jnp.concatenate(es, axis=1))
    keep(7, s[7])
    pair.append(s[6] + row_of(downs[7]) * apply(block(down, 0), s[7]))
    two = [downs[2 * k + 1] * downs[2 * k + 2] for k in range(3)]
    g = [pair[0], s[1], pair[1], s[3], pair[2], s[5]]
    for k in (3, 2, 1):
        out = apply(down[: 2 * k * NP], pair[k])
        weight = None
        for j in reversed(range(k)):
            odd = downs[2 * j + 2] if weight is None else weight * downs[2 * j + 2]
            weight = two[j] if weight is None else weight * two[j]
            power = 2 * (k - j)
            g[2 * j + 1] = g[2 * j + 1] + row_of(odd) * block(out, power - 2)
            g[2 * j] = g[2 * j] + row_of(weight) * block(out, power - 1)
    for i in range(6):
        keep(i, g[i])
    keep(6, pair[3])

    order = local_ref[CX, 8 : 8 + CX, 0:LANES]
    flip = order > 0
    flip_row = row_of(order) > 0

    def oriented(which, p):
        return y_rates(coef_y_ref, which, flip, p)

    a = [jnp.where(flip_row, adj_ref[CY - 1 - p], adj_ref[p]) for p in range(CY)]
    ups = [oriented(1, p) for p in range(CY)]
    downs = [oriented(0, p) for p in range(CY)]
    inverse = [row_of(1.0 / oriented(2, p)) for p in range(CY)]
    out = apply(up_scale_y, a[0])
    f1 = a[1] + row_of(ups[0]) * block(out, 0)
    s = [block(out, 1)]
    out2 = apply(up_scale_y, a[2])
    v3 = a[3] + row_of(ups[2]) * block(out2, 0)
    out1 = apply(jnp.concatenate([w_y, wu_y, wu2_y, u3_y], axis=0), f1)
    out3 = apply(up_scale_y, v3)
    two = ups[1] * ups[2]
    s.append(block(out1, 0))
    s.append(block(out2, 1) + row_of(ups[1]) * block(out1, 1))
    s.append(block(out3, 1) + row_of(two) * block(out1, 2))
    f = row_of(ups[3]) * block(out3, 0) + row_of(ups[3] * two) * block(out1, 3)
    g, weight = 0.0, downs[0]
    for p in range(CY):
        value = s[p] * inverse[p]
        scaled_ref[p] = value
        g = g + row_of(weight) * apply(block(down_y, p), value)
        if p + 1 < CY:
            weight = weight * downs[p + 1]

    down_rate = oriented(0, 0)
    up_rate = jnp.ones_like(down_rate)
    gains = []
    for p in range(CY):
        gains.append(down_rate * up_rate / oriented(2, p))
        up_rate = up_rate * oriented(1, p)
        if p + 1 < CY:
            down_rate = down_rate * oriented(0, p + 1)
    first = regroup([up_rate, down_rate, gains[0], gains[1]], 32)
    second = regroup([gains[2], gains[3], flip.astype(F32), jnp.zeros_like(up_rate)], 32)
    for x, (fx, gx) in enumerate(zip(columns(f), columns(g))):
        chunks = regroup([fx[:32], fx[32:], gx[:32], gx[32:]], 32)
        for a in range(4):
            row = ROWS * (4 * x + a)
            out_ref[row : row + 32, :] = chunks[a]
            out_ref[row + 32 : row + 33, :] = first[a][x : x + 1]
            out_ref[row + 33 : row + 34, :] = second[a][x : x + 1]


def y_owner_kernel(in_ref, gain_ref, up_ref, down_ref, out_ref, res_ref):
    width, ncol = 32, 8
    flip = replicate(in_ref[33:34, :], width)[2] > 0.5

    def oriented(s):
        t = SY - 1 - s
        return jnp.where(flip, in_ref[ROWS * t : ROWS * (t + 1), :], in_ref[ROWS * s : ROWS * (s + 1), :])

    fs, gs, ss = [], [], []
    for j in range(ncol):
        outs = regroup([oriented(ncol * a + j) for a in range(4)], width)
        fs.append(jnp.concatenate([outs[0][:32], outs[1][:32]], axis=0))
        gs.append(jnp.concatenate([outs[2][:32], outs[3][:32]], axis=0))
        ss.append([o[32:33] for o in outs] + [o[33:34] for o in outs[:2]])
    f = jnp.concatenate(fs, axis=1)
    g = jnp.concatenate(gs, axis=1)
    scalars = [jnp.concatenate([s[k] for s in ss], axis=1) for k in range(6)]
    up_rate = scalars[0] * norm_of(up_ref)
    down_rate = scalars[1] * norm_of(down_ref)
    h = scan_segments(
        shifted(f, 1, width, ncol, False),
        shifted(up_rate, 1, width, ncol, False),
        up_ref,
        (7, 3),
        width,
        ncol,
        False,
    )
    through = apply(gain_ref[...], h)
    for p in range(CY):
        g = g + scalars[2 + p] * through[NP * p : NP * (p + 1)]
    e = scan_segments(
        shifted(g, 1, width, ncol, True),
        shifted(down_rate, 1, width, ncol, True),
        down_ref,
        (7, 3),
        width,
        ncol,
        True,
    )
    for j, (hj, ej) in enumerate(zip(columns(h), columns(e))):
        outs = regroup([hj[:32], hj[32:], ej[:32], ej[32:]], width)
        for a in range(4):
            res_ref[ncol * a + j] = outs[a]
    for s in range(SY):
        out_ref[s] = jnp.where(flip, res_ref[SY - 1 - s], res_ref[s])


def y_final_kernel(
    local_ref, coef_y_ref, order_ref, parts_ref, from_ref, in_ref, out_hbm, out_ref, sems
):
    down = parts_ref[5 * NP : 8 * NP, :]
    flip = order_ref[...] > 0

    def oriented(which, p):
        return y_rates(coef_y_ref, which, flip, p)

    up_rates = [jnp.ones((CX, LANES), F32)]
    for p in range(CY - 1):
        up_rates.append(up_rates[-1] * oriented(1, p))
    term_rates = [up_rates[p] / oriented(2, p) for p in range(CY)]
    downs = [oriented(0, p) for p in range(CY)]
    part = CX // HALVES
    copies = []
    for half in range(HALVES):
        first = part * half
        lanes = slice(LANES * first, LANES * (first + part))

        def row(rate):
            return row_of(rate[first : first + part])

        hs, es = [], []
        for x in range(first, first + part):
            outs = regroup([in_ref[4 * x + a] for a in range(4)], 32)
            hs.append(jnp.concatenate(outs[:2], axis=0))
            es.append(jnp.concatenate(outs[2:], axis=0))
        through = apply(from_ref[...], jnp.concatenate(hs, axis=1))
        s = [local_ref[p, :, lanes] + row(term_rates[p]) * block(through, p) for p in range(CY)]
        s[3] = s[3] + jnp.concatenate(es, axis=1)
        g = list(s)
        for p in (3, 2, 1):
            out = apply(down[: NP * p], s[p])
            weight = None
            for j in reversed(range(p)):
                weight = downs[j + 1] if weight is None else weight * downs[j + 1]
                g[j] = g[j] + row(weight) * block(out, p - 1 - j)
        flip_row = row_of(order_ref[first : first + part, :]) > 0
        planes = out_ref.at[half].reshape(NP * CY * part, LANES)
        for y in range(CY):
            plane = jnp.where(flip_row, g[CY - 1 - y], g[y])
            for x, piece in enumerate(columns(plane)):
                planes[pl.ds(CY * x + y, NP, stride=CY * part), :] = piece
        target = out_hbm.at[:, CY * first : CY * (first + part), :]
        copies.append(pltpu.make_async_copy(out_ref.at[half], target, sems.at[half]))
        copies[-1].start()
    for copy in copies:
        copy.wait()


def in_hbm(a):
    return pltpu.with_memory_space_constraint(a, pltpu.HBM)


def call(kernel, outs, spaces, scratch=(), scalars=0):
    shapes = tuple(space(dims, dtype) for space, dims, dtype in outs)
    specs = [pl.BlockSpec(memory_space=pltpu.SMEM)] * scalars
    specs += [pl.BlockSpec(memory_space=s) for s in spaces]
    return pl.pallas_call(
        kernel,
        out_shape=shapes,
        in_specs=specs,
        out_specs=tuple(pl.BlockSpec(memory_space=out[0]) for out in outs),
        scratch_shapes=list(scratch),
        compiler_params=pltpu.CompilerParams(vmem_limit_bytes=VMEM_LIMIT),
    )


def per_device(
    rhs,
    coef_x,
    coef_y,
    out_coupling_x,
    in_coupling_x,
    inverse_x,
    boundary_inverse,
    out_coupling_y,
    in_coupling_y,
    inverse_y,
    bc_flags,
    line_order,
):
    vmem, hbm = pltpu.VMEM, pltpu.HBM
    rank = lax.axis_index("gx").astype(jnp.int32).reshape(1)
    mats_x = (out_coupling_x, inverse_x, in_coupling_x, boundary_inverse)
    mats_y = (out_coupling_y, inverse_y, in_coupling_y)
    rhs = rhs.reshape(NP, CX * CY, LANES)
    coef_x = coef_x.reshape(3, CX * CY, LANES)
    coef_y = coef_y.reshape(3, CX * CY, LANES)

    sent, local, tiles, raw_y = call(
        x_local_kernel,
        (
            (vmem, (SX, NP + 8, LANES), F32),
            (vmem, (CX + 1, NP, CY * LANES), F32),
            (vmem, (6 * NP, 4 * NP), F32),
            (vmem, (3, NP, NP), F32),
        ),
        (hbm,) * 11,
        [
            vmem((PIECES, NP, 8, LANES), F32),
            vmem((3, CX * CY, LANES), F32),
            vmem((CY, LANES), jnp.int32),
            vmem((CX, LANES), jnp.int32),
            vmem((3, NP, NP), F32),
            vmem((3, NP, NP), F32),
            pltpu.SemaphoreType.DMA((10 + PIECES,)),
        ],
        1,
    )(rank, *[in_hbm(a) for a in (rhs, coef_x, bc_flags) + mats_x + mats_y + (line_order,)])
    got = lax.all_to_all(sent, "gx", 0, 0, tiled=True)
    later = [
        (rows, 4 * NP)
        for rows in (11 * NP, 6 * NP, 9 * NP, 4 * NP, 4 * NP, 10 * NP + 16, 10 * NP + 16)
    ]
    gain_x, up_x, down_x, from_x, parts_x, parts_y, gain_y, from_y, up_y, down_y = call(
        prepare_kernel,
        (
            (vmem, (11 * NP, 4 * NP), BF16),
            (vmem, (7 * NP + 16, 4 * NP), BF16),
            (vmem, (7 * NP + 16, 4 * NP), BF16),
        )
        + tuple((hbm, dims, BF16) for dims in later),
        (vmem, vmem),
        [vmem(dims, BF16) for dims in later] + [pltpu.SemaphoreType.DMA((7,))],
    )(tiles, raw_y)
    (back,) = call(x_owner_kernel, ((vmem, (SX, NP, LANES), F32),), (vmem,) * 4)(
        got, gain_x, up_x, down_x
    )
    terms = lax.all_to_all(back, "gx", 0, 0, tiled=True)
    local, sent = call(
        middle_kernel,
        ((vmem, (CY, NP, CX * LANES), F32), (vmem, (SY * ROWS, LANES), F32)),
        (vmem,) * 7,
        [vmem((CY, NP, CX * LANES), F32)],
        1,
    )(rank, local, coef_x, parts_x, parts_y, from_x, terms, coef_y)
    got = lax.all_to_all(sent.reshape(SY, ROWS // 2, 2, LANES), "gy", 0, 0, tiled=True)
    (back,) = call(
        y_owner_kernel,
        ((vmem, (SY, 32, LANES), F32),),
        (vmem,) * 4,
        [vmem((SY, 32, LANES), F32)],
    )(got.reshape(SY * ROWS, LANES), gain_y, up_y, down_y)
    terms = lax.all_to_all(back, "gy", 0, 0, tiled=True)
    (out,) = call(
        y_final_kernel,
        ((hbm, (NP, CX * CY, LANES), F32),),
        (vmem,) * 6,
        [
            vmem((HALVES, NP, CX * CY // HALVES, LANES), F32),
            pltpu.SemaphoreType.DMA((HALVES,)),
        ],
    )(local, coef_y, line_order, parts_y, from_y, terms)
    return out.reshape(NP, CX, CY, LANES)


def solution(mesh):
    grid = P(None, "gx", "gy", None)
    in_specs = (grid, grid, grid) + (P(),) * 7 + (P("gy", None), P("gx", None))
    return jax.shard_map(
        per_device, mesh=mesh, in_specs=in_specs, out_specs=grid, check_vma=False
    )
```

```python
import jax
import jax.numpy as jnp
from jax import lax
from jax.experimental import pallas as pl
from jax.experimental.pallas import tpu as pltpu
from jax.sharding import PartitionSpec as P

NP = 64
LANES = 128
CX = 8
PIECES = 4
HALVES = 2
CY = 4
SX = 8
SY = 32
ROWS = 34
F32 = jnp.float32
BF16 = jnp.bfloat16
VMEM_LIMIT = 48 * 1024 * 1024


def rounded(v):
    return v.astype(BF16).astype(F32)


def split_matrix(m):
    high = rounded(m)
    rest = m - high
    mid = rounded(rest)
    low = rest - mid
    part = lax.broadcasted_iota(jnp.int32, m.shape, 1) // NP
    return jnp.where(part == 1, mid, jnp.where(part == 3, low, high)).astype(BF16)


def split_vectors(v):
    high = v.astype(BF16)
    low = (v - high.astype(F32)).astype(BF16)
    return jnp.concatenate([high, high, low, high], axis=0)


def product(parts, vectors):
    return jnp.dot(parts, vectors, preferred_element_type=F32)


def apply(parts, v):
    return product(parts, split_vectors(v))


def lane_iota(shape):
    return lax.broadcasted_iota(jnp.int32, shape, len(shape) - 1)


def roll(v, shift):
    shift = shift % LANES
    return v if shift == 0 else pltpu.roll(v, shift, 1)


def row_of(block):
    return jnp.concatenate([block[r : r + 1] for r in range(block.shape[0])], axis=1)


def columns(v):
    return [v[:, LANES * j : LANES * (j + 1)] for j in range(v.shape[1] // LANES)]


def regroup(blocks, width):
    n = LANES // width
    rolled = [[roll(b, width * k) for k in range(n)] for b in blocks]
    group = lane_iota(blocks[0].shape) // width
    outs = []
    for a in range(n):
        acc = rolled[0][(0 - a) % n]
        for q in range(1, n):
            acc = jnp.where(group == q, rolled[q][(q - a) % n], acc)
        outs.append(acc)
    return outs


def replicate(block, width):
    return regroup([block] * (LANES // width), width)


def shifted(v, t, width, ncol, reverse):
    cols = columns(v)
    group = lane_iota(cols[0].shape) // width
    n = LANES // width
    out = []
    for j in range(ncol):
        k = j + t if reverse else j - t
        carry = abs(k // ncol)
        src = cols[k % ncol]
        if carry:
            if reverse:
                src = jnp.where(group < n - carry, roll(src, -width * carry), 0.0)
            else:
                src = jnp.where(group >= carry, roll(src, width * carry), 0.0)
        out.append(src)
    return jnp.concatenate(out, axis=1)


def block(stack, k):
    return stack[NP * k : NP * (k + 1)]


def scan_segments(v, rate, powers, counts, width, ncol, reverse):
    stride, row = 1, 0
    for count in counts:
        out = apply(powers[NP * row : NP * (row + count), :], v)
        weight = rate
        for t in range(1, count + 1):
            v = v + weight * shifted(block(out, t - 1), stride * t, width, ncol, reverse)
            weight = rate * shifted(weight, stride, width, ncol, reverse)
        rate = weight
        row += count
        stride *= count + 1
    return v


def tiled(m):
    pair = jnp.concatenate([m, m], axis=0).T
    return jnp.concatenate([pair, pair], axis=1)


def multiply(a, b):
    parts = split_matrix(a)
    high = b.astype(BF16)
    rest = b - high.astype(F32)
    mid = rest.astype(BF16)
    low = (rest - mid.astype(F32)).astype(BF16)
    none = jnp.zeros_like(low)
    return product(parts, jnp.concatenate([high, high, mid, high], axis=0)) + product(
        parts, jnp.concatenate([low, mid, none, none], axis=0)
    )


def powers_of(m, count):
    stack = m
    while stack.shape[0] < count * NP:
        done = stack.shape[0] // NP
        more = min(done, count - done)
        stack = jnp.concatenate([stack, multiply(stack[: NP * more], block(stack, done - 1))], axis=0)
    return stack


def prepare(cells, far, up, down, scale, bounds, gain_ref, from_ref, up_ref, down_ref, done):
    halves = cells.bit_length() - 1
    ups = [up]
    for _ in range(halves):
        ups.append(multiply(ups[-1], ups[-1]))
    scaled = scale
    for k in range(halves):
        scaled = jnp.concatenate([scaled, apply(split_matrix(scaled), ups[k])], axis=0)
    from_ref[0 : cells * NP, :] = split_matrix(scaled)
    if bounds is not None:
        for k in range(halves):
            bounds = apply(split_matrix(bounds), ups[k])
        from_ref[cells * NP :, :] = split_matrix(bounds)
    done(from_ref)
    downs = powers_of(down, cells)
    stack = split_matrix(downs)
    for j in range(cells):
        gain = apply(block(stack, j), block(scaled, j))
        gain_ref[NP * j : NP * (j + 1), :] = split_matrix(gain)
    if bounds is not None:
        for kind in range(3):
            gain = apply(block(stack, cells - 1), block(bounds, kind))
            gain_ref[NP * (cells + kind) : NP * (cells + kind + 1), :] = split_matrix(gain)
    done(gain_ref)
    tops = ((ups[halves], up_ref), (block(downs, cells - 1), down_ref))
    for power, ref in tops:
        norm = jnp.max(jnp.sum(jnp.abs(power[:, :NP]), axis=1, keepdims=True), axis=0, keepdims=True)
        norm = jnp.maximum(norm, 1e-30)
        count = ref.shape[0] // NP
        ref[count * NP :, :] = split_matrix(jnp.broadcast_to(norm, (16, 4 * NP)))
        near = powers_of(power / norm, 7)
        ref[0 : 7 * NP, :] = split_matrix(near)
        if far:
            power8 = multiply(block(near, 3), block(near, 3))
            power16 = multiply(power8, power8)
            power24 = multiply(power16, power8)
            ref[7 * NP : 10 * NP, :] = split_matrix(
                jnp.concatenate([power8, power16, power24], axis=0)
            )
        done(ref)
    return ups, scaled, stack


def norm_of(ref):
    parts = ref[ref.shape[0] - 16 :, :].astype(F32)[0:1]
    return parts[:, 0:1] + parts[:, NP : NP + 1] + parts[:, 3 * NP : 3 * NP + 1]


def prepare_kernel(
    mats_ref,
    raw_ref,
    gain_ref,
    up_ref,
    down_ref,
    from_hbm,
    parts_hbm,
    parts_y_hbm,
    gain_y_hbm,
    from_y_hbm,
    up_y_hbm,
    down_y_hbm,
    from_ref,
    parts_ref,
    parts_y_ref,
    gain_y_ref,
    from_y_ref,
    up_y_ref,
    down_y_ref,
    sems,
):
    targets = (
        (from_ref, from_hbm),
        (parts_ref, parts_hbm),
        (parts_y_ref, parts_y_hbm),
        (gain_y_ref, gain_y_hbm),
        (from_y_ref, from_y_hbm),
        (up_y_ref, up_y_hbm),
        (down_y_ref, down_y_hbm),
    )
    sends = []

    def done(ref):
        for k, (source, target) in enumerate(targets):
            if source is ref:
                sends.append(pltpu.make_async_copy(source, target, sems.at[k]))
                sends[-1].start()

    ux, wx, b0, b1, b2, dx = [mats_ref[NP * k : NP * (k + 1), :] for k in range(6)]
    bounds = jnp.concatenate([b0, b1, b2], axis=0)
    _, _, stack = prepare(
        CX, False, ux, dx, wx, bounds, gain_ref, from_ref, up_ref, down_ref, done
    )
    parts_ref[...] = stack[: 6 * NP]
    done(parts_ref)
    uy, wy, dy = [tiled(raw_ref[k]) for k in range(3)]
    ups, scaled, stack = prepare(
        CY, True, uy, dy, wy, None, gain_y_ref, from_y_ref, up_y_ref, down_y_ref, done
    )
    extra = [uy, scaled[: 3 * NP], multiply(ups[1], uy)]
    parts_y_ref[0 : 5 * NP, :] = split_matrix(jnp.concatenate(extra, axis=0))
    parts_y_ref[5 * NP :, :] = stack
    done(parts_y_ref)
    for copy in sends:
        copy.wait()


def x_rates(coef_ref, which, i):
    return coef_ref[which, CY * i : CY * (i + 1), :]


def x_local_kernel(
    rank_ref,
    rhs_hbm,
    coef_hbm,
    flags_hbm,
    ux,
    wx,
    dx,
    b,
    uy,
    wy,
    dy,
    order_hbm,
    out_ref,
    scaled_ref,
    mats_ref,
    raw_y_ref,
    rhs_ref,
    coef_ref,
    flags_ref,
    order_ref,
    raw_ref,
    bounds_ref,
    sems,
):
    rank = rank_ref[0]
    sources = [ux, wx, b, dx, coef_hbm, flags_hbm]
    targets = [raw_ref.at[0], raw_ref.at[1], bounds_ref, raw_ref.at[2], coef_ref, flags_ref]
    for k in range(PIECES):
        sources.append(rhs_hbm.at[:, 8 * k : 8 * (k + 1), :])
        targets.append(rhs_ref.at[k])
    sources += [uy, wy, dy, order_hbm]
    targets += [raw_y_ref.at[0], raw_y_ref.at[1], raw_y_ref.at[2], order_ref]
    copies = []
    for k, (source, target) in enumerate(zip(sources, targets)):
        copies.append(pltpu.make_async_copy(source, target, sems.at[k]))
    for k in range(len(copies)):
        copies[k].start()
    for copy in copies[:6]:
        copy.wait()

    def place(row, m):
        value = tiled(m)
        mats_ref[NP * row : NP * (row + 1), :] = value
        return split_matrix(value)

    up, scale = place(0, raw_ref[0]), place(1, raw_ref[1])
    bounds = [place(2 + k, bounds_ref[k]) for k in range(3)]
    down = place(5, raw_ref[2])
    up_scale = jnp.concatenate([up, scale], axis=0)
    end_stack = jnp.concatenate([up, scale] + bounds, axis=0)
    u, w = mats_ref[0:NP, :], mats_ref[NP : 2 * NP, :]
    d = mats_ref[5 * NP :, :]
    u2 = multiply(u, u)
    wu = split_matrix(multiply(w, u))
    u4 = split_matrix(multiply(u2, u2))
    u2 = split_matrix(u2)
    d2 = multiply(d, d)
    down24 = split_matrix(jnp.concatenate([d2, multiply(d2, d2)], axis=0))
    for copy in copies[6:]:
        copy.wait()
    planes = rhs_ref.reshape(PIECES * NP * 8, LANES)

    ups = [x_rates(coef_ref, 1, i) for i in range(CX)]
    downs = [x_rates(coef_ref, 0, i) for i in range(CX)]
    flags = row_of(flags_ref[...])

    def given(i):
        start = (CY * i // 8) * NP * 8 + CY * i % 8
        return jnp.concatenate(
            [planes[pl.ds(start + y, NP, stride=8), :] for y in range(CY)], axis=1
        )

    def at_end(i, out):
        chosen = jnp.where(
            flags == 0, block(out, 2), jnp.where(flags == 1, block(out, 3), block(out, 4))
        )
        return jnp.where(rank == (0 if i == 0 else SX - 1), chosen, block(out, 1))

    def scaled(i, value):
        value = value * row_of(1.0 / x_rates(coef_ref, 2, i))
        scaled_ref[i] = value
        return value

    s, v, part = [None] * CX, [], []
    for k in range(PIECES):
        out = apply(end_stack if k == 0 else up_scale, given(2 * k))
        v.append(given(2 * k + 1) + row_of(ups[2 * k]) * block(out, 0))
        part.append(at_end(0, out) if k == 0 else block(out, 1))
    two = [None] + [ups[2 * k] * ups[2 * k - 1] for k in range(1, 4)]
    s[0] = scaled(0, part[0])
    out = apply(jnp.concatenate([scale, wu, u2], axis=0), v[0])
    s[1] = scaled(1, block(out, 0))
    s[2] = scaled(2, part[1] + row_of(ups[1]) * block(out, 1))
    f3 = v[1] + row_of(two[1]) * block(out, 2)
    f7 = v[3] + row_of(two[3]) * apply(u2, v[2])
    out = apply(jnp.concatenate([scale, wu, u2, u4], axis=0), f3)
    s[3] = scaled(3, block(out, 0))
    s[4] = scaled(4, part[2] + row_of(ups[3]) * block(out, 1))
    f5 = v[2] + row_of(two[2]) * block(out, 2)
    f7 = f7 + row_of(two[3] * two[2]) * block(out, 3)
    out = apply(jnp.concatenate([scale, wu], axis=0), f5)
    s[5] = scaled(5, block(out, 0))
    s[6] = scaled(6, part[3] + row_of(ups[5]) * block(out, 1))
    out = apply(end_stack, f7)
    f = row_of(ups[7]) * block(out, 0)
    s[7] = scaled(7, at_end(7, out))
    pair = [s[2 * k] + row_of(downs[2 * k + 1]) * apply(down, s[2 * k + 1]) for k in range(4)]
    two = [downs[2 * k + 1] * downs[2 * k + 2] for k in range(3)]
    first = pair[0] + row_of(two[0]) * apply(down24[:NP], pair[1])
    second = pair[2] + row_of(two[2]) * apply(down24[:NP], pair[3])
    g = first + row_of(two[0] * two[1]) * apply(down24[NP:], second)
    g = row_of(downs[0]) * apply(down, g)
    scaled_ref[CX, 0:CY, 0:LANES] = flags_ref[...].astype(F32)
    scaled_ref[CX, 8 : 8 + CX, 0:LANES] = order_ref[...].astype(F32)
    for y, (fy, gy) in enumerate(zip(columns(f), columns(g))):
        even, odd = regroup([fy, gy], NP)
        out_ref[2 * y, 0:NP, :] = even
        out_ref[2 * y + 1, 0:NP, :] = odd
    down_rate = x_rates(coef_ref, 0, 0)
    up_rate = jnp.ones_like(down_rate)
    gains = []
    for i in range(CX):
        gains.append(down_rate * up_rate / x_rates(coef_ref, 2, i))
        up_rate = up_rate * x_rates(coef_ref, 1, i)
        if i + 1 < CX:
            down_rate = down_rate * x_rates(coef_ref, 0, i + 1)
    last = gains.pop()
    is_last = rank == SX - 1
    flags = flags_ref[...]
    gains.append(jnp.where(is_last, 0.0, last))
    for kind in range(3):
        gains.append(jnp.where(jnp.logical_and(is_last, flags == kind), last, 0.0))
    values = [up_rate, down_rate] + gains + [jnp.zeros_like(last)] * 3
    for r in range(8):
        even, odd = regroup([values[2 * r], values[2 * r + 1]], NP)
        for y in range(CY):
            out_ref[2 * y, NP + r : NP + r + 1, :] = even[y : y + 1]
            out_ref[2 * y + 1, NP + r : NP + r + 1, :] = odd[y : y + 1]


def x_owner_kernel(in_ref, gain_ref, up_ref, down_ref, out_ref):
    half = SX // 2
    fs, gs, sa, sb = [], [], [], []
    for j in range(half):
        f, g = regroup([in_ref[j], in_ref[half + j]], NP)
        fs.append(f[:NP])
        gs.append(g[:NP])
        sa.append(f[NP:])
        sb.append(g[NP:])
    f = jnp.concatenate(fs, axis=1)
    g = jnp.concatenate(gs, axis=1)
    even = jnp.concatenate(sa, axis=1)
    odd = jnp.concatenate(sb, axis=1)
    scalar = [(even if k % 2 == 0 else odd)[k // 2 : k // 2 + 1] for k in range(13)]
    width, ncol = NP, half
    up_rate = scalar[0] * norm_of(up_ref)
    down_rate = scalar[1] * norm_of(down_ref)
    h = scan_segments(
        shifted(f, 1, width, ncol, False),
        shifted(up_rate, 1, width, ncol, False),
        up_ref,
        (7,),
        width,
        ncol,
        False,
    )
    vectors = split_vectors(h)
    through = product(gain_ref[0 : CX * NP], vectors)
    for i in range(CX):
        g = g + scalar[2 + i] * through[NP * i : NP * (i + 1)]
    ends = product(gain_ref[CX * NP :], vectors[:, LANES * (half - 1) :])
    extra = 0.0
    for kind in range(3):
        extra = extra + (
            scalar[10 + kind][:, LANES * (half - 1) :] * ends[NP * kind : NP * (kind + 1)]
        )
    g = jnp.concatenate([g[:, : LANES * (half - 1)], g[:, LANES * (half - 1) :] + extra], axis=1)
    e = scan_segments(
        shifted(g, 1, width, ncol, True),
        shifted(down_rate, 1, width, ncol, True),
        down_ref,
        (7,),
        width,
        ncol,
        True,
    )
    for j, (hj, ej) in enumerate(zip(columns(h), columns(e))):
        first, second = regroup([hj, ej], NP)
        out_ref[j] = first
        out_ref[half + j] = second


def y_rates(coef_ref, which, flip, p):
    here = coef_ref[which, pl.ds(p, CX, stride=CY), :]
    there = coef_ref[which, pl.ds(CY - 1 - p, CX, stride=CY), :]
    return jnp.where(flip, there, here)


def middle_kernel(
    rank_ref,
    local_ref,
    coef_ref,
    parts_ref,
    parts_y_ref,
    from_ref,
    in_ref,
    coef_y_ref,
    scaled_ref,
    out_ref,
    adj_ref,
):
    rank = rank_ref[0]
    parts = parts_ref[...]
    parts_y = parts_y_ref[...]
    down = parts
    u_y, w_y, wu_y, wu2_y, u3_y = [block(parts_y, k) for k in range(5)]
    up_scale_y = parts_y[: 2 * NP]
    down_y = parts_y[5 * NP :]
    hs, es = [], []
    for y in range(CY):
        h, e = regroup([in_ref[2 * y], in_ref[2 * y + 1]], NP)
        hs.append(h)
        es.append(e)
    through = apply(from_ref[...], jnp.concatenate(hs, axis=1))
    up_rates = [jnp.ones((CY, LANES), F32)]
    for i in range(CX - 1):
        up_rates.append(up_rates[-1] * x_rates(coef_ref, 1, i))
    downs = [x_rates(coef_ref, 0, i) for i in range(CX)]

    def scaled(i):
        term = through[NP * i : NP * (i + 1)]
        if i == CX - 1:
            ends = through[NP * CX :]
            chosen = jnp.where(
                flags == 0, ends[:NP], jnp.where(flags == 1, ends[NP : 2 * NP], ends[2 * NP :])
            )
            term = jnp.where(rank == SX - 1, chosen, term)
        return local_ref[i] + row_of(up_rates[i] / x_rates(coef_ref, 2, i)) * term

    def keep(i, g):
        for y in range(CY):
            adj_ref[y, :, LANES * i : LANES * (i + 1)] = g[:, LANES * y : LANES * (y + 1)]

    s = [scaled(i) for i in range(CX - 1)]
    pair = [
        s[2 * k] + row_of(downs[2 * k + 1]) * apply(block(down, 0), s[2 * k + 1]) for k in range(3)
    ]
    flags = row_of(local_ref[CX, 0:CY, 0:LANES])
    s.append(scaled(CX - 1) + jnp.concatenate(es, axis=1))
    keep(7, s[7])
    pair.append(s[6] + row_of(downs[7]) * apply(block(down, 0), s[7]))
    two = [downs[2 * k + 1] * downs[2 * k + 2] for k in range(3)]
    g = [pair[0], s[1], pair[1], s[3], pair[2], s[5]]
    for k in (3, 2, 1):
        out = apply(down[: 2 * k * NP], pair[k])
        weight = None
        for j in reversed(range(k)):
            odd = downs[2 * j + 2] if weight is None else weight * downs[2 * j + 2]
            weight = two[j] if weight is None else weight * two[j]
            power = 2 * (k - j)
            g[2 * j + 1] = g[2 * j + 1] + row_of(odd) * block(out, power - 2)
            g[2 * j] = g[2 * j] + row_of(weight) * block(out, power - 1)
    for i in range(6):
        keep(i, g[i])
    keep(6, pair[3])

    order = local_ref[CX, 8 : 8 + CX, 0:LANES]
    flip = order > 0
    flip_row = row_of(order) > 0

    def oriented(which, p):
        return y_rates(coef_y_ref, which, flip, p)

    a = [jnp.where(flip_row, adj_ref[CY - 1 - p], adj_ref[p]) for p in range(CY)]
    ups = [oriented(1, p) for p in range(CY)]
    downs = [oriented(0, p) for p in range(CY)]
    inverse = [row_of(1.0 / oriented(2, p)) for p in range(CY)]
    out = apply(up_scale_y, a[0])
    f1 = a[1] + row_of(ups[0]) * block(out, 0)
    s = [block(out, 1)]
    out2 = apply(up_scale_y, a[2])
    v3 = a[3] + row_of(ups[2]) * block(out2, 0)
    out1 = apply(jnp.concatenate([w_y, wu_y, wu2_y, u3_y], axis=0), f1)
    out3 = apply(up_scale_y, v3)
    two = ups[1] * ups[2]
    s.append(block(out1, 0))
    s.append(block(out2, 1) + row_of(ups[1]) * block(out1, 1))
    s.append(block(out3, 1) + row_of(two) * block(out1, 2))
    f = row_of(ups[3]) * block(out3, 0) + row_of(ups[3] * two) * block(out1, 3)
    g, weight = 0.0, downs[0]
    for p in range(CY):
        value = s[p] * inverse[p]
        scaled_ref[p] = value
        g = g + row_of(weight) * apply(block(down_y, p), value)
        if p + 1 < CY:
            weight = weight * downs[p + 1]

    down_rate = oriented(0, 0)
    up_rate = jnp.ones_like(down_rate)
    gains = []
    for p in range(CY):
        gains.append(down_rate * up_rate / oriented(2, p))
        up_rate = up_rate * oriented(1, p)
        if p + 1 < CY:
            down_rate = down_rate * oriented(0, p + 1)
    first = regroup([up_rate, down_rate, gains[0], gains[1]], 32)
    second = regroup([gains[2], gains[3], flip.astype(F32), jnp.zeros_like(up_rate)], 32)
    for x, (fx, gx) in enumerate(zip(columns(f), columns(g))):
        chunks = regroup([fx[:32], fx[32:], gx[:32], gx[32:]], 32)
        for a in range(4):
            row = ROWS * (4 * x + a)
            out_ref[row : row + 32, :] = chunks[a]
            out_ref[row + 32 : row + 33, :] = first[a][x : x + 1]
            out_ref[row + 33 : row + 34, :] = second[a][x : x + 1]


def y_owner_kernel(in_ref, gain_ref, up_ref, down_ref, out_ref, res_ref):
    width, ncol = 32, 8
    flip = replicate(in_ref[33:34, :], width)[2] > 0.5

    def oriented(s):
        t = SY - 1 - s
        return jnp.where(flip, in_ref[ROWS * t : ROWS * (t + 1), :], in_ref[ROWS * s : ROWS * (s + 1), :])

    fs, gs, ss = [], [], []
    for j in range(ncol):
        outs = regroup([oriented(ncol * a + j) for a in range(4)], width)
        fs.append(jnp.concatenate([outs[0][:32], outs[1][:32]], axis=0))
        gs.append(jnp.concatenate([outs[2][:32], outs[3][:32]], axis=0))
        ss.append([o[32:33] for o in outs] + [o[33:34] for o in outs[:2]])
    f = jnp.concatenate(fs, axis=1)
    g = jnp.concatenate(gs, axis=1)
    scalars = [jnp.concatenate([s[k] for s in ss], axis=1) for k in range(6)]
    up_rate = scalars[0] * norm_of(up_ref)
    down_rate = scalars[1] * norm_of(down_ref)
    h = scan_segments(
        shifted(f, 1, width, ncol, False),
        shifted(up_rate, 1, width, ncol, False),
        up_ref,
        (7, 3),
        width,
        ncol,
        False,
    )
    through = apply(gain_ref[...], h)
    for p in range(CY):
        g = g + scalars[2 + p] * through[NP * p : NP * (p + 1)]
    e = scan_segments(
        shifted(g, 1, width, ncol, True),
        shifted(down_rate, 1, width, ncol, True),
        down_ref,
        (7, 3),
        width,
        ncol,
        True,
    )
    for j, (hj, ej) in enumerate(zip(columns(h), columns(e))):
        outs = regroup([hj[:32], hj[32:], ej[:32], ej[32:]], width)
        for a in range(4):
            res_ref[ncol * a + j] = outs[a]
    for s in range(SY):
        out_ref[s] = jnp.where(flip, res_ref[SY - 1 - s], res_ref[s])


def y_final_kernel(
    local_ref, coef_y_ref, order_ref, parts_ref, from_ref, in_ref, out_hbm, out_ref, sems
):
    down = parts_ref[5 * NP : 8 * NP, :]
    flip = order_ref[...] > 0

    def oriented(which, p):
        return y_rates(coef_y_ref, which, flip, p)

    up_rates = [jnp.ones((CX, LANES), F32)]
    for p in range(CY - 1):
        up_rates.append(up_rates[-1] * oriented(1, p))
    term_rates = [up_rates[p] / oriented(2, p) for p in range(CY)]
    downs = [oriented(0, p) for p in range(CY)]
    part = CX // HALVES
    copies = []
    for half in range(HALVES):
        first = part * half
        lanes = slice(LANES * first, LANES * (first + part))

        def row(rate):
            return row_of(rate[first : first + part])

        hs, es = [], []
        for x in range(first, first + part):
            outs = regroup([in_ref[4 * x + a] for a in range(4)], 32)
            hs.append(jnp.concatenate(outs[:2], axis=0))
            es.append(jnp.concatenate(outs[2:], axis=0))
        through = apply(from_ref[...], jnp.concatenate(hs, axis=1))
        s = [local_ref[p, :, lanes] + row(term_rates[p]) * block(through, p) for p in range(CY)]
        s[3] = s[3] + jnp.concatenate(es, axis=1)
        g = list(s)
        for p in (3, 2, 1):
            out = apply(down[: NP * p], s[p])
            weight = None
            for j in reversed(range(p)):
                weight = downs[j + 1] if weight is None else weight * downs[j + 1]
                g[j] = g[j] + row(weight) * block(out, p - 1 - j)
        flip_row = row_of(order_ref[first : first + part, :]) > 0
        planes = out_ref.at[half].reshape(NP * CY * part, LANES)
        for y in range(CY):
            plane = jnp.where(flip_row, g[CY - 1 - y], g[y])
            for x, piece in enumerate(columns(plane)):
                planes[pl.ds(CY * x + y, NP, stride=CY * part), :] = piece
        target = out_hbm.at[:, CY * first : CY * (first + part), :]
        copies.append(pltpu.make_async_copy(out_ref.at[half], target, sems.at[half]))
        copies[-1].start()
    for copy in copies:
        copy.wait()


def in_hbm(a):
    return pltpu.with_memory_space_constraint(a, pltpu.HBM)


def call(kernel, outs, spaces, scratch=(), scalars=0):
    shapes = tuple(space(dims, dtype) for space, dims, dtype in outs)
    specs = [pl.BlockSpec(memory_space=pltpu.SMEM)] * scalars
    specs += [pl.BlockSpec(memory_space=s) for s in spaces]
    return pl.pallas_call(
        kernel,
        out_shape=shapes,
        in_specs=specs,
        out_specs=tuple(pl.BlockSpec(memory_space=out[0]) for out in outs),
        scratch_shapes=list(scratch),
        compiler_params=pltpu.CompilerParams(vmem_limit_bytes=VMEM_LIMIT),
    )


def per_device(
    rhs,
    coef_x,
    coef_y,
    out_coupling_x,
    in_coupling_x,
    inverse_x,
    boundary_inverse,
    out_coupling_y,
    in_coupling_y,
    inverse_y,
    bc_flags,
    line_order,
):
    vmem, hbm = pltpu.VMEM, pltpu.HBM
    rank = lax.axis_index("gx").astype(jnp.int32).reshape(1)
    mats_x = (out_coupling_x, inverse_x, in_coupling_x, boundary_inverse)
    mats_y = (out_coupling_y, inverse_y, in_coupling_y)
    rhs = rhs.reshape(NP, CX * CY, LANES)
    coef_x = coef_x.reshape(3, CX * CY, LANES)
    coef_y = coef_y.reshape(3, CX * CY, LANES)

    sent, local, tiles, raw_y = call(
        x_local_kernel,
        (
            (vmem, (SX, NP + 8, LANES), F32),
            (vmem, (CX + 1, NP, CY * LANES), F32),
            (vmem, (6 * NP, 4 * NP), F32),
            (vmem, (3, NP, NP), F32),
        ),
        (hbm,) * 11,
        [
            vmem((PIECES, NP, 8, LANES), F32),
            vmem((3, CX * CY, LANES), F32),
            vmem((CY, LANES), jnp.int32),
            vmem((CX, LANES), jnp.int32),
            vmem((3, NP, NP), F32),
            vmem((3, NP, NP), F32),
            pltpu.SemaphoreType.DMA((10 + PIECES,)),
        ],
        1,
    )(rank, *[in_hbm(a) for a in (rhs, coef_x, bc_flags) + mats_x + mats_y + (line_order,)])
    got = lax.all_to_all(sent, "gx", 0, 0, tiled=True)
    later = [
        (rows, 4 * NP)
        for rows in (11 * NP, 6 * NP, 9 * NP, 4 * NP, 4 * NP, 10 * NP + 16, 10 * NP + 16)
    ]
    gain_x, up_x, down_x, from_x, parts_x, parts_y, gain_y, from_y, up_y, down_y = call(
        prepare_kernel,
        (
            (vmem, (11 * NP, 4 * NP), BF16),
            (vmem, (7 * NP + 16, 4 * NP), BF16),
            (vmem, (7 * NP + 16, 4 * NP), BF16),
        )
        + tuple((hbm, dims, BF16) for dims in later),
        (vmem, vmem),
        [vmem(dims, BF16) for dims in later] + [pltpu.SemaphoreType.DMA((7,))],
    )(tiles, raw_y)
    (back,) = call(x_owner_kernel, ((vmem, (SX, NP, LANES), F32),), (vmem,) * 4)(
        got, gain_x, up_x, down_x
    )
    terms = lax.all_to_all(back, "gx", 0, 0, tiled=True)
    local, sent = call(
        middle_kernel,
        ((vmem, (CY, NP, CX * LANES), F32), (vmem, (SY * ROWS, LANES), F32)),
        (vmem,) * 7,
        [vmem((CY, NP, CX * LANES), F32)],
        1,
    )(rank, local, coef_x, parts_x, parts_y, from_x, terms, coef_y)
    got = lax.all_to_all(sent.reshape(SY, ROWS // 2, 2, LANES), "gy", 0, 0, tiled=True)
    (back,) = call(
        y_owner_kernel,
        ((vmem, (SY, 32, LANES), F32),),
        (vmem,) * 4,
        [vmem((SY, 32, LANES), F32)],
    )(got.reshape(SY * ROWS, LANES), gain_y, up_y, down_y)
    terms = lax.all_to_all(back, "gy", 0, 0, tiled=True)
    (out,) = call(
        y_final_kernel,
        ((hbm, (NP, CX * CY, LANES), F32),),
        (vmem,) * 6,
        [
            vmem((HALVES, NP, CX * CY // HALVES, LANES), F32),
            pltpu.SemaphoreType.DMA((HALVES,)),
        ],
    )(local, coef_y, line_order, parts_y, from_y, terms)
    return out.reshape(NP, CX, CY, LANES)


def solution(mesh):
    grid = P(None, "gx", "gy", None)
    in_specs = (grid, grid, grid) + (P(),) * 7 + (P("gy", None), P("gx", None))
    return jax.shard_map(
        per_device, mesh=mesh, in_specs=in_specs, out_specs=grid, check_vma=False
    )
```

```python
import jax
import jax.numpy as jnp
from jax import lax
from jax.experimental import pallas as pl
from jax.experimental.pallas import tpu as pltpu
from jax.sharding import PartitionSpec as P

NP = 64
LANES = 128
CX = 8
PIECES = 4
HALVES = 2
CY = 4
SX = 8
SY = 32
ROWS = 34
F32 = jnp.float32
BF16 = jnp.bfloat16
VMEM_LIMIT = 48 * 1024 * 1024


def rounded(v):
    return v.astype(BF16).astype(F32)


def split_matrix(m):
    high = rounded(m)
    rest = m - high
    mid = rounded(rest)
    low = rest - mid
    part = lax.broadcasted_iota(jnp.int32, m.shape, 1) // NP
    return jnp.where(part == 1, mid, jnp.where(part == 3, low, high)).astype(BF16)


def split_vectors(v):
    high = v.astype(BF16)
    low = (v - high.astype(F32)).astype(BF16)
    return jnp.concatenate([high, high, low, high], axis=0)


def product(parts, vectors):
    return jnp.dot(parts, vectors, preferred_element_type=F32)


def apply(parts, v):
    return product(parts, split_vectors(v))


def lane_iota(shape):
    return lax.broadcasted_iota(jnp.int32, shape, len(shape) - 1)


def roll(v, shift):
    shift = shift % LANES
    return v if shift == 0 else pltpu.roll(v, shift, 1)


def row_of(block):
    return jnp.concatenate([block[r : r + 1] for r in range(block.shape[0])], axis=1)


def columns(v):
    return [v[:, LANES * j : LANES * (j + 1)] for j in range(v.shape[1] // LANES)]


def regroup(blocks, width):
    n = LANES // width
    rolled = [[roll(b, width * k) for k in range(n)] for b in blocks]
    group = lane_iota(blocks[0].shape) // width
    outs = []
    for a in range(n):
        acc = rolled[0][(0 - a) % n]
        for q in range(1, n):
            acc = jnp.where(group == q, rolled[q][(q - a) % n], acc)
        outs.append(acc)
    return outs


def replicate(block, width):
    return regroup([block] * (LANES // width), width)


def shifted(v, t, width, ncol, reverse):
    cols = columns(v)
    group = lane_iota(cols[0].shape) // width
    n = LANES // width
    out = []
    for j in range(ncol):
        k = j + t if reverse else j - t
        carry = abs(k // ncol)
        src = cols[k % ncol]
        if carry:
            if reverse:
                src = jnp.where(group < n - carry, roll(src, -width * carry), 0.0)
            else:
                src = jnp.where(group >= carry, roll(src, width * carry), 0.0)
        out.append(src)
    return jnp.concatenate(out, axis=1)


def block(stack, k):
    return stack[NP * k : NP * (k + 1)]


def scan_segments(v, rate, powers, counts, width, ncol, reverse):
    stride, row = 1, 0
    for count in counts:
        out = apply(powers[NP * row : NP * (row + count), :], v)
        weight = rate
        for t in range(1, count + 1):
            v = v + weight * shifted(block(out, t - 1), stride * t, width, ncol, reverse)
            weight = rate * shifted(weight, stride, width, ncol, reverse)
        rate = weight
        row += count
        stride *= count + 1
    return v


def tiled(m):
    pair = jnp.concatenate([m, m], axis=0).T
    return jnp.concatenate([pair, pair], axis=1)


def multiply(a, b):
    parts = split_matrix(a)
    high = b.astype(BF16)
    rest = b - high.astype(F32)
    mid = rest.astype(BF16)
    low = (rest - mid.astype(F32)).astype(BF16)
    none = jnp.zeros_like(low)
    return product(parts, jnp.concatenate([high, high, mid, high], axis=0)) + product(
        parts, jnp.concatenate([low, mid, none, none], axis=0)
    )


def powers_of(m, count):
    stack = m
    while stack.shape[0] < count * NP:
        done = stack.shape[0] // NP
        more = min(done, count - done)
        stack = jnp.concatenate([stack, multiply(stack[: NP * more], block(stack, done - 1))], axis=0)
    return stack


def prepare(cells, far, up, down, scale, bounds, gain_ref, from_ref, up_ref, down_ref, done):
    halves = cells.bit_length() - 1
    ups = [up]
    for _ in range(halves):
        ups.append(multiply(ups[-1], ups[-1]))
    scaled = scale
    for k in range(halves):
        scaled = jnp.concatenate([scaled, apply(split_matrix(scaled), ups[k])], axis=0)
    from_ref[0 : cells * NP, :] = split_matrix(scaled)
    if bounds is not None:
        for k in range(halves):
            bounds = apply(split_matrix(bounds), ups[k])
        from_ref[cells * NP :, :] = split_matrix(bounds)
    done(from_ref)
    downs = powers_of(down, cells)
    stack = split_matrix(downs)
    for j in range(cells):
        gain = apply(block(stack, j), block(scaled, j))
        gain_ref[NP * j : NP * (j + 1), :] = split_matrix(gain)
    if bounds is not None:
        for kind in range(3):
            gain = apply(block(stack, cells - 1), block(bounds, kind))
            gain_ref[NP * (cells + kind) : NP * (cells + kind + 1), :] = split_matrix(gain)
    done(gain_ref)
    tops = ((ups[halves], up_ref), (block(downs, cells - 1), down_ref))
    for power, ref in tops:
        norm = jnp.max(jnp.sum(jnp.abs(power[:, :NP]), axis=1, keepdims=True), axis=0, keepdims=True)
        norm = jnp.maximum(norm, 1e-30)
        count = ref.shape[0] // NP
        ref[count * NP :, :] = split_matrix(jnp.broadcast_to(norm, (16, 4 * NP)))
        near = powers_of(power / norm, 7)
        ref[0 : 7 * NP, :] = split_matrix(near)
        if far:
            power8 = multiply(block(near, 3), block(near, 3))
            power16 = multiply(power8, power8)
            power24 = multiply(power16, power8)
            ref[7 * NP : 10 * NP, :] = split_matrix(
                jnp.concatenate([power8, power16, power24], axis=0)
            )
        done(ref)
    return ups, scaled, stack


def norm_of(ref):
    parts = ref[ref.shape[0] - 16 :, :].astype(F32)[0:1]
    return parts[:, 0:1] + parts[:, NP : NP + 1] + parts[:, 3 * NP : 3 * NP + 1]


def prepare_kernel(
    mats_ref,
    raw_ref,
    gain_ref,
    up_ref,
    down_ref,
    from_hbm,
    parts_hbm,
    parts_y_hbm,
    gain_y_hbm,
    from_y_hbm,
    up_y_hbm,
    down_y_hbm,
    from_ref,
    parts_ref,
    parts_y_ref,
    gain_y_ref,
    from_y_ref,
    up_y_ref,
    down_y_ref,
    sems,
):
    targets = (
        (from_ref, from_hbm),
        (parts_ref, parts_hbm),
        (parts_y_ref, parts_y_hbm),
        (gain_y_ref, gain_y_hbm),
        (from_y_ref, from_y_hbm),
        (up_y_ref, up_y_hbm),
        (down_y_ref, down_y_hbm),
    )
    sends = []

    def done(ref):
        for k, (source, target) in enumerate(targets):
            if source is ref:
                sends.append(pltpu.make_async_copy(source, target, sems.at[k]))
                sends[-1].start()

    ux, wx, b0, b1, b2, dx = [mats_ref[NP * k : NP * (k + 1), :] for k in range(6)]
    bounds = jnp.concatenate([b0, b1, b2], axis=0)
    _, _, stack = prepare(
        CX, False, ux, dx, wx, bounds, gain_ref, from_ref, up_ref, down_ref, done
    )
    parts_ref[...] = stack[: 6 * NP]
    done(parts_ref)
    uy, wy, dy = [tiled(raw_ref[k]) for k in range(3)]
    ups, scaled, stack = prepare(
        CY, True, uy, dy, wy, None, gain_y_ref, from_y_ref, up_y_ref, down_y_ref, done
    )
    extra = [uy, scaled[: 3 * NP], multiply(ups[1], uy)]
    parts_y_ref[0 : 5 * NP, :] = split_matrix(jnp.concatenate(extra, axis=0))
    parts_y_ref[5 * NP :, :] = stack
    done(parts_y_ref)
    for copy in sends:
        copy.wait()


def x_rates(coef_ref, which, i):
    return coef_ref[which, CY * i : CY * (i + 1), :]


def x_local_kernel(
    rank_ref,
    rhs_hbm,
    coef_hbm,
    flags_hbm,
    ux,
    wx,
    dx,
    b,
    uy,
    wy,
    dy,
    order_hbm,
    out_ref,
    scaled_ref,
    mats_ref,
    raw_y_ref,
    rhs_ref,
    coef_ref,
    flags_ref,
    order_ref,
    raw_ref,
    bounds_ref,
    sems,
):
    rank = rank_ref[0]
    sources = [ux, wx, b, dx, coef_hbm, flags_hbm]
    targets = [raw_ref.at[0], raw_ref.at[1], bounds_ref, raw_ref.at[2], coef_ref, flags_ref]
    for k in range(PIECES):
        sources.append(rhs_hbm.at[:, 8 * k : 8 * (k + 1), :])
        targets.append(rhs_ref.at[k])
    sources += [uy, wy, dy, order_hbm]
    targets += [raw_y_ref.at[0], raw_y_ref.at[1], raw_y_ref.at[2], order_ref]
    copies = []
    for k, (source, target) in enumerate(zip(sources, targets)):
        copies.append(pltpu.make_async_copy(source, target, sems.at[k]))
    for k in range(len(copies)):
        copies[k].start()
    for copy in copies[:6]:
        copy.wait()

    def place(row, m):
        value = tiled(m)
        mats_ref[NP * row : NP * (row + 1), :] = value
        return split_matrix(value)

    up, scale = place(0, raw_ref[0]), place(1, raw_ref[1])
    bounds = [place(2 + k, bounds_ref[k]) for k in range(3)]
    down = place(5, raw_ref[2])
    up_scale = jnp.concatenate([up, scale], axis=0)
    end_stack = jnp.concatenate([up, scale] + bounds, axis=0)
    u, w = mats_ref[0:NP, :], mats_ref[NP : 2 * NP, :]
    d = mats_ref[5 * NP :, :]
    u2 = multiply(u, u)
    wu = split_matrix(multiply(w, u))
    u4 = split_matrix(multiply(u2, u2))
    u2 = split_matrix(u2)
    d2 = multiply(d, d)
    down24 = split_matrix(jnp.concatenate([d2, multiply(d2, d2)], axis=0))
    for copy in copies[6:]:
        copy.wait()
    planes = rhs_ref.reshape(PIECES * NP * 8, LANES)

    ups = [x_rates(coef_ref, 1, i) for i in range(CX)]
    downs = [x_rates(coef_ref, 0, i) for i in range(CX)]
    flags = row_of(flags_ref[...])

    def given(i):
        start = (CY * i // 8) * NP * 8 + CY * i % 8
        return jnp.concatenate(
            [planes[pl.ds(start + y, NP, stride=8), :] for y in range(CY)], axis=1
        )

    def at_end(i, out):
        chosen = jnp.where(
            flags == 0, block(out, 2), jnp.where(flags == 1, block(out, 3), block(out, 4))
        )
        return jnp.where(rank == (0 if i == 0 else SX - 1), chosen, block(out, 1))

    def scaled(i, value):
        value = value * row_of(1.0 / x_rates(coef_ref, 2, i))
        scaled_ref[i] = value
        return value

    s, v, part = [None] * CX, [], []
    for k in range(PIECES):
        out = apply(end_stack if k == 0 else up_scale, given(2 * k))
        v.append(given(2 * k + 1) + row_of(ups[2 * k]) * block(out, 0))
        part.append(at_end(0, out) if k == 0 else block(out, 1))
    two = [None] + [ups[2 * k] * ups[2 * k - 1] for k in range(1, 4)]
    s[0] = scaled(0, part[0])
    out = apply(jnp.concatenate([scale, wu, u2], axis=0), v[0])
    s[1] = scaled(1, block(out, 0))
    s[2] = scaled(2, part[1] + row_of(ups[1]) * block(out, 1))
    f3 = v[1] + row_of(two[1]) * block(out, 2)
    f7 = v[3] + row_of(two[3]) * apply(u2, v[2])
    out = apply(jnp.concatenate([scale, wu, u2, u4], axis=0), f3)
    s[3] = scaled(3, block(out, 0))
    s[4] = scaled(4, part[2] + row_of(ups[3]) * block(out, 1))
    f5 = v[2] + row_of(two[2]) * block(out, 2)
    f7 = f7 + row_of(two[3] * two[2]) * block(out, 3)
    out = apply(jnp.concatenate([scale, wu], axis=0), f5)
    s[5] = scaled(5, block(out, 0))
    s[6] = scaled(6, part[3] + row_of(ups[5]) * block(out, 1))
    out = apply(end_stack, f7)
    f = row_of(ups[7]) * block(out, 0)
    s[7] = scaled(7, at_end(7, out))
    pair = [s[2 * k] + row_of(downs[2 * k + 1]) * apply(down, s[2 * k + 1]) for k in range(4)]
    two = [downs[2 * k + 1] * downs[2 * k + 2] for k in range(3)]
    first = pair[0] + row_of(two[0]) * apply(down24[:NP], pair[1])
    second = pair[2] + row_of(two[2]) * apply(down24[:NP], pair[3])
    g = first + row_of(two[0] * two[1]) * apply(down24[NP:], second)
    g = row_of(downs[0]) * apply(down, g)
    scaled_ref[CX, 0:CY, 0:LANES] = flags_ref[...].astype(F32)
    scaled_ref[CX, 8 : 8 + CX, 0:LANES] = order_ref[...].astype(F32)
    for y, (fy, gy) in enumerate(zip(columns(f), columns(g))):
        even, odd = regroup([fy, gy], NP)
        out_ref[2 * y, 0:NP, :] = even
        out_ref[2 * y + 1, 0:NP, :] = odd
    down_rate = x_rates(coef_ref, 0, 0)
    up_rate = jnp.ones_like(down_rate)
    gains = []
    for i in range(CX):
        gains.append(down_rate * up_rate / x_rates(coef_ref, 2, i))
        up_rate = up_rate * x_rates(coef_ref, 1, i)
        if i + 1 < CX:
            down_rate = down_rate * x_rates(coef_ref, 0, i + 1)
    last = gains.pop()
    is_last = rank == SX - 1
    flags = flags_ref[...]
    gains.append(jnp.where(is_last, 0.0, last))
    for kind in range(3):
        gains.append(jnp.where(jnp.logical_and(is_last, flags == kind), last, 0.0))
    values = [up_rate, down_rate] + gains + [jnp.zeros_like(last)] * 3
    for r in range(8):
        even, odd = regroup([values[2 * r], values[2 * r + 1]], NP)
        for y in range(CY):
            out_ref[2 * y, NP + r : NP + r + 1, :] = even[y : y + 1]
            out_ref[2 * y + 1, NP + r : NP + r + 1, :] = odd[y : y + 1]


def x_owner_kernel(in_ref, gain_ref, up_ref, down_ref, out_ref):
    half = SX // 2
    fs, gs, sa, sb = [], [], [], []
    for j in range(half):
        f, g = regroup([in_ref[j], in_ref[half + j]], NP)
        fs.append(f[:NP])
        gs.append(g[:NP])
        sa.append(f[NP:])
        sb.append(g[NP:])
    f = jnp.concatenate(fs, axis=1)
    g = jnp.concatenate(gs, axis=1)
    even = jnp.concatenate(sa, axis=1)
    odd = jnp.concatenate(sb, axis=1)
    scalar = [(even if k % 2 == 0 else odd)[k // 2 : k // 2 + 1] for k in range(13)]
    width, ncol = NP, half
    up_rate = scalar[0] * norm_of(up_ref)
    down_rate = scalar[1] * norm_of(down_ref)
    h = scan_segments(
        shifted(f, 1, width, ncol, False),
        shifted(up_rate, 1, width, ncol, False),
        up_ref,
        (7,),
        width,
        ncol,
        False,
    )
    vectors = split_vectors(h)
    through = product(gain_ref[0 : CX * NP], vectors)
    for i in range(CX):
        g = g + scalar[2 + i] * through[NP * i : NP * (i + 1)]
    ends = product(gain_ref[CX * NP :], vectors[:, LANES * (half - 1) :])
    extra = 0.0
    for kind in range(3):
        extra = extra + (
            scalar[10 + kind][:, LANES * (half - 1) :] * ends[NP * kind : NP * (kind + 1)]
        )
    g = jnp.concatenate([g[:, : LANES * (half - 1)], g[:, LANES * (half - 1) :] + extra], axis=1)
    e = scan_segments(
        shifted(g, 1, width, ncol, True),
        shifted(down_rate, 1, width, ncol, True),
        down_ref,
        (7,),
        width,
        ncol,
        True,
    )
    for j, (hj, ej) in enumerate(zip(columns(h), columns(e))):
        first, second = regroup([hj, ej], NP)
        out_ref[j] = first
        out_ref[half + j] = second


def y_rates(coef_ref, which, flip, p):
    here = coef_ref[which, pl.ds(p, CX, stride=CY), :]
    there = coef_ref[which, pl.ds(CY - 1 - p, CX, stride=CY), :]
    return jnp.where(flip, there, here)


def middle_kernel(
    rank_ref,
    local_ref,
    coef_ref,
    parts_ref,
    parts_y_ref,
    from_ref,
    in_ref,
    coef_y_ref,
    scaled_ref,
    out_ref,
    adj_ref,
):
    rank = rank_ref[0]
    parts = parts_ref[...]
    parts_y = parts_y_ref[...]
    down = parts
    u_y, w_y, wu_y, wu2_y, u3_y = [block(parts_y, k) for k in range(5)]
    up_scale_y = parts_y[: 2 * NP]
    down_y = parts_y[5 * NP :]
    hs, es = [], []
    for y in range(CY):
        h, e = regroup([in_ref[2 * y], in_ref[2 * y + 1]], NP)
        hs.append(h)
        es.append(e)
    through = apply(from_ref[...], jnp.concatenate(hs, axis=1))
    up_rates = [jnp.ones((CY, LANES), F32)]
    for i in range(CX - 1):
        up_rates.append(up_rates[-1] * x_rates(coef_ref, 1, i))
    downs = [x_rates(coef_ref, 0, i) for i in range(CX)]

    def scaled(i):
        term = through[NP * i : NP * (i + 1)]
        if i == CX - 1:
            ends = through[NP * CX :]
            chosen = jnp.where(
                flags == 0, ends[:NP], jnp.where(flags == 1, ends[NP : 2 * NP], ends[2 * NP :])
            )
            term = jnp.where(rank == SX - 1, chosen, term)
        return local_ref[i] + row_of(up_rates[i] / x_rates(coef_ref, 2, i)) * term

    def keep(i, g):
        for y in range(CY):
            adj_ref[y, :, LANES * i : LANES * (i + 1)] = g[:, LANES * y : LANES * (y + 1)]

    s = [scaled(i) for i in range(CX - 1)]
    pair = [
        s[2 * k] + row_of(downs[2 * k + 1]) * apply(block(down, 0), s[2 * k + 1]) for k in range(3)
    ]
    flags = row_of(local_ref[CX, 0:CY, 0:LANES])
    s.append(scaled(CX - 1) + jnp.concatenate(es, axis=1))
    keep(7, s[7])
    pair.append(s[6] + row_of(downs[7]) * apply(block(down, 0), s[7]))
    two = [downs[2 * k + 1] * downs[2 * k + 2] for k in range(3)]
    g = [pair[0], s[1], pair[1], s[3], pair[2], s[5]]
    for k in (3, 2, 1):
        out = apply(down[: 2 * k * NP], pair[k])
        weight = None
        for j in reversed(range(k)):
            odd = downs[2 * j + 2] if weight is None else weight * downs[2 * j + 2]
            weight = two[j] if weight is None else weight * two[j]
            power = 2 * (k - j)
            g[2 * j + 1] = g[2 * j + 1] + row_of(odd) * block(out, power - 2)
            g[2 * j] = g[2 * j] + row_of(weight) * block(out, power - 1)
    for i in range(6):
        keep(i, g[i])
    keep(6, pair[3])

    order = local_ref[CX, 8 : 8 + CX, 0:LANES]
    flip = order > 0
    flip_row = row_of(order) > 0

    def oriented(which, p):
        return y_rates(coef_y_ref, which, flip, p)

    a = [jnp.where(flip_row, adj_ref[CY - 1 - p], adj_ref[p]) for p in range(CY)]
    ups = [oriented(1, p) for p in range(CY)]
    downs = [oriented(0, p) for p in range(CY)]
    inverse = [row_of(1.0 / oriented(2, p)) for p in range(CY)]
    out = apply(up_scale_y, a[0])
    f1 = a[1] + row_of(ups[0]) * block(out, 0)
    s = [block(out, 1)]
    out2 = apply(up_scale_y, a[2])
    v3 = a[3] + row_of(ups[2]) * block(out2, 0)
    out1 = apply(jnp.concatenate([w_y, wu_y, wu2_y, u3_y], axis=0), f1)
    out3 = apply(up_scale_y, v3)
    two = ups[1] * ups[2]
    s.append(block(out1, 0))
    s.append(block(out2, 1) + row_of(ups[1]) * block(out1, 1))
    s.append(block(out3, 1) + row_of(two) * block(out1, 2))
    f = row_of(ups[3]) * block(out3, 0) + row_of(ups[3] * two) * block(out1, 3)
    g, weight = 0.0, downs[0]
    for p in range(CY):
        value = s[p] * inverse[p]
        scaled_ref[p] = value
        g = g + row_of(weight) * apply(block(down_y, p), value)
        if p + 1 < CY:
            weight = weight * downs[p + 1]

    down_rate = oriented(0, 0)
    up_rate = jnp.ones_like(down_rate)
    gains = []
    for p in range(CY):
        gains.append(down_rate * up_rate / oriented(2, p))
        up_rate = up_rate * oriented(1, p)
        if p + 1 < CY:
            down_rate = down_rate * oriented(0, p + 1)
    first = regroup([up_rate, down_rate, gains[0], gains[1]], 32)
    second = regroup([gains[2], gains[3], flip.astype(F32), jnp.zeros_like(up_rate)], 32)
    for x, (fx, gx) in enumerate(zip(columns(f), columns(g))):
        chunks = regroup([fx[:32], fx[32:], gx[:32], gx[32:]], 32)
        for a in range(4):
            row = ROWS * (4 * x + a)
            out_ref[row : row + 32, :] = chunks[a]
            out_ref[row + 32 : row + 33, :] = first[a][x : x + 1]
            out_ref[row + 33 : row + 34, :] = second[a][x : x + 1]


def y_owner_kernel(in_ref, gain_ref, up_ref, down_ref, out_ref, res_ref):
    width, ncol = 32, 8
    flip = replicate(in_ref[33:34, :], width)[2] > 0.5

    def oriented(s):
        t = SY - 1 - s
        return jnp.where(flip, in_ref[ROWS * t : ROWS * (t + 1), :], in_ref[ROWS * s : ROWS * (s + 1), :])

    fs, gs, ss = [], [], []
    for j in range(ncol):
        outs = regroup([oriented(ncol * a + j) for a in range(4)], width)
        fs.append(jnp.concatenate([outs[0][:32], outs[1][:32]], axis=0))
        gs.append(jnp.concatenate([outs[2][:32], outs[3][:32]], axis=0))
        ss.append([o[32:33] for o in outs] + [o[33:34] for o in outs[:2]])
    f = jnp.concatenate(fs, axis=1)
    g = jnp.concatenate(gs, axis=1)
    scalars = [jnp.concatenate([s[k] for s in ss], axis=1) for k in range(6)]
    up_rate = scalars[0] * norm_of(up_ref)
    down_rate = scalars[1] * norm_of(down_ref)
    h = scan_segments(
        shifted(f, 1, width, ncol, False),
        shifted(up_rate, 1, width, ncol, False),
        up_ref,
        (7, 3),
        width,
        ncol,
        False,
    )
    through = apply(gain_ref[...], h)
    for p in range(CY):
        g = g + scalars[2 + p] * through[NP * p : NP * (p + 1)]
    e = scan_segments(
        shifted(g, 1, width, ncol, True),
        shifted(down_rate, 1, width, ncol, True),
        down_ref,
        (7, 3),
        width,
        ncol,
        True,
    )
    for j, (hj, ej) in enumerate(zip(columns(h), columns(e))):
        outs = regroup([hj[:32], hj[32:], ej[:32], ej[32:]], width)
        for a in range(4):
            res_ref[ncol * a + j] = outs[a]
    for s in range(SY):
        out_ref[s] = jnp.where(flip, res_ref[SY - 1 - s], res_ref[s])


def y_final_kernel(
    local_ref, coef_y_ref, order_ref, parts_ref, from_ref, in_ref, out_hbm, out_ref, sems
):
    down = parts_ref[5 * NP : 8 * NP, :]
    flip = order_ref[...] > 0

    def oriented(which, p):
        return y_rates(coef_y_ref, which, flip, p)

    up_rates = [jnp.ones((CX, LANES), F32)]
    for p in range(CY - 1):
        up_rates.append(up_rates[-1] * oriented(1, p))
    term_rates = [up_rates[p] / oriented(2, p) for p in range(CY)]
    downs = [oriented(0, p) for p in range(CY)]
    part = CX // HALVES
    copies, sums = [], []
    for half in range(HALVES):
        first = part * half
        lanes = slice(LANES * first, LANES * (first + part))

        def row(rate):
            return row_of(rate[first : first + part])

        hs, es = [], []
        for x in range(first, first + part):
            outs = regroup([in_ref[4 * x + a] for a in range(4)], 32)
            hs.append(jnp.concatenate(outs[:2], axis=0))
            es.append(jnp.concatenate(outs[2:], axis=0))
        through = apply(from_ref[...], jnp.concatenate(hs, axis=1))
        s = [local_ref[p, :, lanes] + row(term_rates[p]) * block(through, p) for p in range(CY)]
        s[3] = s[3] + jnp.concatenate(es, axis=1)
        sums.append(s)
    for half, s in enumerate(sums):
        first = part * half

        def row(rate):
            return row_of(rate[first : first + part])

        g = list(s)
        for p in (3, 2, 1):
            out = apply(down[: NP * p], s[p])
            weight = None
            for j in reversed(range(p)):
                weight = downs[j + 1] if weight is None else weight * downs[j + 1]
                g[j] = g[j] + row(weight) * block(out, p - 1 - j)
        flip_row = row_of(order_ref[first : first + part, :]) > 0
        planes = out_ref.at[half].reshape(NP * CY * part, LANES)
        for y in range(CY):
            plane = jnp.where(flip_row, g[CY - 1 - y], g[y])
            for x, piece in enumerate(columns(plane)):
                planes[pl.ds(CY * x + y, NP, stride=CY * part), :] = piece
        target = out_hbm.at[:, CY * first : CY * (first + part), :]
        copies.append(pltpu.make_async_copy(out_ref.at[half], target, sems.at[half]))
        copies[-1].start()
    for copy in copies:
        copy.wait()


def in_hbm(a):
    return pltpu.with_memory_space_constraint(a, pltpu.HBM)


def call(kernel, outs, spaces, scratch=(), scalars=0):
    shapes = tuple(space(dims, dtype) for space, dims, dtype in outs)
    specs = [pl.BlockSpec(memory_space=pltpu.SMEM)] * scalars
    specs += [pl.BlockSpec(memory_space=s) for s in spaces]
    return pl.pallas_call(
        kernel,
        out_shape=shapes,
        in_specs=specs,
        out_specs=tuple(pl.BlockSpec(memory_space=out[0]) for out in outs),
        scratch_shapes=list(scratch),
        compiler_params=pltpu.CompilerParams(vmem_limit_bytes=VMEM_LIMIT),
    )


def per_device(
    rhs,
    coef_x,
    coef_y,
    out_coupling_x,
    in_coupling_x,
    inverse_x,
    boundary_inverse,
    out_coupling_y,
    in_coupling_y,
    inverse_y,
    bc_flags,
    line_order,
):
    vmem, hbm = pltpu.VMEM, pltpu.HBM
    rank = lax.axis_index("gx").astype(jnp.int32).reshape(1)
    mats_x = (out_coupling_x, inverse_x, in_coupling_x, boundary_inverse)
    mats_y = (out_coupling_y, inverse_y, in_coupling_y)
    rhs = rhs.reshape(NP, CX * CY, LANES)
    coef_x = coef_x.reshape(3, CX * CY, LANES)
    coef_y = coef_y.reshape(3, CX * CY, LANES)

    sent, local, tiles, raw_y = call(
        x_local_kernel,
        (
            (vmem, (SX, NP + 8, LANES), F32),
            (vmem, (CX + 1, NP, CY * LANES), F32),
            (vmem, (6 * NP, 4 * NP), F32),
            (vmem, (3, NP, NP), F32),
        ),
        (hbm,) * 11,
        [
            vmem((PIECES, NP, 8, LANES), F32),
            vmem((3, CX * CY, LANES), F32),
            vmem((CY, LANES), jnp.int32),
            vmem((CX, LANES), jnp.int32),
            vmem((3, NP, NP), F32),
            vmem((3, NP, NP), F32),
            pltpu.SemaphoreType.DMA((10 + PIECES,)),
        ],
        1,
    )(rank, *[in_hbm(a) for a in (rhs, coef_x, bc_flags) + mats_x + mats_y + (line_order,)])
    got = lax.all_to_all(sent, "gx", 0, 0, tiled=True)
    later = [
        (rows, 4 * NP)
        for rows in (11 * NP, 6 * NP, 9 * NP, 4 * NP, 4 * NP, 10 * NP + 16, 10 * NP + 16)
    ]
    gain_x, up_x, down_x, from_x, parts_x, parts_y, gain_y, from_y, up_y, down_y = call(
        prepare_kernel,
        (
            (vmem, (11 * NP, 4 * NP), BF16),
            (vmem, (7 * NP + 16, 4 * NP), BF16),
            (vmem, (7 * NP + 16, 4 * NP), BF16),
        )
        + tuple((hbm, dims, BF16) for dims in later),
        (vmem, vmem),
        [vmem(dims, BF16) for dims in later] + [pltpu.SemaphoreType.DMA((7,))],
    )(tiles, raw_y)
    (back,) = call(x_owner_kernel, ((vmem, (SX, NP, LANES), F32),), (vmem,) * 4)(
        got, gain_x, up_x, down_x
    )
    terms = lax.all_to_all(back, "gx", 0, 0, tiled=True)
    local, sent = call(
        middle_kernel,
        ((vmem, (CY, NP, CX * LANES), F32), (vmem, (SY * ROWS, LANES), F32)),
        (vmem,) * 7,
        [vmem((CY, NP, CX * LANES), F32)],
        1,
    )(rank, local, coef_x, parts_x, parts_y, from_x, terms, coef_y)
    got = lax.all_to_all(sent.reshape(SY, ROWS // 2, 2, LANES), "gy", 0, 0, tiled=True)
    (back,) = call(
        y_owner_kernel,
        ((vmem, (SY, 32, LANES), F32),),
        (vmem,) * 4,
        [vmem((SY, 32, LANES), F32)],
    )(got.reshape(SY * ROWS, LANES), gain_y, up_y, down_y)
    terms = lax.all_to_all(back, "gy", 0, 0, tiled=True)
    (out,) = call(
        y_final_kernel,
        ((hbm, (NP, CX * CY, LANES), F32),),
        (vmem,) * 6,
        [
            vmem((HALVES, NP, CX * CY // HALVES, LANES), F32),
            pltpu.SemaphoreType.DMA((HALVES,)),
        ],
    )(local, coef_y, line_order, parts_y, from_y, terms)
    return out.reshape(NP, CX, CY, LANES)


def solution(mesh):
    grid = P(None, "gx", "gy", None)
    in_specs = (grid, grid, grid) + (P(),) * 7 + (P("gy", None), P("gx", None))
    return jax.shard_map(
        per_device, mesh=mesh, in_specs=in_specs, out_specs=grid, check_vma=False
    )
```
